256 devices in a mesh: dp: 32 (over x, z), tensor: 8 (over y, core).
Axes of the slice: x: 4, y: 4, z: 8, core: 2. Of those that a mesh axis runs over, the one named last changes fastest.
Arguments:
- queries: bfloat16 [8192, 4096], P('dp', 'tensor'), may hold values from -64 to 64
- keys: bfloat16 [32768, 4096], P('dp', 'tensor'), may hold values from -16 to 16
- values: bfloat16 [32768, 4096], P('dp', 'tensor'), may hold values from -6 to 6
- out_weight: bfloat16 [4096, 8192], P('tensor', 'dp'), may hold values from -0.75 to 0.75
- grad_out: bfloat16 [8192, 8192], P(('dp', 'tensor')), may hold values from -1.5 to 1.5
- neighbour_owner: int32 [128, 2], P('dp'), may hold values from 0 to 31, all different within a row; in each aligned block of 4 rows (0 to 3, 4 to 7, ...) no two rows name the same one
- neighbour_local: int32 [128, 2], P('dp'), may hold values from 0 to 7
Outputs:
- attended_out: bfloat16 [8192, 8192], P(('dp', 'tensor'))
- grad_queries: bfloat16 [8192, 4096], P('dp', 'tensor')
- grad_keys: float32 [32768, 4096], P('dp', 'tensor')
- grad_values: float32 [32768, 4096], P('dp', 'tensor')
The draws below stay inside these ranges and needn't reach their ends.
Inputs may be any that keep to these rules, and one draw needn't show every extreme that they name: `neighbour_owner`: among the groups of one index of dp, each owner is named at most 1 times, and exactly 1 times somewhere; the 2 owners of a group differ.
All inputs are finite; a program needn't handle non-finite values.
Results may differ from the reference program's by a relative error of at most 0.04.
Values may be sent and summed in bfloat16 or wider, within the bound.
A program may use at most 128 MiB of HBM per device.

```python
import math
import jax
import jax.numpy as jnp
import numpy as np
from jax import lax

D = 8192
HEADS = 32
HD = 128
GROUP = 64
NLEN = 128
NBRS = 2
CH_DEV = 4
NB_DEV = 8
CAP = 1
NCH = 128
TOKENS = 8192
NROWS = 32768
N_DP = 32


def draw_queries(key, part):
    key = jax.random.fold_in(key, 11)
    noise_key = jax.random.fold_in(key, 0)
    noise = jax.random.normal(noise_key, (TOKENS, HEADS, HD), jnp.float32)
    return jnp.clip(noise, -64.0, 64.0).reshape(TOKENS, HEADS * HD).astype(jnp.bfloat16)


def draw_keys(key, part):
    key = jax.random.fold_in(key, 23)
    noise_key = jax.random.fold_in(key, 0)
    noise = jax.random.normal(noise_key, (NROWS, HEADS, HD), jnp.float32)
    return jnp.clip(noise, -16.0, 16.0).reshape(NROWS, HEADS * HD).astype(jnp.bfloat16)


def set_ends(result, key, low, top_value):
    place = [jax.random.randint(jax.random.fold_in(key, axis), (), 0, length) for axis, length in enumerate(result.shape)]
    longest = result.shape.index(max(result.shape))
    neighbour = place[:longest] + [(place[longest] + 1) % result.shape[longest]] + place[longest + 1:]
    return result.at[tuple(place)].set(low).at[tuple(neighbour)].set(top_value)


def block_scale(stream_key, shape, cuts, least, top_value):
    gain = 1.0
    for position, blocks in cuts:
        draws = jax.random.uniform(jax.random.fold_in(jax.random.fold_in(stream_key, 6), position), (blocks,), jnp.float32, least / len(cuts), top_value / len(cuts))
        gain = gain * jnp.repeat(jnp.exp(draws), shape[position] // blocks).reshape((-1,) + (1,) * (len(shape) - 1 - position))
    return gain


def routed_block(rng, own, number, rows, count, top, bound, lean):
    ranking = jax.random.permutation(rng, count)
    crowded, ordinary = shares(count, rows * top, bound, lean, True), shares(count, rows * top, bound, lean, False)
    places = jnp.arange(count)

    def named(lengths, turn):
        used = int((lengths > 0).sum())
        fixed = max(1, used // 4)
        shifted = fixed + (places - fixed + turn * (used - fixed)) % max(1, count - fixed)
        return jnp.zeros((count,), jnp.int32).at[ranking[jnp.where(places < fixed, places, shifted)]].set(jnp.asarray(lengths, jnp.int32))

    lengths = jnp.where(number % 4 == 0, named(crowded, number // 4), named(ordinary, number - number // 4 - 1))
    mixed = jax.random.permutation(jax.random.fold_in(own, 3), count)
    source_of, receiver = mixed[0:count // 2 * 2:2], mixed[1:count // 2 * 2:2]
    room = jnp.minimum(lengths[source_of] - 1, bound - lengths[receiver]) // 2
    room = jnp.where((source_of == ranking[0]) | (receiver == ranking[0]) | (lengths[receiver] == 0), 0, jnp.maximum(room, 0))
    shifted = jax.random.randint(jax.random.fold_in(own, 4), (count // 2,), 0, 1 << 20) % (room + 1)
    lengths = lengths.at[source_of].add(-shifted).at[receiver].add(shifted)
    members = jnp.searchsorted(jnp.cumsum(lengths), jnp.arange(rows * top), side="right").astype(jnp.int32)
    grid = members.reshape(top, rows).T
    grid = grid[jax.random.permutation(jax.random.fold_in(own, 1), rows)]
    turn = jax.random.randint(jax.random.fold_in(own, 2), (rows, 1), 0, top)
    return jnp.take_along_axis(grid, (jnp.arange(top)[None, :] + turn) % top, axis=1)


def shares(number_of, total, bound, slope, full):
    loads = [(1 << 20) // math.isqrt(grade ** slope) + 1 for grade in range(1, number_of + 1)]
    largest = bound if full else min(bound, max(-(-total // number_of), total * loads[0] // sum(loads)))
    least = 1 if total - largest >= number_of - 1 else 0
    holding, spare = [largest] + [least] * (number_of - 1), total - largest - least * (number_of - 1)
    while spare > 0:
        movable = [i for i in range(1, number_of) if holding[i] < largest] or [i for i in range(1, number_of) if holding[i] < bound]
        mass, budget = sum([loads[i] for i in movable]), spare
        for i in movable:
            more = min(bound - holding[i], max(1, budget * loads[i] // mass), spare)
            holding[i] = holding[i] + more
            spare = spare - more
    return np.array(holding)


def normal_values(rng, extent, spread, reach, shards=(), kind=jnp.bfloat16):
    values = spread * jax.random.normal(rng, extent, jnp.float32)
    if shards:
        values = values * block_scale(rng, extent, shards, -0.22, 0.18)
    return jnp.clip(values, -reach, reach).astype(kind)


def setup_inputs(seed: int = 0) -> dict:
    streams_of = jax.random.split(jax.random.key(seed), 8)
    queries = draw_queries(jax.random.fold_in(streams_of[7], 71), 0)
    keys = draw_keys(jax.random.fold_in(streams_of[7], 71), 0)
    values = normal_values(streams_of[2], (NROWS, HEADS * HD), 1.0, 6.0, ((0, 32), (1, 8)))
    out_weight = normal_values(streams_of[3], (HEADS * HD, D), (HEADS * HD // 64) ** -0.5, 0.75, ((0, 8), (1, 32)))
    grad_out = normal_values(streams_of[4], (TOKENS, D), 0.1, 1.5, ((0, 256),))
    neighbour_owner_keys = jax.random.split(jax.random.fold_in(streams_of[5], 1), NCH // CH_DEV)
    neighbour_owner_turns = jax.random.permutation(jax.random.fold_in(streams_of[5], 3), NCH // CH_DEV)
    neighbour_owner = jax.vmap(lambda own, number: routed_block(jax.random.fold_in(streams_of[5], 2), own, number, CH_DEV, N_DP, NBRS, CAP, 2))(neighbour_owner_keys, neighbour_owner_turns).reshape((NCH, NBRS))
    neighbour_local = set_ends(jax.random.randint(streams_of[6], (NCH, NBRS), 0, NB_DEV), jax.random.fold_in(streams_of[6], 1), 0, NB_DEV - 1).astype(jnp.int32)
    return dict(queries=queries, keys=keys, values=values, out_weight=out_weight, grad_out=grad_out, neighbour_owner=neighbour_owner, neighbour_local=neighbour_local)


def partial_attend(query_rows, key_rows, value_rows, score_scale):
    scores = jnp.einsum("...qhd,...khd->...hqk", query_rows.astype(jnp.float32), key_rows.astype(jnp.float32)) * score_scale
    peak_value = jnp.max(scores, axis=-1)
    exponent = jnp.exp(scores - peak_value[..., None])
    exp_total = jnp.sum(exponent, axis=-1)
    probability = lax.optimization_barrier(exponent.astype(jnp.bfloat16)).astype(jnp.float32)
    weighted = jnp.einsum("...hqk,...khd->...hqd", probability, value_rows.astype(jnp.float32))
    return peak_value, exp_total, weighted


def combine_parts(peak_value, exp_total, weighted):
    top_peak = jnp.max(peak_value, axis=1, keepdims=True)
    factor = jnp.exp(peak_value - top_peak)
    denominator = jnp.sum(factor * exp_total, axis=1)
    merged = jnp.sum(factor[..., None] * weighted, axis=1) / denominator[..., None]
    return merged, top_peak[:, 0] + jnp.log(denominator)


def attend_grads(query_rows, key_rows, value_rows, upstream, log_total, inner_term, score_scale):
    query_wide = query_rows.astype(jnp.float32)
    key_wide = key_rows.astype(jnp.float32)
    upstream_wide = upstream.astype(jnp.float32)
    scores = jnp.einsum("...qhd,...khd->...hqk", query_wide, key_wide) * score_scale
    back_prob = jnp.exp(scores - log_total[..., None])
    prob_short = lax.optimization_barrier(back_prob.astype(jnp.bfloat16)).astype(jnp.float32)
    grad_value = jnp.einsum("...hqk,...qhd->...khd", prob_short, upstream_wide).astype(jnp.bfloat16)
    grad_probs = jnp.einsum("...qhd,...khd->...hqk", upstream_wide, value_rows.astype(jnp.float32))
    grad_scores = (back_prob * (grad_probs - inner_term[..., None])).astype(jnp.bfloat16)
    scores_short = lax.optimization_barrier(grad_scores).astype(jnp.float32)
    grad_key = (jnp.einsum("...hqk,...qhd->...khd", scores_short, query_wide) * score_scale).astype(jnp.bfloat16)
    grad_query = jnp.einsum("...hqk,...khd->...qhd", scores_short, key_wide) * score_scale
    return grad_key, grad_value, grad_query


def reference(queries, keys, values, out_weight, grad_out, neighbour_owner, neighbour_local):
    score_scale = HD ** -0.5
    group_total = CH_DEV * N_DP
    neighbour_total = NB_DEV * N_DP
    row_ids = (neighbour_owner * NB_DEV + neighbour_local).astype(jnp.int32)
    key_table = keys.reshape(neighbour_total, NLEN, HEADS, HD)
    value_table = values.reshape(neighbour_total, NLEN, HEADS, HD)
    query_groups = queries.reshape(group_total, GROUP, HEADS, HD)
    upstream = jnp.dot(grad_out, out_weight.T, preferred_element_type=jnp.float32).astype(jnp.bfloat16)
    upstream_groups = upstream.reshape(group_total, GROUP, HEADS, HD)

    def one_group(inputs):
        query_rows, upstream_rows, group_ids = inputs
        key_rows = key_table[group_ids]
        value_rows = value_table[group_ids]
        query_both = jnp.broadcast_to(query_rows, (NBRS,) + query_rows.shape)
        peak_value, exp_total, weighted = partial_attend(query_both, key_rows, value_rows, score_scale)
        merged, log_total = combine_parts(peak_value[None], exp_total[None], weighted[None])
        context = merged[0].transpose(1, 0, 2).astype(jnp.bfloat16)
        inner_term = jnp.sum(upstream_rows.astype(jnp.float32) * context.astype(jnp.float32), axis=-1).T
        upstream_both = jnp.broadcast_to(upstream_rows, (NBRS,) + upstream_rows.shape)
        log_both = jnp.broadcast_to(log_total[0], (NBRS,) + log_total.shape[1:])
        inner_both = jnp.broadcast_to(inner_term, (NBRS,) + inner_term.shape)
        grad_key, grad_value, grad_query = attend_grads(query_both, key_rows, value_rows, upstream_both, log_both, inner_both, score_scale)
        return context, jnp.sum(grad_query, axis=0), grad_key, grad_value

    context, grad_query, grad_key, grad_value = lax.map(one_group, (query_groups, upstream_groups, row_ids))
    context = context.reshape(TOKENS, HEADS * HD)
    attended_out = jnp.dot(context, out_weight, preferred_element_type=jnp.float32).astype(jnp.bfloat16)
    grad_queries = grad_query.reshape(TOKENS, HEADS * HD).astype(jnp.bfloat16)
    flat_ids = row_ids.reshape(-1)
    key_terms = lax.optimization_barrier(grad_key).reshape(group_total * NBRS, NLEN, HEADS * HD).astype(jnp.float32)
    value_terms = lax.optimization_barrier(grad_value).reshape(group_total * NBRS, NLEN, HEADS * HD).astype(jnp.float32)
    grad_keys = jnp.zeros((neighbour_total, NLEN, HEADS * HD), jnp.float32).at[flat_ids].add(key_terms)
    grad_values = jnp.zeros((neighbour_total, NLEN, HEADS * HD), jnp.float32).at[flat_ids].add(value_terms)
    return attended_out, grad_queries, grad_keys.reshape(NROWS, HEADS * HD), grad_values.reshape(NROWS, HEADS * HD)
```

```python
import jax
import jax.numpy as jnp
from jax import lax
from jax.experimental import pallas as pl
from jax.experimental.pallas import tpu as pltpu
from jax.sharding import PartitionSpec as P

X, Z, Y, C = 4, 8, 4, 2
HD = 128
GROUP = 64
NLEN = 128
NB_DEV = 8
TOK = 256
SCALE = HD**-0.5
LOW = -1e30
BF = jnp.bfloat16
F32 = jnp.float32
VMEM = pl.BlockSpec(memory_space=pltpu.VMEM)
SMEM = pl.BlockSpec(memory_space=pltpu.SMEM)
LIMIT = 60 * 1024 * 1024


def place():
    dp, t = lax.axis_index("dp"), lax.axis_index("tensor")
    return lax.div(dp, Z), lax.rem(dp, Z), lax.div(t, C), lax.rem(t, C)


def device(x, z, y, c):
    return (x * Z + z, y * C + c)


def step_from(i, by, n):
    return lax.rem(i + (by + n), n)


def columns(i, width):
    return pl.ds(pl.multiple_of(i * width, width), width)


def enter(peers):
    barrier = pltpu.get_barrier_semaphore()
    for peer in peers:
        pl.semaphore_signal(barrier, inc=1, device_id=peer, device_id_type=pl.DeviceIdType.MESH)
    pl.semaphore_wait(barrier, len(peers))


class Copies:
    def __init__(self, send, recv):
        self.send, self.recv, self.count, self.started = send, recv, 0, []

    def take(self, n=1):
        first = self.count
        self.count += n
        return first

    def make(self, sem, src, dst, to):
        return pltpu.make_async_remote_copy(
            src_ref=src,
            dst_ref=dst,
            send_sem=self.send.at[sem],
            recv_sem=self.recv.at[sem],
            device_id=to,
            device_id_type=pl.DeviceIdType.MESH,
        )

    def start(self, src, dst, to):
        copy = self.make(self.take(), src, dst, to)
        copy.start()
        self.started.append(copy)
        return copy

    def finish(self):
        for copy in self.started:
            copy.wait_send()


class Gather:
    def __init__(self, copies, first, view, hops, where):
        self.copies, self.first, self.view, self.hops, self.where = copies, first, view, hops, where
        self.sent = [[], []]

    def step(self, s):
        x, z, y, c = self.where
        for way, sign in ((0, 1), (1, -1)):
            if 0 < s <= self.hops[way]:
                self.sent[way][s - 1].wait_recv()
            if s < self.hops[way]:
                block = step_from(z, -sign * s, Z)
                src = self.first if s == 0 else self.view(block)
                to = device(x, step_from(z, sign, Z), y, c)
                self.sent[way].append(self.copies.start(src, self.view(block), to))


class Scatter:
    def __init__(self, copies, part, held, hops, where):
        self.copies, self.part, self.held, self.hops, self.where = copies, part, held, hops, where
        self.sent = [[], []]

    def step(self, s):
        x, z, y, c = self.where
        for way, sign in ((0, 1), (1, -1)):
            n = self.hops[way]
            if 0 < s <= n:
                self.sent[way][s - 1].wait_recv()
            if s < n:
                goal = step_from(z, sign * (n - s), Z)
                if s == 0:
                    src = self.part(goal)
                else:
                    src = self.held(way, s - 1)
                    src[...] = (src[...].astype(F32) + self.part(goal)[...].astype(F32)).astype(BF)
                to = device(x, step_from(z, sign, Z), y, c)
                self.sent[way].append(self.copies.start(src, self.held(way, s), to))

    def total(self):
        z = self.where[1]
        total = self.part(z)[...].astype(F32)
        for way in (0, 1):
            total += self.held(way, self.hops[way] - 1)[...].astype(F32)
        return total


HOPS = ((4, 3), (3, 4))


def spread_kernel(
    q_ref, k_ref, v_ref, w_ref, g_ref,
    qall, ktab, vtab, wf, upall,
    gfull, upp, upr, send, recv, local,
):
    where = x, z, y, c = place()
    t = y * C + c
    depth = w_ref.shape[0] // 4
    width = w_ref.shape[1]
    span = Z * width
    xs = [step_from(x, i, X) for i in range(X)]
    ys = [step_from(y, i, Y) for i in range(Y)]
    other = 1 - c
    enter(
        [device(xs[i], z, y, c) for i in (1, 2, 3)]
        + [device(x, step_from(z, i, Z), y, c) for i in (1, -1)]
        + [device(x, z, ys[i], c) for i in (1, 2, 3)]
        + [device(x, z, y, other)]
    )
    copies = Copies(send, recv)
    kept = []

    def keep(src, dst):
        copy = pltpu.make_async_copy(src, dst, local.at[len(kept)])
        copy.start()
        kept.append(copy)

    keep(g_ref.at[:, columns(x, span)], gfull.at[x, t])
    keep(q_ref.at[:, columns(x, HD)], qall.at[z, x])
    keep(k_ref.at[:, columns(x, HD)], ktab.at[x])
    keep(v_ref.at[:, columns(x, HD)], vtab.at[x])
    keep(w_ref, wf.at[:, columns(z, width)])

    g_in = [
        copies.start(g_ref.at[:, columns(xs[i], span)], gfull.at[x, t], device(xs[i], z, y, c))
        for i in (1, 3, 2)
    ]

    def weight_piece(i):
        rows = pl.ds(i * depth, depth)
        return Gather(
            copies, w_ref.at[rows], lambda b: wf.at[rows, columns(b, width)], HOPS[i % 2], where
        )

    def piece(ref, i):
        return Gather(copies, ref.at[z, i], lambda b: ref.at[b, i], HOPS[i % 2], where)

    pieces = [weight_piece(i) for i in range(4)]
    pieces += [piece(qall, i) for i in range(X)]
    pieces += [piece(upall, i) for i in range(X)]

    table_in, q_in, g_y, g_core, up_in = [], [], {}, {}, {}

    def before(wave):
        if wave == 4:
            for copy in q_in:
                copy.wait_recv()
            kept[1].wait()
        if 8 <= wave < 8 + X:
            i = wave - 8
            for copy in up_in[i]:
                copy.wait_recv()
            total = upp[i, :, columns(x, HD)].astype(F32)
            for j in range(3):
                total += upr[i, j].astype(F32)
            upall[z, i] = total.astype(BF)

    def after(wave):
        if wave == 0:
            for i in (1, 3, 2):
                q_in.append(
                    copies.start(
                        q_ref.at[:, columns(xs[i], HD)], qall.at[z, x], device(xs[i], z, y, c)
                    )
                )
            kept[0].wait()
            for copy in g_in:
                copy.wait_recv()
            for i in range(X):
                block = gfull.at[i, t]
                g_y[i] = [copies.start(block, block, device(x, z, ys[j], c)) for j in (1, 3, 2)]
                g_core[i] = [copies.start(block, block, device(x, z, y, other))]
            for i in (1, 3, 2):
                for src, dst in ((k_ref, ktab), (v_ref, vtab)):
                    table_in.append(
                        copies.start(
                            src.at[:, columns(xs[i], HD)], dst.at[x], device(xs[i], z, y, c)
                        )
                    )
        if 3 <= wave < 3 + X:
            i = wave - 3
            for copy, j in zip(g_y[i], (-1, -3, -2)):
                copy.wait_recv()
                block = gfull.at[i, step_from(y, j, Y) * C + c]
                g_core[i].append(copies.start(block, block, device(x, z, y, other)))
        if 7 <= wave < 7 + X:
            i = wave - 7
            if wave == 7:
                kept[4].wait()
            for copy in g_core[i]:
                copy.wait_recv()
            rows = gfull[i].reshape(TOK, span)
            upp[i] = lax.dot_general(
                rows, wf[...], (((1,), (1,)), ((), ())), preferred_element_type=F32
            ).astype(BF)
            up_in[i] = [
                copies.start(
                    upp.at[i, :, columns(xs[j], HD)], upr.at[i, j - 1], device(xs[j], z, y, c)
                )
                for j in (1, 3, 2)
            ]

    for wave in range(len(pieces) + 4):
        before(wave)
        for i, one in enumerate(pieces):
            if 0 <= wave - i <= 4:
                one.step(wave - i)
        after(wave)
    for copy in table_in:
        copy.wait_recv()
    for copy in kept[2:4]:
        copy.wait()
    copies.finish()


def spread(queries, keys, values, out_weight, grad_out):
    depth, width = out_weight.shape
    rows, head_cols = keys.shape
    return pl.pallas_call(
        spread_kernel,
        out_shape=(
            jax.ShapeDtypeStruct((Z, X, TOK, HD), BF),
            jax.ShapeDtypeStruct((X, rows, HD), BF),
            jax.ShapeDtypeStruct((X, rows, HD), BF),
            jax.ShapeDtypeStruct((depth, Z * width), BF),
            jax.ShapeDtypeStruct((Z, X, TOK, HD), BF),
        ),
        in_specs=[VMEM] * 5,
        out_specs=[VMEM] * 5,
        scratch_shapes=[
            pltpu.VMEM((X, Y * C, grad_out.shape[0], Z * width), BF),
            pltpu.VMEM((X, TOK, head_cols), BF),
            pltpu.VMEM((X, X - 1, TOK, HD), BF),
            pltpu.SemaphoreType.DMA((140,)),
            pltpu.SemaphoreType.DMA((140,)),
            pltpu.SemaphoreType.DMA((8,)),
        ],
        compiler_params=pltpu.CompilerParams(
            collective_id=0, has_side_effects=True, vmem_limit_bytes=LIMIT
        ),
        name="spread",
    )(queries, keys, values, out_weight, grad_out)


def list_uses(ids, groups, names):
    z = lax.rem(lax.axis_index("dp"), Z)

    def add(i, n):
        owner = ids[2 * i]
        dp, group = lax.shift_right_logical(i, 3), lax.shift_right_logical(i, 1) & 3
        groups[n] = (dp & 7) * 16 + lax.shift_right_logical(dp, 3) * 4 + group
        names[n] = lax.shift_right_logical(owner, 3) * NB_DEV + ids[2 * i + 1]
        return n + ((owner & 7) == z).astype(jnp.int32)

    n = lax.fori_loop(0, X * Z * 8, add, jnp.int32(0), unroll=8)
    last = jnp.maximum(n - 1, 0)
    groups[n] = groups[last]
    names[n] = names[last]
    return n


def pair_rows(ref, a, b, size):
    return [ref[pl.ds(pl.multiple_of(i * size, size), size), :] for i in (a, b)]


def pair_scores(first, second, both, left):
    product = lax.dot_general(
        jnp.concatenate([first, second], axis=0),
        both,
        (((1,), (1,)), ((), ())),
        preferred_element_type=F32,
    )
    return jnp.where(left, product[:NLEN], product[NLEN:])


def merge(one, two):
    peak = jnp.maximum(one[0], two[0])
    f, g = jnp.exp(one[0] - peak), jnp.exp(two[0] - peak)
    return peak, f * one[1] + g * two[1], f * one[2] + g * two[2]


def stats_kernel(ids, qall, upall, ktab, vtab, stats, groups, names):
    n = list_uses(ids, groups, names)
    stats[0] = jnp.full(stats.shape[1:], LOW, F32)
    stats[1] = jnp.zeros(stats.shape[1:], F32)
    stats[2] = jnp.zeros(stats.shape[1:], F32)
    left = lax.broadcasted_iota(jnp.int32, (1, 2 * GROUP), 1) < GROUP

    def pair(p, carry):
        a, b = 2 * p, 2 * p + 1
        ga, gb, na, nb = groups[a], groups[b], names[a], names[b]
        qq = jnp.concatenate(pair_rows(qall, ga, gb, GROUP), axis=0)
        uu = jnp.concatenate(pair_rows(upall, ga, gb, GROUP), axis=0)
        scores = pair_scores(*pair_rows(ktab, na, nb, NLEN), qq, left) * SCALE
        grad_probs = pair_scores(*pair_rows(vtab, na, nb, NLEN), uu, left)
        peak = jnp.max(scores, axis=0, keepdims=True)
        exponent = jnp.exp(scores - peak)
        total = jnp.sum(exponent, axis=0, keepdims=True)
        inner = jnp.sum(exponent * grad_probs, axis=0, keepdims=True)
        real = left | (b < n)
        new = (
            jnp.where(real, peak, LOW),
            jnp.where(real, total, 0.0),
            jnp.where(real, inner, 0.0),
        )
        for g, mine in ((ga, left), (gb, jnp.logical_not(left))):
            old = tuple(stats[i, pl.ds(g, 1), :] for i in range(3))
            merged = merge(old, new)
            for i in range(3):
                stats[i, pl.ds(g, 1), :] = jnp.where(mine, merged[i], old[i])
        return carry

    lax.fori_loop(0, (n + 1) // 2, pair, 0)


def stats_of_uses(ids, qall, upall, ktab, vtab):
    return pl.pallas_call(
        stats_kernel,
        out_shape=jax.ShapeDtypeStruct((3, 16 * Z, 2 * GROUP), F32),
        in_specs=[SMEM] + [VMEM] * 4,
        out_specs=VMEM,
        scratch_shapes=[pltpu.SMEM((264,), jnp.int32), pltpu.SMEM((264,), jnp.int32)],
        compiler_params=pltpu.CompilerParams(vmem_limit_bytes=LIMIT),
        name="stats",
    )(ids, qall, upall, ktab, vtab)


def totals_kernel(stats, out, held, send, recv):
    x, z, y, c = place()
    zs = [step_from(z, i, Z) for i in range(Z)]
    order = (1, 7, 2, 6, 3, 5, 4)
    enter([device(x, zs[i], y, c) for i in order])
    copies = Copies(send, recv)
    sent = [
        copies.start(
            stats.at[:, columns(zs[i], 16), :], held.at[i - 1], device(x, zs[i], y, c)
        )
        for i in order
    ]
    own = pl.ds(pl.multiple_of(z * 16, 16), 16)
    state = tuple(stats[i, own, :] for i in range(3))
    for copy, i in zip(sent, order):
        copy.wait_recv()
        state = merge(state, tuple(held[i - 1, j] for j in range(3)))
    state = merge(state, tuple(pltpu.roll(v, GROUP, 1) for v in state))
    out[0, own, :] = state[0] + jnp.log(state[1])
    out[1, own, :] = state[2] / state[1]
    back = out.at[:, own, :]
    sent = [copies.start(back, back, device(x, zs[i], y, c)) for i in order]
    for copy in sent:
        copy.wait_recv()
    copies.finish()


def totals(stats):
    return pl.pallas_call(
        totals_kernel,
        out_shape=jax.ShapeDtypeStruct((2,) + stats.shape[1:], F32),
        in_specs=[VMEM],
        out_specs=VMEM,
        scratch_shapes=[
            pltpu.VMEM((Z - 1, 3, 16, 2 * GROUP), F32),
            pltpu.SemaphoreType.DMA((16,)),
            pltpu.SemaphoreType.DMA((16,)),
        ],
        compiler_params=pltpu.CompilerParams(
            collective_id=1, has_side_effects=True, vmem_limit_bytes=LIMIT
        ),
        name="totals",
    )(stats)


def grads_kernel(
    ids, qall, upall, ktab, vtab, sums, ctx, gq, dkey, dvalue, groups, names, dk, dv
):
    n = list_uses(ids, groups, names)
    for ref in (ctx, gq, dk, dv):
        rows = 512

        @pl.loop(0, ref.shape[0] // rows)
        def _(i, ref=ref):
            ref[pl.ds(pl.multiple_of(i * rows, rows), rows), :] = jnp.zeros((rows, HD), ref.dtype)

    left = lax.broadcasted_iota(jnp.int32, (1, 2 * GROUP), 1) < GROUP
    zero = jnp.zeros((), BF)

    def add(ref, i, size, value):
        at = pl.ds(pl.multiple_of(i * size, size), size)
        ref[at, :] = (ref[at, :].astype(F32) + value).astype(ref.dtype)

    def dot(a, b):
        return jnp.dot(a, b, preferred_element_type=F32)

    def pair(p, carry):
        a, b = 2 * p, 2 * p + 1
        ga, gb, na, nb = groups[a], groups[b], names[a], names[b]
        qq = jnp.concatenate(pair_rows(qall, ga, gb, GROUP), axis=0)
        uu = jnp.concatenate(pair_rows(upall, ga, gb, GROUP), axis=0)
        keys = pair_rows(ktab, na, nb, NLEN)
        values = pair_rows(vtab, na, nb, NLEN)
        scores = pair_scores(*keys, qq, left) * SCALE
        grad_probs = pair_scores(*values, uu, left)
        log_total = jnp.where(left, sums[0, pl.ds(ga, 1), :], sums[0, pl.ds(gb, 1), :])
        inner = jnp.where(left, sums[1, pl.ds(ga, 1), :], sums[1, pl.ds(gb, 1), :])
        real = left | (b < n)
        prob = jnp.where(real, jnp.exp(scores - log_total), 0.0)
        grad_scores = prob * (grad_probs - inner)
        prob_t = prob.T.astype(BF)
        grad_t = grad_scores.T.astype(BF)
        prob, grad_scores = prob.astype(BF), grad_scores.astype(BF)

        def halves(v):
            return jnp.concatenate([jnp.where(left, v, zero), jnp.where(left, zero, v)], axis=0)

        context = dot(prob_t, jnp.concatenate(values, axis=1))
        grad_q = dot(grad_t, jnp.concatenate(keys, axis=1)) * SCALE
        grad_v = dot(halves(prob), uu)
        grad_k = dot(halves(grad_scores), qq) * SCALE
        add(ctx, ga, GROUP, context[:GROUP, :HD])
        add(ctx, gb, GROUP, context[GROUP:, HD:])
        add(gq, ga, GROUP, grad_q[:GROUP, :HD])
        add(gq, gb, GROUP, grad_q[GROUP:, HD:])
        add(dv, na, NLEN, grad_v[:NLEN])
        add(dv, nb, NLEN, grad_v[NLEN:])
        add(dk, na, NLEN, grad_k[:NLEN])
        add(dk, nb, NLEN, grad_k[NLEN:])
        return carry

    lax.fori_loop(0, (n + 1) // 2, pair, 0)
    for src, dst in ((dk, dkey), (dv, dvalue)):
        rows = 512

        @pl.loop(0, src.shape[0] // rows)
        def _(i, src=src, dst=dst):
            at = pl.ds(pl.multiple_of(i * rows, rows), rows)
            dst[at, :] = src[at, :].astype(BF)


def grads_of_uses(ids, qall, upall, ktab, vtab, sums):
    tokens, rows = qall.shape[0], ktab.shape[0]
    return pl.pallas_call(
        grads_kernel,
        out_shape=(
            jax.ShapeDtypeStruct((tokens, HD), BF),
            jax.ShapeDtypeStruct((tokens, HD), BF),
            jax.ShapeDtypeStruct((rows, HD), BF),
            jax.ShapeDtypeStruct((rows, HD), BF),
        ),
        in_specs=[SMEM] + [VMEM] * 5,
        out_specs=[VMEM] * 4,
        scratch_shapes=[
            pltpu.SMEM((264,), jnp.int32),
            pltpu.SMEM((264,), jnp.int32),
            pltpu.VMEM((rows, HD), F32),
            pltpu.VMEM((rows, HD), F32),
        ],
        compiler_params=pltpu.CompilerParams(vmem_limit_bytes=LIMIT),
        name="grads",
    )(ids, qall, upall, ktab, vtab, sums)


def collect_kernel(
    ctx, gq, dkey, dvalue, wf,
    out, gq_out, dk_out, dv_out,
    held, ctx4, part, core_in, y_in, done, gq_done, send, recv, out_send, out_recv, local,
):
    where = x, z, y, c = place()
    t = y * C + c
    span = wf.shape[1]
    xs = [step_from(x, i, X) for i in range(X)]
    ys = [step_from(y, i, Y) for i in range(Y)]
    other = 1 - c
    enter(
        [device(xs[i], z, y, c) for i in (1, 2, 3)]
        + [device(x, step_from(z, i, Z), y, c) for i in (1, -1)]
        + [device(x, z, ys[i], c) for i in (1, 2, 3)]
        + [device(x, z, y, other)]
    )
    copies = Copies(send, recv)
    kept = []

    def keep(src, dst):
        copy = pltpu.make_async_copy(src, dst, local.at[len(kept)])
        copy.start()
        kept.append(copy)

    def piece(ref, i, n):
        return Scatter(
            copies,
            lambda b: ref.at[b, i],
            lambda way, s: held.at[n, 4 * way + s],
            HOPS[n % 2],
            where,
        )

    pieces = [piece(ctx, i, i) for i in range(X)]
    pieces += [piece(gq, xs[i], X + i) for i in range(X)]
    table_in, ctx_in, core_sent, y_sent, gq_sent = [], {}, {}, {}, []

    def tables():
        for src, dst in ((dkey, dk_out), (dvalue, dv_out)):
            keep(src.at[x], dst.at[:, columns(x, HD)])
            for i in (1, 3, 2):
                table_in.append(
                    copies.start(src.at[xs[i]], dst.at[:, columns(x, HD)], device(xs[i], z, y, c))
                )

    def share(i):
        mine = ctx4.at[i, :, columns(x, HD)]
        mine[...] = pieces[i].total().astype(BF)
        ctx_in[i] = [copies.start(mine, mine, device(xs[j], z, y, c)) for j in (1, 3, 2)]

    def multiply(i):
        for copy in ctx_in[i]:
            copy.wait_recv()
        for j in range(2):
            cols = pl.ds(j * (span // 2), span // 2)
            product = jnp.dot(ctx4[i], wf[:, cols], preferred_element_type=F32).astype(BF)
            part[i, :, :, :, cols] = product.reshape(Y, C, TOK // (Y * C), span // 2)
        core_sent[i] = copies.start(part.at[i, :, other], core_in.at[i], device(x, z, y, other))

    def join(i):
        core_sent[i].wait_recv()
        core_in[i] = (core_in[i].astype(F32) + part[i, :, c].astype(F32)).astype(BF)
        y_sent[i] = [
            copies.start(core_in.at[i, ys[j]], y_in.at[i, j - 1], device(x, z, ys[j], c))
            for j in (1, 3, 2)
        ]

    def total(i):
        for copy in y_sent[i]:
            copy.wait_recv()
        value = core_in[i, y].astype(F32)
        for j in range(3):
            value += y_in[i, j].astype(F32)
        done[i] = value.astype(BF)
        goal = out.at[:, columns(x, span)]

        @pl.when(x == i)
        def _():
            copy = pltpu.make_async_copy(done.at[i], goal, local.at[7])
            copy.start()
            copy.wait()

        @pl.when(x != i)
        def _():
            sem = step_from(i - x, 0, X)
            pltpu.make_async_remote_copy(
                src_ref=done.at[i],
                dst_ref=goal,
                send_sem=out_send.at[sem],
                recv_sem=out_recv.at[sem],
                device_id=device(i, z, y, c),
                device_id_type=pl.DeviceIdType.MESH,
            ).start()

    def queries(i):
        gq_done[i] = pieces[X + i].total().astype(BF)
        goal = gq_out.at[:, columns(x, HD)]
        if i == 0:
            keep(gq_done.at[i], goal)
        else:
            gq_sent.append(copies.start(gq_done.at[i], goal, device(xs[i], z, y, c)))

    def last_hop(n):
        return n + 4

    for wave in range(12):
        for n, one in enumerate(pieces):
            if 0 <= wave - n <= 4:
                one.step(wave - n)
        if wave == 0:
            tables()
        for stage, ref in enumerate((share, multiply, join, total)):
            i = wave - 4 - stage
            if 0 <= i < X:
                ref(i)
        if 8 <= wave:
            queries(wave - 8)
    for copy in table_in + gq_sent:
        copy.wait_recv()
    for i in (1, 2, 3):
        copy = pltpu.make_async_remote_copy(
            src_ref=done.at[0],
            dst_ref=out.at[:, columns(xs[i], span)],
            send_sem=out_send.at[i],
            recv_sem=out_recv.at[i],
            device_id=device(xs[i], z, y, c),
            device_id_type=pl.DeviceIdType.MESH,
        )
        copy.wait_recv()
        copy.wait_send()
    for copy in kept:
        copy.wait()
    copies.finish()


def collect(ctx, gq, dkey, dvalue, wf):
    head_cols, span = wf.shape
    rows = dkey.shape[1]
    slots = TOK // (Y * C)
    return pl.pallas_call(
        collect_kernel,
        out_shape=(
            jax.ShapeDtypeStruct((slots, X * span), BF),
            jax.ShapeDtypeStruct((TOK, head_cols), BF),
            jax.ShapeDtypeStruct((rows, head_cols), BF),
            jax.ShapeDtypeStruct((rows, head_cols), BF),
        ),
        in_specs=[VMEM] * 5,
        out_specs=[VMEM] * 4,
        scratch_shapes=[
            pltpu.VMEM((2 * X, 8, TOK, HD), BF),
            pltpu.VMEM((X, TOK, head_cols), BF),
            pltpu.VMEM((X, Y, C, slots, span), BF),
            pltpu.VMEM((X, Y, slots, span), BF),
            pltpu.VMEM((X, Y - 1, slots, span), BF),
            pltpu.VMEM((X, slots, span), BF),
            pltpu.VMEM((X, TOK, HD), BF),
            pltpu.SemaphoreType.DMA((120,)),
            pltpu.SemaphoreType.DMA((120,)),
            pltpu.SemaphoreType.DMA((4,)),
            pltpu.SemaphoreType.DMA((4,)),
            pltpu.SemaphoreType.DMA((8,)),
        ],
        compiler_params=pltpu.CompilerParams(
            collective_id=2, has_side_effects=True, vmem_limit_bytes=LIMIT
        ),
        name="collect",
    )(ctx, gq, dkey, dvalue, wf)


def shards(queries, keys, values, out_weight, grad_out, neighbour_owner, neighbour_local):
    ids = jnp.stack([neighbour_owner, neighbour_local], axis=-1).reshape(1, -1)
    ids = lax.all_gather(ids, "dp", axis=0, tiled=True).reshape(-1)
    qall, ktab, vtab, wf, upall = spread(queries, keys, values, out_weight, grad_out)
    qall, upall = (a.reshape(Z * X * TOK, HD) for a in (qall, upall))
    ktab, vtab = (a.reshape(X * keys.shape[0], HD) for a in (ktab, vtab))
    sums = totals(stats_of_uses(ids, qall, upall, ktab, vtab))
    ctx, gq, dkey, dvalue = grads_of_uses(ids, qall, upall, ktab, vtab, sums)
    ctx, gq = (a.reshape(Z, X, TOK, HD) for a in (ctx, gq))
    dkey, dvalue = (a.reshape((X,) + keys.shape[:1] + (HD,)) for a in (dkey, dvalue))
    out, grad_queries, grad_keys, grad_values = collect(ctx, gq, dkey, dvalue, wf)
    return out, grad_queries, grad_keys.astype(F32), grad_values.astype(F32)


def solution(mesh):
    return jax.shard_map(
        shards,
        mesh=mesh,
        in_specs=(
            P("dp", "tensor"),
            P("dp", "tensor"),
            P("dp", "tensor"),
            P("tensor", "dp"),
            P(("dp", "tensor"), None),
            P("dp", None),
            P("dp", None),
        ),
        out_specs=(
            P(("dp", "tensor"), None),
            P("dp", "tensor"),
            P("dp", "tensor"),
            P("dp", "tensor"),
        ),
        check_vma=False,
    )
```

```python
import jax
import jax.numpy as jnp
from jax import lax
from jax.experimental import pallas as pl
from jax.experimental.pallas import tpu as pltpu
from jax.sharding import PartitionSpec as P

X, Z, Y, C = 4, 8, 4, 2
HD = 128
GROUP = 64
NLEN = 128
NB_DEV = 8
TOK = 256
SCALE = HD**-0.5
LOW = -1e30
BF = jnp.bfloat16
F32 = jnp.float32
VMEM = pl.BlockSpec(memory_space=pltpu.VMEM)
SMEM = pl.BlockSpec(memory_space=pltpu.SMEM)
LIMIT = 60 * 1024 * 1024


def place():
    dp, t = lax.axis_index("dp"), lax.axis_index("tensor")
    return lax.div(dp, Z), lax.rem(dp, Z), lax.div(t, C), lax.rem(t, C)


def device(x, z, y, c):
    return (x * Z + z, y * C + c)


def step_from(i, by, n):
    return lax.rem(i + (by + n), n)


def columns(i, width):
    return pl.ds(pl.multiple_of(i * width, width), width)


def enter(peers):
    barrier = pltpu.get_barrier_semaphore()
    for peer in peers:
        pl.semaphore_signal(barrier, inc=1, device_id=peer, device_id_type=pl.DeviceIdType.MESH)
    pl.semaphore_wait(barrier, len(peers))


class Copies:
    def __init__(self, send, recv):
        self.send, self.recv, self.count, self.started = send, recv, 0, []

    def take(self, n=1):
        first = self.count
        self.count += n
        return first

    def make(self, sem, src, dst, to):
        return pltpu.make_async_remote_copy(
            src_ref=src,
            dst_ref=dst,
            send_sem=self.send.at[sem],
            recv_sem=self.recv.at[sem],
            device_id=to,
            device_id_type=pl.DeviceIdType.MESH,
        )

    def start(self, src, dst, to):
        copy = self.make(self.take(), src, dst, to)
        copy.start()
        self.started.append(copy)
        return copy

    def finish(self):
        for copy in self.started:
            copy.wait_send()


class Gather:
    def __init__(self, copies, first, view, hops, where):
        self.copies, self.first, self.view, self.hops, self.where = copies, first, view, hops, where
        self.sent = [[], []]

    def step(self, s):
        x, z, y, c = self.where
        for way, sign in ((0, 1), (1, -1)):
            if 0 < s <= self.hops[way]:
                self.sent[way][s - 1].wait_recv()
            if s < self.hops[way]:
                block = step_from(z, -sign * s, Z)
                src = self.first if s == 0 else self.view(block)
                to = device(x, step_from(z, sign, Z), y, c)
                self.sent[way].append(self.copies.start(src, self.view(block), to))


class Scatter:
    def __init__(self, copies, part, held, hops, where):
        self.copies, self.part, self.held, self.hops, self.where = copies, part, held, hops, where
        self.sent = [[], []]

    def step(self, s):
        x, z, y, c = self.where
        for way, sign in ((0, 1), (1, -1)):
            n = self.hops[way]
            if 0 < s <= n:
                self.sent[way][s - 1].wait_recv()
            if s < n:
                goal = step_from(z, sign * (n - s), Z)
                if s == 0:
                    src = self.part(goal)
                else:
                    src = self.held(way, s - 1)
                    src[...] = (src[...].astype(F32) + self.part(goal)[...].astype(F32)).astype(BF)
                to = device(x, step_from(z, sign, Z), y, c)
                self.sent[way].append(self.copies.start(src, self.held(way, s), to))

    def total(self):
        z = self.where[1]
        total = self.part(z)[...].astype(F32)
        for way in (0, 1):
            total += self.held(way, self.hops[way] - 1)[...].astype(F32)
        return total


HOPS = ((4, 3), (3, 4))


def spread_kernel(
    ids_ref, q_ref, k_ref, v_ref, w_ref, g_ref,
    idall, qall, ktab, vtab, wf, upall,
    gfull, upp, upr, send, recv, local,
):
    where = x, z, y, c = place()
    t = y * C + c
    depth = w_ref.shape[0] // 4
    width = w_ref.shape[1]
    span = Z * width
    xs = [step_from(x, i, X) for i in range(X)]
    ys = [step_from(y, i, Y) for i in range(Y)]
    other = 1 - c
    enter(
        [device(xs[i], z, y, c) for i in (1, 2, 3)]
        + [device(x, step_from(z, i, Z), y, c) for i in (1, -1)]
        + [device(x, z, ys[i], c) for i in (1, 2, 3)]
        + [device(x, z, y, other)]
    )
    copies = Copies(send, recv)
    kept = []

    def keep(src, dst):
        copy = pltpu.make_async_copy(src, dst, local.at[len(kept)])
        copy.start()
        kept.append(copy)

    keep(g_ref.at[:, columns(x, span)], gfull.at[x, t])
    keep(q_ref.at[:, columns(x, HD)], qall.at[z, x])
    keep(k_ref.at[:, columns(x, HD)], ktab.at[x])
    keep(v_ref.at[:, columns(x, HD)], vtab.at[x])
    keep(w_ref, wf.at[:, columns(z, width)])
    keep(ids_ref, idall.at[z, x])

    g_in = [
        copies.start(g_ref.at[:, columns(xs[i], span)], gfull.at[x, t], device(xs[i], z, y, c))
        for i in (1, 3, 2)
    ]

    def weight_piece(i):
        rows = pl.ds(i * depth, depth)
        return Gather(
            copies, w_ref.at[rows], lambda b: wf.at[rows, columns(b, width)], HOPS[i % 2], where
        )

    def piece(ref, i):
        return Gather(copies, ref.at[z, i], lambda b: ref.at[b, i], HOPS[i % 2], where)

    weights = [weight_piece(i) for i in range(4)]
    asked = [piece(qall, i) for i in range(X)]
    asked.append(
        Gather(copies, idall.at[z], lambda b: idall.at[b], HOPS[0], where),
    )
    upstream = [piece(upall, i) for i in range(X)]
    table_in, q_in, g_y, g_core, up_in = [], [], {}, {}, {}

    def step(pieces, s):
        for one in pieces:
            one.step(s)

    def send_queries():
        for i in (1, 3, 2):
            to = device(xs[i], z, y, c)
            q_in.append(copies.start(q_ref.at[:, columns(xs[i], HD)], qall.at[z, x], to))
            q_in.append(copies.start(ids_ref, idall.at[z, x], to))

    def send_table(src, dst):
        for i in (1, 3, 2):
            to = device(xs[i], z, y, c)
            table_in.append(copies.start(src.at[:, columns(xs[i], HD)], dst.at[x], to))

    def send_rows():
        kept[0].wait()
        for copy in g_in:
            copy.wait_recv()
        for i in range(X):
            block = gfull.at[i, t]
            g_y[i] = [copies.start(block, block, device(x, z, ys[j], c)) for j in (1, 3, 2)]
            g_core[i] = [copies.start(block, block, device(x, z, y, other))]

    def hand_over(i):
        for copy, j in zip(g_y[i], (-1, -3, -2)):
            copy.wait_recv()
            block = gfull.at[i, step_from(y, j, Y) * C + c]
            g_core[i].append(copies.start(block, block, device(x, z, y, other)))

    def multiply(i):
        for copy in g_core[i]:
            copy.wait_recv()
        rows = gfull[i].reshape(TOK, span)
        upp[i] = lax.dot_general(
            rows, wf[...], (((1,), (1,)), ((), ())), preferred_element_type=F32
        ).astype(BF)
        up_in[i] = [
            copies.start(
                upp.at[i, :, columns(xs[j], HD)], upr.at[i, j - 1], device(xs[j], z, y, c)
            )
            for j in (1, 3, 2)
        ]

    def total(i):
        for copy in up_in[i]:
            copy.wait_recv()
        value = upp[i, :, columns(x, HD)].astype(F32)
        for j in range(3):
            value += upr[i, j].astype(F32)
        upall[z, i] = value.astype(BF)
        upstream[i].step(0)

    step(weights, 0)
    send_queries()
    step(weights, 1)
    send_rows()
    step(weights, 2)
    for copy in q_in:
        copy.wait_recv()
    kept[1].wait()
    kept[5].wait()
    send_table(k_ref, ktab)
    step(weights, 3)
    step(asked, 0)
    hand_over(0)
    step(weights, 4)
    kept[4].wait()
    multiply(0)
    hand_over(1)
    step(asked, 1)
    multiply(1)
    hand_over(2)
    step(asked, 2)
    multiply(2)
    hand_over(3)
    total(0)
    total(1)
    step(asked, 3)
    multiply(3)
    step(upstream[:1], 1)
    total(2)
    send_table(v_ref, vtab)
    step(upstream[1:2], 1)
    step(asked, 4)
    step(upstream[:1], 2)
    total(3)
    step(upstream[1:2], 2)
    step(upstream[2:3], 1)
    step(upstream[:1], 3)
    step(upstream[3:], 1)
    step(upstream[1:2], 3)
    step(upstream[2:3], 2)
    step(upstream[:1], 4)
    step(upstream[3:], 2)
    step(upstream[1:2], 4)
    step(upstream[2:], 3)
    step(upstream[2:], 4)
    for copy in table_in:
        copy.wait_recv()
    for copy in kept[2:4]:
        copy.wait()
    copies.finish()


def spread(ids, queries, keys, values, out_weight, grad_out):
    depth, width = out_weight.shape
    rows, head_cols = keys.shape
    return pl.pallas_call(
        spread_kernel,
        out_shape=(
            jax.ShapeDtypeStruct((Z, X) + ids.shape, jnp.int32),
            jax.ShapeDtypeStruct((Z, X, TOK, HD), BF),
            jax.ShapeDtypeStruct((X, rows, HD), BF),
            jax.ShapeDtypeStruct((X, rows, HD), BF),
            jax.ShapeDtypeStruct((depth, Z * width), BF),
            jax.ShapeDtypeStruct((Z, X, TOK, HD), BF),
        ),
        in_specs=[VMEM] * 6,
        out_specs=[VMEM] * 6,
        scratch_shapes=[
            pltpu.VMEM((X, Y * C, grad_out.shape[0], Z * width), BF),
            pltpu.VMEM((X, TOK, head_cols), BF),
            pltpu.VMEM((X, X - 1, TOK, HD), BF),
            pltpu.SemaphoreType.DMA((152,)),
            pltpu.SemaphoreType.DMA((152,)),
            pltpu.SemaphoreType.DMA((8,)),
        ],
        compiler_params=pltpu.CompilerParams(
            collective_id=0, has_side_effects=True, vmem_limit_bytes=LIMIT
        ),
        name="spread",
    )(ids, queries, keys, values, out_weight, grad_out)


def list_uses(ids, groups, names):
    z = lax.rem(lax.axis_index("dp"), Z)

    def add(i, n):
        dp_z, dp_x = lax.shift_right_logical(i, 5), lax.shift_right_logical(i, 3) & 3
        owner, name = (ids[dp_z, dp_x, 0, 2 * (i & 7) + j] for j in (0, 1))
        groups[n] = lax.shift_right_logical(i, 1)
        names[n] = lax.shift_right_logical(owner, 3) * NB_DEV + name
        return n + ((owner & 7) == z).astype(jnp.int32)

    n = lax.fori_loop(0, X * Z * 8, add, jnp.int32(0), unroll=8)
    last = jnp.maximum(n - 1, 0)
    groups[n] = groups[last]
    names[n] = names[last]
    return n


def pair_rows(ref, a, b, size):
    return [ref[pl.ds(pl.multiple_of(i * size, size), size), :] for i in (a, b)]


def pair_scores(first, second, both, left):
    product = lax.dot_general(
        jnp.concatenate([first, second], axis=0),
        both,
        (((1,), (1,)), ((), ())),
        preferred_element_type=F32,
    )
    return jnp.where(left, product[:NLEN], product[NLEN:])


def merge(one, two):
    peak = jnp.maximum(one[0], two[0])
    f, g = jnp.exp(one[0] - peak), jnp.exp(two[0] - peak)
    return peak, f * one[1] + g * two[1], f * one[2] + g * two[2]


def stats_kernel(ids, qall, upall, ktab, vtab, stats, groups, names):
    n = list_uses(ids, groups, names)
    stats[0] = jnp.full(stats.shape[1:], LOW, F32)
    stats[1] = jnp.zeros(stats.shape[1:], F32)
    stats[2] = jnp.zeros(stats.shape[1:], F32)
    left = lax.broadcasted_iota(jnp.int32, (1, 2 * GROUP), 1) < GROUP

    def pair(p, carry):
        a, b = 2 * p, 2 * p + 1
        ga, gb, na, nb = groups[a], groups[b], names[a], names[b]
        qq = jnp.concatenate(pair_rows(qall, ga, gb, GROUP), axis=0)
        uu = jnp.concatenate(pair_rows(upall, ga, gb, GROUP), axis=0)
        scores = pair_scores(*pair_rows(ktab, na, nb, NLEN), qq, left) * SCALE
        grad_probs = pair_scores(*pair_rows(vtab, na, nb, NLEN), uu, left)
        peak = jnp.max(scores, axis=0, keepdims=True)
        exponent = jnp.exp(scores - peak)
        total = jnp.sum(exponent, axis=0, keepdims=True)
        inner = jnp.sum(exponent * grad_probs, axis=0, keepdims=True)
        real = left | (b < n)
        new = (
            jnp.where(real, peak, LOW),
            jnp.where(real, total, 0.0),
            jnp.where(real, inner, 0.0),
        )
        for g, mine in ((ga, left), (gb, jnp.logical_not(left))):
            old = tuple(stats[i, pl.ds(g, 1), :] for i in range(3))
            merged = merge(old, new)
            for i in range(3):
                stats[i, pl.ds(g, 1), :] = jnp.where(mine, merged[i], old[i])
        return carry

    lax.fori_loop(0, (n + 1) // 2, pair, 0)


def stats_of_uses(ids, qall, upall, ktab, vtab):
    return pl.pallas_call(
        stats_kernel,
        out_shape=jax.ShapeDtypeStruct((3, 16 * Z, 2 * GROUP), F32),
        in_specs=[SMEM] + [VMEM] * 4,
        out_specs=VMEM,
        scratch_shapes=[pltpu.SMEM((264,), jnp.int32), pltpu.SMEM((264,), jnp.int32)],
        compiler_params=pltpu.CompilerParams(vmem_limit_bytes=LIMIT),
        name="stats",
    )(ids, qall, upall, ktab, vtab)


def totals_kernel(stats, out, held, send, recv):
    x, z, y, c = place()
    zs = [step_from(z, i, Z) for i in range(Z)]
    order = (1, 7, 2, 6, 3, 5, 4)
    enter([device(x, zs[i], y, c) for i in order])
    copies = Copies(send, recv)
    sent = [
        copies.start(
            stats.at[:, columns(zs[i], 16), :], held.at[i - 1], device(x, zs[i], y, c)
        )
        for i in order
    ]
    own = pl.ds(pl.multiple_of(z * 16, 16), 16)
    state = tuple(stats[i, own, :] for i in range(3))
    for copy, i in zip(sent, order):
        copy.wait_recv()
        state = merge(state, tuple(held[i - 1, j] for j in range(3)))
    state = merge(state, tuple(pltpu.roll(v, GROUP, 1) for v in state))
    out[0, own, :] = state[0] + jnp.log(state[1])
    out[1, own, :] = state[2] / state[1]
    back = out.at[:, own, :]
    sent = [copies.start(back, back, device(x, zs[i], y, c)) for i in order]
    for copy in sent:
        copy.wait_recv()
    copies.finish()


def totals(stats):
    return pl.pallas_call(
        totals_kernel,
        out_shape=jax.ShapeDtypeStruct((2,) + stats.shape[1:], F32),
        in_specs=[VMEM],
        out_specs=VMEM,
        scratch_shapes=[
            pltpu.VMEM((Z - 1, 3, 16, 2 * GROUP), F32),
            pltpu.SemaphoreType.DMA((16,)),
            pltpu.SemaphoreType.DMA((16,)),
        ],
        compiler_params=pltpu.CompilerParams(
            collective_id=1, has_side_effects=True, vmem_limit_bytes=LIMIT
        ),
        name="totals",
    )(stats)


def grads_kernel(
    ids, qall, upall, ktab, vtab, sums, ctx, gq, dkey, dvalue, groups, names, dk, dv
):
    n = list_uses(ids, groups, names)
    for ref in (ctx, gq, dk, dv):
        rows = 512

        @pl.loop(0, ref.shape[0] // rows)
        def _(i, ref=ref):
            ref[pl.ds(pl.multiple_of(i * rows, rows), rows), :] = jnp.zeros((rows, HD), ref.dtype)

    left = lax.broadcasted_iota(jnp.int32, (1, 2 * GROUP), 1) < GROUP
    zero = jnp.zeros((), BF)

    def add(ref, i, size, value):
        at = pl.ds(pl.multiple_of(i * size, size), size)
        ref[at, :] = (ref[at, :].astype(F32) + value).astype(ref.dtype)

    def dot(a, b):
        return jnp.dot(a, b, preferred_element_type=F32)

    def pair(p, carry):
        a, b = 2 * p, 2 * p + 1
        ga, gb, na, nb = groups[a], groups[b], names[a], names[b]
        qq = jnp.concatenate(pair_rows(qall, ga, gb, GROUP), axis=0)
        uu = jnp.concatenate(pair_rows(upall, ga, gb, GROUP), axis=0)
        keys = pair_rows(ktab, na, nb, NLEN)
        values = pair_rows(vtab, na, nb, NLEN)
        scores = pair_scores(*keys, qq, left) * SCALE
        grad_probs = pair_scores(*values, uu, left)
        log_total = jnp.where(left, sums[0, pl.ds(ga, 1), :], sums[0, pl.ds(gb, 1), :])
        inner = jnp.where(left, sums[1, pl.ds(ga, 1), :], sums[1, pl.ds(gb, 1), :])
        real = left | (b < n)
        prob = jnp.where(real, jnp.exp(scores - log_total), 0.0)
        grad_scores = prob * (grad_probs - inner)
        prob_t = prob.T.astype(BF)
        grad_t = grad_scores.T.astype(BF)
        prob, grad_scores = prob.astype(BF), grad_scores.astype(BF)

        def halves(v):
            return jnp.concatenate([jnp.where(left, v, zero), jnp.where(left, zero, v)], axis=0)

        context = dot(prob_t, jnp.concatenate(values, axis=1))
        grad_q = dot(grad_t, jnp.concatenate(keys, axis=1)) * SCALE
        grad_v = dot(halves(prob), uu)
        grad_k = dot(halves(grad_scores), qq) * SCALE
        add(ctx, ga, GROUP, context[:GROUP, :HD])
        add(ctx, gb, GROUP, context[GROUP:, HD:])
        add(gq, ga, GROUP, grad_q[:GROUP, :HD])
        add(gq, gb, GROUP, grad_q[GROUP:, HD:])
        add(dv, na, NLEN, grad_v[:NLEN])
        add(dv, nb, NLEN, grad_v[NLEN:])
        add(dk, na, NLEN, grad_k[:NLEN])
        add(dk, nb, NLEN, grad_k[NLEN:])
        return carry

    lax.fori_loop(0, (n + 1) // 2, pair, 0)
    for src, dst in ((dk, dkey), (dv, dvalue)):
        rows = 512

        @pl.loop(0, src.shape[0] // rows)
        def _(i, src=src, dst=dst):
            at = pl.ds(pl.multiple_of(i * rows, rows), rows)
            dst[at, :] = src[at, :].astype(BF)


def grads_of_uses(ids, qall, upall, ktab, vtab, sums):
    tokens, rows = qall.shape[0], ktab.shape[0]
    return pl.pallas_call(
        grads_kernel,
        out_shape=(
            jax.ShapeDtypeStruct((tokens, HD), BF),
            jax.ShapeDtypeStruct((tokens, HD), BF),
            jax.ShapeDtypeStruct((rows, HD), BF),
            jax.ShapeDtypeStruct((rows, HD), BF),
        ),
        in_specs=[SMEM] + [VMEM] * 5,
        out_specs=[VMEM] * 4,
        scratch_shapes=[
            pltpu.SMEM((264,), jnp.int32),
            pltpu.SMEM((264,), jnp.int32),
            pltpu.VMEM((rows, HD), F32),
            pltpu.VMEM((rows, HD), F32),
        ],
        compiler_params=pltpu.CompilerParams(vmem_limit_bytes=LIMIT),
        name="grads",
    )(ids, qall, upall, ktab, vtab, sums)


def collect_kernel(
    ctx, gq, dkey, dvalue, wf,
    out, gq_out, dk_out, dv_out,
    held, ctx4, part, core_in, y_in, done, gq_done, send, recv, out_send, out_recv, local,
):
    where = x, z, y, c = place()
    t = y * C + c
    span = wf.shape[1]
    xs = [step_from(x, i, X) for i in range(X)]
    ys = [step_from(y, i, Y) for i in range(Y)]
    other = 1 - c
    enter(
        [device(xs[i], z, y, c) for i in (1, 2, 3)]
        + [device(x, step_from(z, i, Z), y, c) for i in (1, -1)]
        + [device(x, z, ys[i], c) for i in (1, 2, 3)]
        + [device(x, z, y, other)]
    )
    copies = Copies(send, recv)
    kept = []

    def keep(src, dst):
        copy = pltpu.make_async_copy(src, dst, local.at[len(kept)])
        copy.start()
        kept.append(copy)

    def piece(ref, i, n):
        return Scatter(
            copies,
            lambda b: ref.at[b, i],
            lambda way, s: held.at[n, 4 * way + s],
            HOPS[n % 2],
            where,
        )

    pieces = [piece(ctx, i, i) for i in range(X)]
    pieces += [piece(gq, xs[i], X + i) for i in range(X)]
    table_in, ctx_in, core_sent, y_sent, gq_sent = [], {}, {}, {}, []

    def tables():
        for src, dst in ((dkey, dk_out), (dvalue, dv_out)):
            keep(src.at[x], dst.at[:, columns(x, HD)])
            for i in (1, 3, 2):
                table_in.append(
                    copies.start(src.at[xs[i]], dst.at[:, columns(x, HD)], device(xs[i], z, y, c))
                )

    def share(i):
        mine = ctx4.at[i, :, columns(x, HD)]
        mine[...] = pieces[i].total().astype(BF)
        ctx_in[i] = [copies.start(mine, mine, device(xs[j], z, y, c)) for j in (1, 3, 2)]

    def multiply(i):
        for copy in ctx_in[i]:
            copy.wait_recv()
        for j in range(2):
            cols = pl.ds(j * (span // 2), span // 2)
            product = jnp.dot(ctx4[i], wf[:, cols], preferred_element_type=F32).astype(BF)
            part[i, :, :, :, cols] = product.reshape(Y, C, TOK // (Y * C), span // 2)
        core_sent[i] = copies.start(part.at[i, :, other], core_in.at[i], device(x, z, y, other))

    def join(i):
        core_sent[i].wait_recv()
        core_in[i] = (core_in[i].astype(F32) + part[i, :, c].astype(F32)).astype(BF)
        y_sent[i] = [
            copies.start(core_in.at[i, ys[j]], y_in.at[i, j - 1], device(x, z, ys[j], c))
            for j in (1, 3, 2)
        ]

    def total(i):
        for copy in y_sent[i]:
            copy.wait_recv()
        value = core_in[i, y].astype(F32)
        for j in range(3):
            value += y_in[i, j].astype(F32)
        done[i] = value.astype(BF)
        goal = out.at[:, columns(x, span)]

        @pl.when(x == i)
        def _():
            copy = pltpu.make_async_copy(done.at[i], goal, local.at[7])
            copy.start()
            copy.wait()

        @pl.when(x != i)
        def _():
            sem = step_from(i - x, 0, X)
            pltpu.make_async_remote_copy(
                src_ref=done.at[i],
                dst_ref=goal,
                send_sem=out_send.at[sem],
                recv_sem=out_recv.at[sem],
                device_id=device(i, z, y, c),
                device_id_type=pl.DeviceIdType.MESH,
            ).start()

    def queries(i):
        gq_done[i] = pieces[X + i].total().astype(BF)
        goal = gq_out.at[:, columns(x, HD)]
        if i == 0:
            keep(gq_done.at[i], goal)
        else:
            gq_sent.append(copies.start(gq_done.at[i], goal, device(xs[i], z, y, c)))

    def step(pieces, s):
        for one in pieces:
            one.step(s)

    contexts, grads = pieces[:X], pieces[X:]
    step(contexts, 0)
    tables()
    for s in (1, 2, 3):
        step(contexts, s)
    step(grads, 0)
    for i in range(X):
        contexts[i].step(4)
        share(i)
    step(grads, 1)
    multiply(0)
    multiply(1)
    join(0)
    multiply(2)
    join(1)
    step(grads, 2)
    multiply(3)
    join(2)
    join(3)
    step(grads, 3)
    total(0)
    for i in range(X):
        grads[i].step(4)
        queries(i)
    for i in (1, 2, 3):
        total(i)
    for copy in table_in + gq_sent:
        copy.wait_recv()
    for i in (1, 2, 3):
        copy = pltpu.make_async_remote_copy(
            src_ref=done.at[0],
            dst_ref=out.at[:, columns(xs[i], span)],
            send_sem=out_send.at[i],
            recv_sem=out_recv.at[i],
            device_id=device(xs[i], z, y, c),
            device_id_type=pl.DeviceIdType.MESH,
        )
        copy.wait_recv()
        copy.wait_send()
    for copy in kept:
        copy.wait()
    copies.finish()


def collect(ctx, gq, dkey, dvalue, wf):
    head_cols, span = wf.shape
    rows = dkey.shape[1]
    slots = TOK // (Y * C)
    return pl.pallas_call(
        collect_kernel,
        out_shape=(
            jax.ShapeDtypeStruct((slots, X * span), BF),
            jax.ShapeDtypeStruct((TOK, head_cols), BF),
            jax.ShapeDtypeStruct((rows, head_cols), BF),
            jax.ShapeDtypeStruct((rows, head_cols), BF),
        ),
        in_specs=[VMEM] * 5,
        out_specs=[VMEM] * 4,
        scratch_shapes=[
            pltpu.VMEM((2 * X, 8, TOK, HD), BF),
            pltpu.VMEM((X, TOK, head_cols), BF),
            pltpu.VMEM((X, Y, C, slots, span), BF),
            pltpu.VMEM((X, Y, slots, span), BF),
            pltpu.VMEM((X, Y - 1, slots, span), BF),
            pltpu.VMEM((X, slots, span), BF),
            pltpu.VMEM((X, TOK, HD), BF),
            pltpu.SemaphoreType.DMA((120,)),
            pltpu.SemaphoreType.DMA((120,)),
            pltpu.SemaphoreType.DMA((4,)),
            pltpu.SemaphoreType.DMA((4,)),
            pltpu.SemaphoreType.DMA((8,)),
        ],
        compiler_params=pltpu.CompilerParams(
            collective_id=2, has_side_effects=True, vmem_limit_bytes=LIMIT
        ),
        name="collect",
    )(ctx, gq, dkey, dvalue, wf)


def shards(queries, keys, values, out_weight, grad_out, neighbour_owner, neighbour_local):
    ids = jnp.stack([neighbour_owner, neighbour_local], axis=-1).reshape(1, -1)
    ids = jnp.pad(ids, ((0, 0), (0, 128 - ids.shape[1])))
    ids, qall, ktab, vtab, wf, upall = spread(ids, queries, keys, values, out_weight, grad_out)
    qall, upall = (a.reshape(Z * X * TOK, HD) for a in (qall, upall))
    ktab, vtab = (a.reshape(X * keys.shape[0], HD) for a in (ktab, vtab))
    sums = totals(stats_of_uses(ids, qall, upall, ktab, vtab))
    ctx, gq, dkey, dvalue = grads_of_uses(ids, qall, upall, ktab, vtab, sums)
    ctx, gq = (a.reshape(Z, X, TOK, HD) for a in (ctx, gq))
    dkey, dvalue = (a.reshape((X,) + keys.shape[:1] + (HD,)) for a in (dkey, dvalue))
    out, grad_queries, grad_keys, grad_values = collect(ctx, gq, dkey, dvalue, wf)
    return out, grad_queries, grad_keys.astype(F32), grad_values.astype(F32)


def solution(mesh):
    return jax.shard_map(
        shards,
        mesh=mesh,
        in_specs=(
            P("dp", "tensor"),
            P("dp", "tensor"),
            P("dp", "tensor"),
            P("tensor", "dp"),
            P(("dp", "tensor"), None),
            P("dp", None),
            P("dp", None),
        ),
        out_specs=(
            P(("dp", "tensor"), None),
            P("dp", "tensor"),
            P("dp", "tensor"),
            P("dp", "tensor"),
        ),
        check_vma=False,
    )
```

```python
import jax
import jax.numpy as jnp
from jax import lax
from jax.experimental import pallas as pl
from jax.experimental.pallas import tpu as pltpu
from jax.sharding import PartitionSpec as P

X, Z, Y, C = 4, 8, 4, 2
HD = 128
GROUP = 64
NLEN = 128
NB_DEV = 8
TOK = 256
SCALE = HD**-0.5
LOW = -1e30
BF = jnp.bfloat16
F32 = jnp.float32
VMEM = pl.BlockSpec(memory_space=pltpu.VMEM)
SMEM = pl.BlockSpec(memory_space=pltpu.SMEM)
LIMIT = 28 * 1024 * 1024


def place():
    dp, t = lax.axis_index("dp"), lax.axis_index("tensor")
    return lax.div(dp, Z), lax.rem(dp, Z), lax.div(t, C), lax.rem(t, C)


def device(x, z, y, c):
    return (x * Z + z, y * C + c)


def step_from(i, by, n):
    return lax.rem(i + (by + n), n)


def columns(i, width):
    return pl.ds(pl.multiple_of(i * width, width), width)


def enter(peers):
    barrier = pltpu.get_barrier_semaphore()
    for peer in peers:
        pl.semaphore_signal(barrier, inc=1, device_id=peer, device_id_type=pl.DeviceIdType.MESH)
    pl.semaphore_wait(barrier, len(peers))


class Copies:
    def __init__(self, send, recv):
        self.send, self.recv, self.count, self.started = send, recv, 0, []

    def take(self, n=1):
        first = self.count
        self.count += n
        return first

    def make(self, sem, src, dst, to):
        return pltpu.make_async_remote_copy(
            src_ref=src,
            dst_ref=dst,
            send_sem=self.send.at[sem],
            recv_sem=self.recv.at[sem],
            device_id=to,
            device_id_type=pl.DeviceIdType.MESH,
        )

    def start(self, src, dst, to):
        copy = self.make(self.take(), src, dst, to)
        copy.start()
        self.started.append(copy)
        return copy

    def finish(self):
        for copy in self.started:
            copy.wait_send()


class Gather:
    def __init__(self, copies, first, view, hops, ring, arrived=None):
        self.copies, self.first, self.view, self.hops = copies, first, view, hops
        self.place, self.size, self.sides = ring
        self.arrived = arrived
        self.sent = [[], []]

    def step(self, s):
        for way, sign in ((0, 1), (1, -1)):
            block = step_from(self.place, -sign * s, self.size)
            if 0 < s <= self.hops[way]:
                self.sent[way][s - 1].wait_recv()
            if s < self.hops[way]:
                src = self.first if s == 0 else self.view(block)
                self.sent[way].append(self.copies.start(src, self.view(block), self.sides[way]))
            if self.arrived is not None and 0 < s <= self.hops[way]:
                self.arrived(block)


class Scatter:
    def __init__(self, copies, part, held, hops, ring):
        self.copies, self.part, self.held, self.hops = copies, part, held, hops
        self.place, self.size, self.sides = ring
        self.sent = [[], []]

    def step(self, s):
        for way, sign in ((0, 1), (1, -1)):
            n = self.hops[way]
            if 0 < s <= n:
                self.sent[way][s - 1].wait_recv()
            if s < n:
                goal = step_from(self.place, sign * (n - s), self.size)
                if s == 0:
                    src = self.part(goal)
                else:
                    src = self.held(way, s - 1)
                    src[...] = (src[...].astype(F32) + self.part(goal)[...].astype(F32)).astype(BF)
                self.sent[way].append(self.copies.start(src, self.held(way, s), self.sides[way]))

    def total(self):
        total = self.part(self.place)[...].astype(F32)
        for way in (0, 1):
            total += self.held(way, self.hops[way] - 1)[...].astype(F32)
        return total


def rings(x, z, y, c):
    along_z = z, Z, tuple(device(x, step_from(z, i, Z), y, c) for i in (1, -1))
    along_y = y, Y, tuple(device(x, z, step_from(y, i, Y), c) for i in (1, -1))
    return along_z, along_y


HOPS = ((4, 3), (3, 4))
HOPS_Y = ((2, 1), (1, 2))


def spread_kernel(
    ids_ref, q_ref, k_ref, v_ref, w_ref, g_ref,
    idall, qall, ktab, vtab, wf, upall,
    gfull, upp, upr, send, recv, local,
):
    x, z, y, c = place()
    t = y * C + c
    depth = w_ref.shape[0] // 4
    width = w_ref.shape[1]
    span = Z * width
    xs = [step_from(x, i, X) for i in range(X)]
    along_z, along_y = rings(x, z, y, c)
    sibling = device(x, z, y, 1 - c)
    enter(
        [device(xs[i], z, y, c) for i in (1, 2, 3)]
        + list(along_z[2])
        + list(along_y[2])
        + [sibling]
    )
    copies = Copies(send, recv)
    kept = []

    def keep(src, dst):
        copy = pltpu.make_async_copy(src, dst, local.at[len(kept)])
        copy.start()
        kept.append(copy)

    keep(g_ref.at[:, columns(x, span)], gfull.at[x, t])
    keep(q_ref.at[:, columns(x, HD)], qall.at[z, x])
    keep(k_ref.at[:, columns(x, HD)], ktab.at[x])
    keep(v_ref.at[:, columns(x, HD)], vtab.at[x])
    keep(w_ref, wf.at[:, columns(z, width)])
    keep(ids_ref, idall.at[z, x])

    g_in = [
        copies.start(g_ref.at[:, columns(xs[i], span)], gfull.at[x, t], device(xs[i], z, y, c))
        for i in (1, 3, 2)
    ]

    def weight_piece(i):
        rows = pl.ds(i * depth, depth)
        return Gather(
            copies, w_ref.at[rows], lambda b: wf.at[rows, columns(b, width)], HOPS[i % 2], along_z
        )

    def piece(ref, i):
        return Gather(copies, ref.at[z, i], lambda b: ref.at[b, i], HOPS[i % 2], along_z)

    weights = [weight_piece(i) for i in range(4)]
    asked = [piece(qall, i) for i in range(X)]
    asked.append(
        Gather(copies, idall.at[z], lambda b: idall.at[b], HOPS[0], along_z),
    )
    upstream = [piece(upall, i) for i in range(X)]
    table_in, q_in, g_core, up_in = [], [], {}, {}

    def step(pieces, s):
        for one in pieces:
            one.step(s)

    def send_queries():
        for i in (1, 3, 2):
            to = device(xs[i], z, y, c)
            q_in.append(copies.start(q_ref.at[:, columns(xs[i], HD)], qall.at[z, x], to))
            q_in.append(copies.start(ids_ref, idall.at[z, x], to))

    def send_table(src, dst):
        for i in (1, 3, 2):
            to = device(xs[i], z, y, c)
            table_in.append(copies.start(src.at[:, columns(xs[i], HD)], dst.at[x], to))

    def hand_over(i, block):
        block = gfull.at[i, block * C + c]
        g_core[i].append(copies.start(block, block, sibling))

    def rows_piece(i):
        return Gather(
            copies,
            gfull.at[i, t],
            lambda b: gfull.at[i, b * C + c],
            HOPS_Y[i % 2],
            along_y,
            lambda b: hand_over(i, b),
        )

    rows = [rows_piece(i) for i in range(X)]

    def send_rows(i):
        rows[i].step(0)
        g_core[i] = []
        hand_over(i, y)

    def multiply(i):
        for copy in g_core[i]:
            copy.wait_recv()
        upp[i] = lax.dot_general(
            gfull[i].reshape(TOK, span), wf[...], (((1,), (1,)), ((), ())), preferred_element_type=F32
        ).astype(BF)
        up_in[i] = [
            copies.start(
                upp.at[i, :, columns(xs[j], HD)], upr.at[i, j - 1], device(xs[j], z, y, c)
            )
            for j in (1, 3, 2)
        ]

    def total(i):
        for copy in up_in[i]:
            copy.wait_recv()
        value = upp[i, :, columns(x, HD)].astype(F32)
        for j in range(3):
            value += upr[i, j].astype(F32)
        upall[z, i] = value.astype(BF)
        upstream[i].step(0)

    step(weights, 0)
    send_queries()
    step(weights, 1)
    kept[0].wait()
    for copy in g_in:
        copy.wait_recv()
    send_rows(0)
    send_rows(1)
    step(weights, 2)
    for copy in q_in:
        copy.wait_recv()
    kept[1].wait()
    kept[5].wait()
    step(rows[:1], 1)
    step(weights[:2], 3)
    step(rows[1:2], 1)
    send_rows(2)
    send_rows(3)
    step(weights[2:], 3)
    step(asked, 0)
    send_table(k_ref, ktab)
    step(rows[:2], 2)
    step(weights, 4)
    kept[4].wait()
    multiply(0)
    step(asked[:2], 1)
    multiply(1)
    step(rows[2:3], 1)
    step(asked[2:], 1)
    step(rows[3:], 1)
    step(asked, 2)
    step(rows[2:], 2)
    multiply(2)
    total(0)
    multiply(3)
    total(1)
    step(asked, 3)
    total(2)
    total(3)
    send_table(v_ref, vtab)
    step(asked, 4)
    for s in (1, 2, 3, 4):
        step(upstream, s)
    for copy in table_in:
        copy.wait_recv()
    for copy in kept[2:4]:
        copy.wait()
    copies.finish()


def spread(ids, queries, keys, values, out_weight, grad_out):
    depth, width = out_weight.shape
    rows, head_cols = keys.shape
    return pl.pallas_call(
        spread_kernel,
        out_shape=(
            jax.ShapeDtypeStruct((Z, X) + ids.shape, jnp.int32),
            jax.ShapeDtypeStruct((Z, X, TOK, HD), BF),
            jax.ShapeDtypeStruct((X, rows, HD), BF),
            jax.ShapeDtypeStruct((X, rows, HD), BF),
            jax.ShapeDtypeStruct((depth, Z * width), BF),
            jax.ShapeDtypeStruct((Z, X, TOK, HD), BF),
        ),
        in_specs=[VMEM] * 6,
        out_specs=[VMEM] * 6,
        scratch_shapes=[
            pltpu.VMEM((X, Y * C, grad_out.shape[0], Z * width), BF),
            pltpu.VMEM((X, TOK, head_cols), BF),
            pltpu.VMEM((X, X - 1, TOK, HD), BF),
            pltpu.SemaphoreType.DMA((152,)),
            pltpu.SemaphoreType.DMA((152,)),
            pltpu.SemaphoreType.DMA((8,)),
        ],
        compiler_params=pltpu.CompilerParams(
            collective_id=0, has_side_effects=True, vmem_limit_bytes=LIMIT
        ),
        name="spread",
    )(ids, queries, keys, values, out_weight, grad_out)


def list_uses(ids, groups, names):
    z = lax.rem(lax.axis_index("dp"), Z)

    def add(i, n):
        dp_z, dp_x = lax.shift_right_logical(i, 5), lax.shift_right_logical(i, 3) & 3
        owner, name = (ids[dp_z, dp_x, 0, 2 * (i & 7) + j] for j in (0, 1))
        groups[n] = lax.shift_right_logical(i, 1)
        names[n] = lax.shift_right_logical(owner, 3) * NB_DEV + name
        return n + ((owner & 7) == z).astype(jnp.int32)

    n = lax.fori_loop(0, X * Z * 8, add, jnp.int32(0), unroll=8)
    last = jnp.maximum(n - 1, 0)
    groups[n] = groups[last]
    names[n] = names[last]
    return n


def pair_rows(ref, a, b, size):
    return [ref[pl.ds(pl.multiple_of(i * size, size), size), :] for i in (a, b)]


def pair_scores(first, second, both, left):
    product = lax.dot_general(
        jnp.concatenate([first, second], axis=0),
        both,
        (((1,), (1,)), ((), ())),
        preferred_element_type=F32,
    )
    return jnp.where(left, product[:NLEN], product[NLEN:])


def merge(one, two):
    peak = jnp.maximum(one[0], two[0])
    f, g = jnp.exp(one[0] - peak), jnp.exp(two[0] - peak)
    return peak, f * one[1] + g * two[1], f * one[2] + g * two[2]


def stats_kernel(ids, qall, upall, ktab, vtab, stats, groups, names):
    n = list_uses(ids, groups, names)
    stats[0] = jnp.full(stats.shape[1:], LOW, F32)
    stats[1] = jnp.zeros(stats.shape[1:], F32)
    stats[2] = jnp.zeros(stats.shape[1:], F32)
    left = lax.broadcasted_iota(jnp.int32, (1, 2 * GROUP), 1) < GROUP

    def pair(p, carry):
        a, b = 2 * p, 2 * p + 1
        ga, gb, na, nb = groups[a], groups[b], names[a], names[b]
        qq = jnp.concatenate(pair_rows(qall, ga, gb, GROUP), axis=0)
        uu = jnp.concatenate(pair_rows(upall, ga, gb, GROUP), axis=0)
        scores = pair_scores(*pair_rows(ktab, na, nb, NLEN), qq, left) * SCALE
        grad_probs = pair_scores(*pair_rows(vtab, na, nb, NLEN), uu, left)
        peak = jnp.max(scores, axis=0, keepdims=True)
        exponent = jnp.exp(scores - peak)
        total = jnp.sum(exponent, axis=0, keepdims=True)
        inner = jnp.sum(exponent * grad_probs, axis=0, keepdims=True)
        real = left | (b < n)
        new = (
            jnp.where(real, peak, LOW),
            jnp.where(real, total, 0.0),
            jnp.where(real, inner, 0.0),
        )
        for g, mine in ((ga, left), (gb, jnp.logical_not(left))):
            old = tuple(stats[i, pl.ds(g, 1), :] for i in range(3))
            merged = merge(old, new)
            for i in range(3):
                stats[i, pl.ds(g, 1), :] = jnp.where(mine, merged[i], old[i])
        return carry

    lax.fori_loop(0, (n + 1) // 2, pair, 0)


def stats_of_uses(ids, qall, upall, ktab, vtab):
    return pl.pallas_call(
        stats_kernel,
        out_shape=jax.ShapeDtypeStruct((3, 16 * Z, 2 * GROUP), F32),
        in_specs=[SMEM] + [VMEM] * 4,
        out_specs=VMEM,
        scratch_shapes=[pltpu.SMEM((264,), jnp.int32), pltpu.SMEM((264,), jnp.int32)],
        compiler_params=pltpu.CompilerParams(vmem_limit_bytes=LIMIT),
        name="stats",
    )(ids, qall, upall, ktab, vtab)


def totals_kernel(stats, out, held, send, recv):
    x, z, y, c = place()
    zs = [step_from(z, i, Z) for i in range(Z)]
    order = (1, 7, 2, 6, 3, 5, 4)
    enter([device(x, zs[i], y, c) for i in order])
    copies = Copies(send, recv)
    sent = [
        copies.start(
            stats.at[:, columns(zs[i], 16), :], held.at[i - 1], device(x, zs[i], y, c)
        )
        for i in order
    ]
    own = pl.ds(pl.multiple_of(z * 16, 16), 16)
    state = tuple(stats[i, own, :] for i in range(3))
    for copy, i in zip(sent, order):
        copy.wait_recv()
        state = merge(state, tuple(held[i - 1, j] for j in range(3)))
    state = merge(state, tuple(pltpu.roll(v, GROUP, 1) for v in state))
    out[0, own, :] = state[0] + jnp.log(state[1])
    out[1, own, :] = state[2] / state[1]
    back = out.at[:, own, :]
    sent = [copies.start(back, back, device(x, zs[i], y, c)) for i in order]
    for copy in sent:
        copy.wait_recv()
    copies.finish()


def totals(stats):
    return pl.pallas_call(
        totals_kernel,
        out_shape=jax.ShapeDtypeStruct((2,) + stats.shape[1:], F32),
        in_specs=[VMEM],
        out_specs=VMEM,
        scratch_shapes=[
            pltpu.VMEM((Z - 1, 3, 16, 2 * GROUP), F32),
            pltpu.SemaphoreType.DMA((16,)),
            pltpu.SemaphoreType.DMA((16,)),
        ],
        compiler_params=pltpu.CompilerParams(
            collective_id=1, has_side_effects=True, vmem_limit_bytes=LIMIT
        ),
        name="totals",
    )(stats)


def grads_kernel(
    ids, qall, upall, ktab, vtab, sums, ctx, gq, dkey, dvalue, groups, names, dk, dv
):
    n = list_uses(ids, groups, names)
    for ref in (ctx, gq, dk, dv):
        rows = 512

        @pl.loop(0, ref.shape[0] // rows)
        def _(i, ref=ref):
            ref[pl.ds(pl.multiple_of(i * rows, rows), rows), :] = jnp.zeros((rows, HD), ref.dtype)

    left = lax.broadcasted_iota(jnp.int32, (1, 2 * GROUP), 1) < GROUP
    zero = jnp.zeros((), BF)

    def add(ref, i, size, value):
        at = pl.ds(pl.multiple_of(i * size, size), size)
        ref[at, :] = (ref[at, :].astype(F32) + value).astype(ref.dtype)

    def dot(a, b):
        return jnp.dot(a, b, preferred_element_type=F32)

    def pair(p, carry):
        a, b = 2 * p, 2 * p + 1
        ga, gb, na, nb = groups[a], groups[b], names[a], names[b]
        qq = jnp.concatenate(pair_rows(qall, ga, gb, GROUP), axis=0)
        uu = jnp.concatenate(pair_rows(upall, ga, gb, GROUP), axis=0)
        keys = pair_rows(ktab, na, nb, NLEN)
        values = pair_rows(vtab, na, nb, NLEN)
        scores = pair_scores(*keys, qq, left) * SCALE
        grad_probs = pair_scores(*values, uu, left)
        log_total = jnp.where(left, sums[0, pl.ds(ga, 1), :], sums[0, pl.ds(gb, 1), :])
        inner = jnp.where(left, sums[1, pl.ds(ga, 1), :], sums[1, pl.ds(gb, 1), :])
        real = left | (b < n)
        prob = jnp.where(real, jnp.exp(scores - log_total), 0.0)
        grad_scores = prob * (grad_probs - inner)
        prob_t = prob.T.astype(BF)
        grad_t = grad_scores.T.astype(BF)
        prob, grad_scores = prob.astype(BF), grad_scores.astype(BF)

        def halves(v):
            return jnp.concatenate([jnp.where(left, v, zero), jnp.where(left, zero, v)], axis=0)

        context = dot(prob_t, jnp.concatenate(values, axis=1))
        grad_q = dot(grad_t, jnp.concatenate(keys, axis=1)) * SCALE
        grad_v = dot(halves(prob), uu)
        grad_k = dot(halves(grad_scores), qq) * SCALE
        add(ctx, ga, GROUP, context[:GROUP, :HD])
        add(ctx, gb, GROUP, context[GROUP:, HD:])
        add(gq, ga, GROUP, grad_q[:GROUP, :HD])
        add(gq, gb, GROUP, grad_q[GROUP:, HD:])
        add(dv, na, NLEN, grad_v[:NLEN])
        add(dv, nb, NLEN, grad_v[NLEN:])
        add(dk, na, NLEN, grad_k[:NLEN])
        add(dk, nb, NLEN, grad_k[NLEN:])
        return carry

    lax.fori_loop(0, (n + 1) // 2, pair, 0)
    for src, dst in ((dk, dkey), (dv, dvalue)):
        rows = 512

        @pl.loop(0, src.shape[0] // rows)
        def _(i, src=src, dst=dst):
            at = pl.ds(pl.multiple_of(i * rows, rows), rows)
            dst[at, :] = src[at, :].astype(BF)


def grads_of_uses(ids, qall, upall, ktab, vtab, sums):
    tokens, rows = qall.shape[0], ktab.shape[0]
    return pl.pallas_call(
        grads_kernel,
        out_shape=(
            jax.ShapeDtypeStruct((tokens, HD), BF),
            jax.ShapeDtypeStruct((tokens, HD), BF),
            jax.ShapeDtypeStruct((rows, HD), BF),
            jax.ShapeDtypeStruct((rows, HD), BF),
        ),
        in_specs=[SMEM] + [VMEM] * 5,
        out_specs=[VMEM] * 4,
        scratch_shapes=[
            pltpu.SMEM((264,), jnp.int32),
            pltpu.SMEM((264,), jnp.int32),
            pltpu.VMEM((rows, HD), F32),
            pltpu.VMEM((rows, HD), F32),
        ],
        compiler_params=pltpu.CompilerParams(vmem_limit_bytes=LIMIT),
        name="grads",
    )(ids, qall, upall, ktab, vtab, sums)


def collect_kernel(
    ctx, gq, dkey, dvalue, wf,
    out, gq_out, dk_out, dv_out,
    held, ctx4, ctx_other, wf_other, part, y_held, done, gq_done,
    send, recv, out_send, out_recv, local,
):
    x, z, y, c = place()
    head_cols, span = wf.shape
    slots = TOK // (Y * C)
    xs = [step_from(x, i, X) for i in range(X)]
    along_z, along_y = rings(x, z, y, c)
    sibling = device(x, z, y, 1 - c)
    enter(
        [device(xs[i], z, y, c) for i in (1, 2, 3)]
        + list(along_z[2])
        + list(along_y[2])
        + [sibling]
    )
    copies = Copies(send, recv)
    kept = []

    def keep(src, dst):
        copy = pltpu.make_async_copy(src, dst, local.at[len(kept)])
        copy.start()
        kept.append(copy)

    def piece(ref, i, n):
        return Scatter(
            copies,
            lambda b: ref.at[b, i],
            lambda way, s: held.at[n, 4 * way + s],
            HOPS[n % 2],
            along_z,
        )

    def out_piece(i):
        return Scatter(
            copies,
            lambda b: part.at[i, b],
            lambda way, s: y_held.at[i, 2 * way + s],
            HOPS_Y[i % 2],
            along_y,
        )

    contexts = [piece(ctx, i, i) for i in range(X)]
    grads = [piece(gq, xs[i], X + i) for i in range(X)]
    outs = [out_piece(i) for i in range(X)]
    table_in, ctx_in, core_in, gq_sent = [], {}, {}, []

    def step(pieces, s):
        for one in pieces:
            one.step(s)

    def send_table(src, dst):
        keep(src.at[x], dst.at[:, columns(x, HD)])
        for i in (1, 3, 2):
            table_in.append(
                copies.start(src.at[xs[i]], dst.at[:, columns(x, HD)], device(xs[i], z, y, c))
            )

    def share(i):
        mine = ctx4.at[i, :, :, :, columns(x, HD)]
        mine[...] = contexts[i].total().astype(BF).reshape(Y, C, slots, HD)
        ctx_in[i] = [copies.start(mine, mine, device(xs[j], z, y, c)) for j in (1, 3, 2)]

    def swap(i):
        for copy in ctx_in[i]:
            copy.wait_recv()
        core_in[i] = copies.start(ctx4.at[i, :, 1 - c], ctx_other.at[i], sibling)

    def multiply(i):
        core_in[i].wait_recv()
        mine = ctx4[i, :, c].reshape(Y * slots, head_cols)
        others = ctx_other[i].reshape(Y * slots, head_cols)
        for j in range(2):
            cols = pl.ds(j * (span // 2), span // 2)
            product = jnp.dot(mine, wf[:, cols], preferred_element_type=F32)
            product += jnp.dot(others, wf_other[:, cols], preferred_element_type=F32)
            part[i, :, :, cols] = product.astype(BF).reshape(Y, slots, span // 2)
        outs[i].step(0)

    def finish_out(i):
        outs[i].step(2)
        done[i] = outs[i].total().astype(BF)
        goal = out.at[:, columns(x, span)]

        @pl.when(x == i)
        def _():
            copy = pltpu.make_async_copy(done.at[i], goal, local.at[7])
            copy.start()
            copy.wait()

        @pl.when(x != i)
        def _():
            sem = step_from(i - x, 0, X)
            pltpu.make_async_remote_copy(
                src_ref=done.at[i],
                dst_ref=goal,
                send_sem=out_send.at[sem],
                recv_sem=out_recv.at[sem],
                device_id=device(i, z, y, c),
                device_id_type=pl.DeviceIdType.MESH,
            ).start()

    def queries(i):
        gq_done[i] = grads[i].total().astype(BF)
        goal = gq_out.at[:, columns(x, HD)]
        if i == 0:
            keep(gq_done.at[i], goal)
        else:
            gq_sent.append(copies.start(gq_done.at[i], goal, device(xs[i], z, y, c)))

    step(contexts, 0)
    weight_in = copies.start(wf, wf_other, sibling)
    send_table(dkey, dk_out)
    send_table(dvalue, dv_out)
    for s in (1, 2, 3):
        step(contexts, s)
    step(grads, 0)
    for i in range(X):
        contexts[i].step(4)
        share(i)
    weight_in.wait_recv()
    swap(0)
    step(grads[:2], 1)
    multiply(0)
    swap(1)
    step(grads[2:], 1)
    multiply(1)
    swap(2)
    step(grads[:2], 2)
    multiply(2)
    swap(3)
    step(grads[2:], 2)
    multiply(3)
    step(outs[:2], 1)
    step(grads, 3)
    finish_out(0)
    finish_out(1)
    step(outs[2:], 1)
    for i in range(X):
        grads[i].step(4)
        queries(i)
    finish_out(2)
    finish_out(3)
    for copy in table_in + gq_sent:
        copy.wait_recv()
    for i in (1, 2, 3):
        copy = pltpu.make_async_remote_copy(
            src_ref=done.at[0],
            dst_ref=out.at[:, columns(xs[i], span)],
            send_sem=out_send.at[i],
            recv_sem=out_recv.at[i],
            device_id=device(xs[i], z, y, c),
            device_id_type=pl.DeviceIdType.MESH,
        )
        copy.wait_recv()
        copy.wait_send()
    for copy in kept:
        copy.wait()
    copies.finish()


def collect(ctx, gq, dkey, dvalue, wf):
    head_cols, span = wf.shape
    rows = dkey.shape[1]
    slots = TOK // (Y * C)
    return pl.pallas_call(
        collect_kernel,
        out_shape=(
            jax.ShapeDtypeStruct((slots, X * span), BF),
            jax.ShapeDtypeStruct((TOK, head_cols), BF),
            jax.ShapeDtypeStruct((rows, head_cols), BF),
            jax.ShapeDtypeStruct((rows, head_cols), BF),
        ),
        in_specs=[VMEM] * 5,
        out_specs=[VMEM] * 4,
        scratch_shapes=[
            pltpu.VMEM((2 * X, 8, TOK, HD), BF),
            pltpu.VMEM((X, Y, C, slots, head_cols), BF),
            pltpu.VMEM((X, Y, slots, head_cols), BF),
            pltpu.VMEM((head_cols, span), BF),
            pltpu.VMEM((X, Y, slots, span), BF),
            pltpu.VMEM((X, 4, slots, span), BF),
            pltpu.VMEM((X, slots, span), BF),
            pltpu.VMEM((X, TOK, HD), BF),
            pltpu.SemaphoreType.DMA((120,)),
            pltpu.SemaphoreType.DMA((120,)),
            pltpu.SemaphoreType.DMA((4,)),
            pltpu.SemaphoreType.DMA((4,)),
            pltpu.SemaphoreType.DMA((8,)),
        ],
        compiler_params=pltpu.CompilerParams(
            collective_id=2, has_side_effects=True, vmem_limit_bytes=LIMIT
        ),
        name="collect",
    )(ctx, gq, dkey, dvalue, wf)


def shards(queries, keys, values, out_weight, grad_out, neighbour_owner, neighbour_local):
    ids = jnp.stack([neighbour_owner, neighbour_local], axis=-1).reshape(1, -1)
    ids = jnp.pad(ids, ((0, 0), (0, 128 - ids.shape[1])))
    ids, qall, ktab, vtab, wf, upall = spread(ids, queries, keys, values, out_weight, grad_out)
    qall, upall = (a.reshape(Z * X * TOK, HD) for a in (qall, upall))
    ktab, vtab = (a.reshape(X * keys.shape[0], HD) for a in (ktab, vtab))
    sums = totals(stats_of_uses(ids, qall, upall, ktab, vtab))
    ctx, gq, dkey, dvalue = grads_of_uses(ids, qall, upall, ktab, vtab, sums)
    ctx, gq = (a.reshape(Z, X, TOK, HD) for a in (ctx, gq))
    dkey, dvalue = (a.reshape((X,) + keys.shape[:1] + (HD,)) for a in (dkey, dvalue))
    out, grad_queries, grad_keys, grad_values = collect(ctx, gq, dkey, dvalue, wf)
    return out, grad_queries, grad_keys.astype(F32), grad_values.astype(F32)


def solution(mesh):
    return jax.shard_map(
        shards,
        mesh=mesh,
        in_specs=(
            P("dp", "tensor"),
            P("dp", "tensor"),
            P("dp", "tensor"),
            P("tensor", "dp"),
            P(("dp", "tensor"), None),
            P("dp", None),
            P("dp", None),
        ),
        out_specs=(
            P(("dp", "tensor"), None),
            P("dp", "tensor"),
            P("dp", "tensor"),
            P("dp", "tensor"),
        ),
        check_vma=False,
    )
```

```python
import functools

import jax
import jax.numpy as jnp
from jax import lax
from jax.experimental import pallas as pl
from jax.experimental.pallas import tpu as pltpu
from jax.sharding import PartitionSpec as P

X, Z, Y, C = 4, 8, 4, 2
HD = 128
GROUP = 64
NLEN = 128
NB_DEV = 8
TOK = 256
SCALE = HD**-0.5
LOW = -1e30
BF = jnp.bfloat16
F32 = jnp.float32
VMEM = pl.BlockSpec(memory_space=pltpu.VMEM)
SMEM = pl.BlockSpec(memory_space=pltpu.SMEM)
HBM = pl.BlockSpec(memory_space=pltpu.HBM)
LIMIT = 28 * 1024 * 1024


def place():
    dp, t = lax.axis_index("dp"), lax.axis_index("tensor")
    return lax.div(dp, Z), lax.rem(dp, Z), lax.div(t, C), lax.rem(t, C)


def device(x, z, y, c):
    return (x * Z + z, y * C + c)


def step_from(i, by, n):
    return lax.rem(i + (by + n), n)


def columns(i, width):
    return pl.ds(pl.multiple_of(i * width, width), width)


def enter(peers):
    barrier = pltpu.get_barrier_semaphore()
    for peer in peers:
        pl.semaphore_signal(barrier, inc=1, device_id=peer, device_id_type=pl.DeviceIdType.MESH)
    pl.semaphore_wait(barrier, len(peers))


class Copies:
    def __init__(self, send, recv):
        self.send, self.recv, self.count, self.started = send, recv, 0, []

    def take(self, n=1):
        first = self.count
        self.count += n
        return first

    def make(self, sem, src, dst, to):
        return pltpu.make_async_remote_copy(
            src_ref=src,
            dst_ref=dst,
            send_sem=self.send.at[sem],
            recv_sem=self.recv.at[sem],
            device_id=to,
            device_id_type=pl.DeviceIdType.MESH,
        )

    def start(self, src, dst, to):
        copy = self.make(self.take(), src, dst, to)
        copy.start()
        self.started.append(copy)
        return copy

    def finish(self):
        for copy in self.started:
            copy.wait_send()


class Gather:
    def __init__(self, copies, first, view, hops, ring, arrived=None):
        self.copies, self.first, self.view, self.hops = copies, first, view, hops
        self.place, self.size, self.sides = ring
        self.arrived = arrived
        self.sent = [[], []]

    def step(self, s):
        for way, sign in ((0, 1), (1, -1)):
            block = step_from(self.place, -sign * s, self.size)
            if 0 < s <= self.hops[way]:
                self.sent[way][s - 1].wait_recv()
            if s < self.hops[way]:
                src = self.first if s == 0 else self.view(block)
                self.sent[way].append(self.copies.start(src, self.view(block), self.sides[way]))
            if self.arrived is not None and 0 < s <= self.hops[way]:
                self.arrived(block)


class Scatter:
    def __init__(self, copies, first, value, held, hops, ring):
        self.copies, self.first, self.value, self.held, self.hops = copies, first, value, held, hops
        self.place, self.size, self.sides = ring
        self.sent = [[], []]

    def step(self, s):
        for way, sign in ((0, 1), (1, -1)):
            n = self.hops[way]
            if 0 < s <= n:
                self.sent[way][s - 1].wait_recv()
            if s < n:
                goal = step_from(self.place, sign * (n - s), self.size)
                if s == 0:
                    src = self.first(way, goal)
                else:
                    src = self.held(way, s - 1)
                    src[...] = (src[...].astype(F32) + self.value(goal)).astype(BF)
                self.sent[way].append(self.copies.start(src, self.held(way, s), self.sides[way]))

    def total(self):
        total = self.value(self.place)
        for way in (0, 1):
            total += self.held(way, self.hops[way] - 1)[...].astype(F32)
        return total


def rings(x, z, y, c):
    along_z = z, Z, tuple(device(x, step_from(z, i, Z), y, c) for i in (1, -1))
    along_y = y, Y, tuple(device(x, z, step_from(y, i, Y), c) for i in (1, -1))
    return along_z, along_y


HOPS = ((4, 3), (3, 4))
HOPS_Y = ((2, 1), (1, 2))


def start_local(local, kept, src, dst):
    copy = pltpu.make_async_copy(src, dst, local.at[len(kept)])
    copy.start()
    kept.append(copy)


def step_all(pieces, s):
    for one in pieces:
        one.step(s)


def weight_piece(copies, first, wf, width, i, along_z):
    depth = wf.shape[0] // 2
    rows = pl.ds(i * depth, depth)
    return Gather(
        copies, first, lambda b: wf.at[rows, columns(b, width)], HOPS[i % 2], along_z
    )


def spread_kernel(
    ids_ref, q_ref, k_ref, v_ref, w_ref, g_ref,
    idall, qall, ktab, vtab, wf, gfull,
    send, recv, local,
):
    x, z, y, c = place()
    t = y * C + c
    width = w_ref.shape[1]
    depth = w_ref.shape[0] // 4
    span = Z * width
    xs = [step_from(x, i, X) for i in range(X)]
    along_z, along_y = rings(x, z, y, c)
    sibling = device(x, z, y, 1 - c)
    enter(
        [device(xs[i], z, y, c) for i in (1, 2, 3)]
        + list(along_z[2])
        + list(along_y[2])
        + [sibling]
    )
    copies = Copies(send, recv)
    kept = []

    def keep(src, dst):
        start_local(local, kept, src, dst)

    table_in, q_in, g_core = [], [], {}

    def piece(ref, i):
        return Gather(copies, ref.at[z, i], lambda b: ref.at[b, i], HOPS[i % 2], along_z)

    weights = [
        weight_piece(copies, w_ref.at[pl.ds(i * depth, depth)], wf, width, i, along_z)
        for i in range(2)
    ]
    asked = [piece(qall, i) for i in range(X)]
    asked.append(Gather(copies, idall.at[z], lambda b: idall.at[b], HOPS[0], along_z))

    def send_table(src, dst):
        for i in (1, 3, 2):
            to = device(xs[i], z, y, c)
            table_in.append(copies.start(src.at[:, columns(xs[i], HD)], dst.at[x], to))

    def hand_over(i, block):
        block = gfull.at[i, block * C + c]
        g_core[i].append(copies.start(block, block, sibling))

    def rows_piece(i):
        return Gather(
            copies,
            gfull.at[i, t],
            lambda b: gfull.at[i, b * C + c],
            HOPS_Y[i % 2],
            along_y,
            lambda b: hand_over(i, b),
        )

    rows = [rows_piece(i) for i in range(X)]

    def send_rows(i):
        rows[i].step(0)
        g_core[i] = []
        hand_over(i, y)

    for i in (1, 3, 2):
        to = device(xs[i], z, y, c)
        q_in.append(copies.start(q_ref.at[:, columns(xs[i], HD)], qall.at[z, x], to))
        q_in.append(copies.start(ids_ref, idall.at[z, x], to))
    step_all(weights, 0)
    g_in = [
        copies.start(g_ref.at[:, columns(xs[i], span)], gfull.at[x, t], device(xs[i], z, y, c))
        for i in (1, 3, 2)
    ]
    keep(q_ref.at[:, columns(x, HD)], qall.at[z, x])
    keep(ids_ref, idall.at[z, x])
    keep(g_ref.at[:, columns(x, span)], gfull.at[x, t])
    keep(w_ref.at[pl.ds(0, 2 * depth)], wf.at[:, columns(z, width)])
    keep(k_ref.at[:, columns(x, HD)], ktab.at[x])
    keep(v_ref.at[:, columns(x, HD)], vtab.at[x])
    step_all(weights, 1)
    for copy in q_in:
        copy.wait_recv()
    for copy in kept[:2]:
        copy.wait()
    step_all(asked, 0)
    send_table(k_ref, ktab)
    send_table(v_ref, vtab)
    step_all(weights, 2)
    kept[2].wait()
    for copy in g_in:
        copy.wait_recv()
    send_rows(0)
    send_rows(1)
    step_all(asked, 1)
    step_all(weights, 3)
    step_all(rows[:2], 1)
    send_rows(2)
    send_rows(3)
    step_all(asked, 2)
    step_all(rows[:2], 2)
    step_all(weights, 4)
    step_all(asked, 3)
    step_all(rows[2:], 1)
    step_all(rows[2:], 2)
    step_all(asked, 4)
    for i in range(X):
        for copy in g_core[i]:
            copy.wait_recv()
    for copy in table_in:
        copy.wait_recv()
    for copy in kept[3:]:
        copy.wait()
    copies.finish()


def spread(ids, queries, keys, values, out_weight, grad_out):
    depth, width = out_weight.shape
    rows = keys.shape[0]
    return pl.pallas_call(
        spread_kernel,
        out_shape=(
            jax.ShapeDtypeStruct((Z, X) + ids.shape, jnp.int32),
            jax.ShapeDtypeStruct((Z, X, TOK, HD), BF),
            jax.ShapeDtypeStruct((X, rows, HD), BF),
            jax.ShapeDtypeStruct((X, rows, HD), BF),
            jax.ShapeDtypeStruct((depth // 2, Z * width), BF),
            jax.ShapeDtypeStruct((X, Y * C, grad_out.shape[0], Z * width), BF),
        ),
        in_specs=[VMEM] + [HBM] * 5,
        out_specs=[VMEM] * 6,
        scratch_shapes=[
            pltpu.SemaphoreType.DMA((96,)),
            pltpu.SemaphoreType.DMA((96,)),
            pltpu.SemaphoreType.DMA((8,)),
        ],
        compiler_params=pltpu.CompilerParams(
            collective_id=0, has_side_effects=True, vmem_limit_bytes=LIMIT
        ),
        name="spread",
    )(ids, queries, keys, values, out_weight, grad_out)


def list_uses(ids, groups, names):
    z = lax.rem(lax.axis_index("dp"), Z)

    def add(i, n):
        dp_z, dp_x = lax.shift_right_logical(i, 5), lax.shift_right_logical(i, 3) & 3
        owner, name = (ids[dp_z, dp_x, 0, 2 * (i & 7) + j] for j in (0, 1))
        groups[n] = lax.shift_right_logical(i, 1)
        names[n] = lax.shift_right_logical(owner, 3) * NB_DEV + name
        return n + ((owner & 7) == z).astype(jnp.int32)

    n = lax.fori_loop(0, X * Z * 8, add, jnp.int32(0), unroll=8)
    last = jnp.maximum(n - 1, 0)
    groups[n] = groups[last]
    names[n] = names[last]
    return n


def pair_rows(ref, a, b, size):
    return [ref[pl.ds(pl.multiple_of(i * size, size), size), :] for i in (a, b)]


def pair_scores(first, second, both, left):
    product = lax.dot_general(
        jnp.concatenate([first, second], axis=0),
        both,
        (((1,), (1,)), ((), ())),
        preferred_element_type=F32,
    )
    return jnp.where(left, product[:NLEN], product[NLEN:])


def merge(one, two):
    peak = jnp.maximum(one[0], two[0])
    return peak, jnp.exp(one[0] - peak) * one[1] + jnp.exp(two[0] - peak) * two[1]


def clear(ref, rows=512):
    @pl.loop(0, ref.shape[0] // rows)
    def _(i):
        ref[pl.ds(pl.multiple_of(i * rows, rows), rows), :] = jnp.zeros((rows, HD), ref.dtype)


def add_rows(ref, i, size, value):
    at = pl.ds(pl.multiple_of(i * size, size), size)
    ref[at, :] = (ref[at, :].astype(F32) + value).astype(ref.dtype)


def attend_kernel(ids, qall, ktab, vtab, logs, ctx, groups, names, stats):
    n = list_uses(ids, groups, names)
    stats[0] = jnp.full(stats.shape[1:], LOW, F32)
    stats[1] = jnp.zeros(stats.shape[1:], F32)
    clear(ctx)
    left = lax.broadcasted_iota(jnp.int32, (1, 2 * GROUP), 1) < GROUP

    def scores_of(ga, gb, na, nb):
        qq = jnp.concatenate(pair_rows(qall, ga, gb, GROUP), axis=0)
        return pair_scores(*pair_rows(ktab, na, nb, NLEN), qq, left) * SCALE

    def measure(p, carry):
        a, b = 2 * p, 2 * p + 1
        ga, gb, na, nb = groups[a], groups[b], names[a], names[b]
        scores = scores_of(ga, gb, na, nb)
        peak = jnp.max(scores, axis=0, keepdims=True)
        total = jnp.sum(jnp.exp(scores - peak), axis=0, keepdims=True)
        real = left | (b < n)
        new = jnp.where(real, peak, LOW), jnp.where(real, total, 0.0)
        for g, mine in ((ga, left), (gb, jnp.logical_not(left))):
            old = tuple(stats[i, pl.ds(g, 1), :] for i in range(2))
            merged = merge(old, new)
            for i in range(2):
                stats[i, pl.ds(g, 1), :] = jnp.where(mine, merged[i], old[i])
        return carry

    def weigh(p, carry):
        a, b = 2 * p, 2 * p + 1
        ga, gb, na, nb = groups[a], groups[b], names[a], names[b]
        scores = scores_of(ga, gb, na, nb)
        log_total = jnp.where(left, logs[pl.ds(ga, 1), :], logs[pl.ds(gb, 1), :])
        prob = jnp.where(left | (b < n), jnp.exp(scores - log_total), 0.0)
        values = pair_rows(vtab, na, nb, NLEN)
        context = jnp.dot(
            prob.T.astype(BF), jnp.concatenate(values, axis=1), preferred_element_type=F32
        )
        add_rows(ctx, ga, GROUP, context[:GROUP, :HD])
        add_rows(ctx, gb, GROUP, context[GROUP:, HD:])
        return carry

    lax.fori_loop(0, (n + 1) // 2, measure, 0)
    state = stats[0], stats[1]
    peak, total = merge(state, tuple(pltpu.roll(v, GROUP, 1) for v in state))
    logs[...] = jnp.where(total > 0.0, peak + jnp.log(jnp.maximum(total, 1e-30)), LOW)
    lax.fori_loop(0, (n + 1) // 2, weigh, 0)


def attend(ids, qall, ktab, vtab):
    return pl.pallas_call(
        attend_kernel,
        out_shape=(
            jax.ShapeDtypeStruct((16 * Z, 2 * GROUP), F32),
            jax.ShapeDtypeStruct(qall.shape, BF),
        ),
        in_specs=[SMEM] + [VMEM] * 3,
        out_specs=[VMEM] * 2,
        scratch_shapes=[
            pltpu.SMEM((264,), jnp.int32),
            pltpu.SMEM((264,), jnp.int32),
            pltpu.VMEM((2, 16 * Z, 2 * GROUP), F32),
        ],
        compiler_params=pltpu.CompilerParams(vmem_limit_bytes=LIMIT),
        name="attend",
    )(ids, qall, ktab, vtab)


def project_kernel(
    logs, ctx, wa, w_ref, gfull,
    sums, upall, out,
    wb, wo, logs_in, upp, upr, staged, held, ctx4, ctx_other, part, y_held, done,
    send, recv, out_send, out_recv, local,
):
    x, z, y, c = place()
    half, span = wa.shape
    width = w_ref.shape[1]
    depth = half // 2
    head_cols = 2 * half
    slots = TOK // (Y * C)
    xs = [step_from(x, i, X) for i in range(X)]
    zs = [step_from(z, i, Z) for i in range(Z)]
    order = (4, 3, 5, 2, 6, 1, 7)
    along_z, along_y = rings(x, z, y, c)
    sibling = device(x, z, y, 1 - c)
    enter(
        [device(xs[i], z, y, c) for i in (1, 2, 3)]
        + [device(x, zs[i], y, c) for i in order]
        + list(along_y[2])
        + [sibling]
    )
    copies = Copies(send, recv)
    kept = []
    left = lax.broadcasted_iota(jnp.int32, (1, 2 * GROUP), 1) < GROUP
    own = pl.ds(pl.multiple_of(z * 16, 16), 16)
    up_in, ctx_in, core_in = {}, {}, {}

    def tell(ref):
        return [copies.start(ref, ref, device(x, zs[i], y, c)) for i in order]

    def send_logs():
        return [
            copies.start(logs.at[columns(zs[i], 16)], logs_in.at[i - 1], device(x, zs[i], y, c))
            for i in order
        ]

    def merge_logs():
        parts = [logs[own, :]] + [logs_in[i] for i in range(Z - 1)]
        peak = functools.reduce(jnp.maximum, parts)
        total = sum(jnp.exp(v - peak) for v in parts)
        sums[0, own, :] = peak + jnp.log(total)

    def multiply_rows(i, w, at):
        upp[i, :, at] = lax.dot_general(
            gfull[i].reshape(TOK, span),
            w[...],
            (((1,), (1,)), ((), ())),
            preferred_element_type=F32,
        ).astype(BF)

    def send_up(i):
        up_in[i] = [
            copies.start(
                upp.at[i, :, columns(xs[j], HD)], upr.at[i, j - 1], device(xs[j], z, y, c)
            )
            for j in (1, 3, 2)
        ]

    def total_up(i):
        for copy in up_in[i]:
            copy.wait_recv()
        value = upp[i, :, columns(x, HD)].astype(F32)
        for j in range(3):
            value += upr[i, j].astype(F32)
        upall[z, i] = value.astype(BF)
        upstream[i].step(0)

    def scaled(b, i):
        rows = []
        for j in range(2):
            at = [pl.ds(b * 16 + i * 4 + 2 * j + k, 1) for k in (0, 1)]
            factor = [jnp.exp(logs[r, :] - sums[0, r, :]) for r in at]
            factor = jnp.broadcast_to(jnp.where(left, *factor), (2 * GROUP, HD))
            rows.append(factor.T)
        return jnp.concatenate(rows, axis=0) * ctx[b, i].astype(F32)

    def context_piece(i):
        def first(way, b):
            staged[i, way] = scaled(b, i).astype(BF)
            return staged.at[i, way]

        return Scatter(
            copies,
            first,
            lambda b: scaled(b, i),
            lambda way, s: held.at[i, 4 * way + s],
            HOPS[i % 2],
            along_z,
        )

    def out_piece(i):
        return Scatter(
            copies,
            lambda way, b: part.at[i, b],
            lambda b: part[i, b].astype(F32),
            lambda way, s: y_held.at[i, 2 * way + s],
            HOPS_Y[i % 2],
            along_y,
        )

    weights = [
        weight_piece(copies, w_ref.at[pl.ds(half + i * depth, depth)], wb, width, i, along_z)
        for i in range(2)
    ]
    contexts = [context_piece(i) for i in range(X)]
    outs = [out_piece(i) for i in range(X)]
    upstream = [
        Gather(copies, upall.at[z, i], lambda b, i=i: upall.at[b, i], HOPS[i % 2], along_z)
        for i in range(X)
    ]

    def share(i):
        context = contexts[i].total().astype(BF)
        mine = ctx4.at[i, :, :, :, columns(x, HD)]
        mine[...] = context.reshape(Y, C, slots, HD)
        ctx_in[i] = [copies.start(mine, mine, device(xs[j], z, y, c)) for j in (1, 3, 2)]

    def inner(i):
        context = ctx4[i, :, :, :, columns(x, HD)].reshape(TOK, HD)
        product = upall[z, i].astype(F32) * context.astype(F32)
        for j in range(2):
            rows = product[j * 2 * GROUP : (j + 1) * 2 * GROUP]
            row = jnp.sum(rows.T, axis=0, keepdims=True)
            turned = pltpu.roll(row, GROUP, 1)
            at = z * 16 + i * 4 + 2 * j
            sums[1, pl.ds(at, 1), :] = jnp.where(left, row, turned)
            sums[1, pl.ds(at + 1, 1), :] = jnp.where(left, turned, row)

    def swap(i):
        for copy in ctx_in[i]:
            copy.wait_recv()
        core_in[i] = copies.start(ctx4.at[i, :, 1 - c], ctx_other.at[i], sibling)

    def multiply(i):
        core_in[i].wait_recv()
        terms = (
            (ctx4[i, :, c].reshape(Y * slots, head_cols), wa, wb),
            (ctx_other[i].reshape(Y * slots, head_cols), wo.at[0], wo.at[1]),
        )
        for j in range(2):
            cols = pl.ds(j * (span // 2), span // 2)
            product = 0.0
            for rows, first, second in terms:
                product += jnp.dot(rows[:, :half], first[:, cols], preferred_element_type=F32)
                product += jnp.dot(rows[:, half:], second[:, cols], preferred_element_type=F32)
            part[i, :, :, cols] = product.astype(BF).reshape(Y, slots, span // 2)
        outs[i].step(0)

    def finish_out(i):
        outs[i].step(2)
        done[i] = outs[i].total().astype(BF)
        goal = out.at[:, columns(x, span)]

        @pl.when(x == i)
        def _():
            copy = pltpu.make_async_copy(done.at[i], goal, local.at[7])
            copy.start()
            copy.wait()

        @pl.when(x != i)
        def _():
            sem = step_from(i - x, 0, X)
            pltpu.make_async_remote_copy(
                src_ref=done.at[i],
                dst_ref=goal,
                send_sem=out_send.at[sem],
                recv_sem=out_recv.at[sem],
                device_id=device(i, z, y, c),
                device_id_type=pl.DeviceIdType.MESH,
            ).start()

    logs_sent = send_logs()
    step_all(weights, 0)
    wa_in = copies.start(wa, wo.at[0], sibling)
    start_local(local, kept, w_ref.at[pl.ds(half, half)], wb.at[:, columns(z, width)])
    multiply_rows(0, wa, pl.ds(0, half))
    multiply_rows(1, wa, pl.ds(0, half))
    step_all(weights, 1)
    for copy in logs_sent:
        copy.wait_recv()
    merge_logs()
    logs_back = tell(sums.at[0, own])
    multiply_rows(2, wa, pl.ds(0, half))
    multiply_rows(3, wa, pl.ds(0, half))
    step_all(weights, 2)
    step_all(weights, 3)
    for copy in logs_back:
        copy.wait_recv()
    step_all(contexts, 0)
    step_all(weights, 4)
    kept[0].wait()
    wb_in = copies.start(wb, wo.at[1], sibling)
    multiply_rows(0, wb, pl.ds(half, half))
    send_up(0)
    step_all(contexts[:2], 1)
    multiply_rows(1, wb, pl.ds(half, half))
    send_up(1)
    step_all(contexts[2:], 1)
    multiply_rows(2, wb, pl.ds(half, half))
    send_up(2)
    step_all(contexts[:2], 2)
    multiply_rows(3, wb, pl.ds(half, half))
    send_up(3)
    step_all(contexts[2:], 2)
    step_all(contexts, 3)
    total_up(0)
    total_up(1)
    for i in range(X):
        contexts[i].step(4)
        share(i)
    total_up(2)
    total_up(3)
    wa_in.wait_recv()
    wb_in.wait_recv()
    swap(0)
    step_all(upstream, 1)
    multiply(0)
    swap(1)
    for i in range(X):
        inner(i)
    inner_back = tell(sums.at[1, own])
    multiply(1)
    swap(2)
    step_all(upstream, 2)
    multiply(2)
    swap(3)
    multiply(3)
    step_all(outs[:2], 1)
    step_all(upstream, 3)
    finish_out(0)
    finish_out(1)
    step_all(outs[2:], 1)
    step_all(upstream, 4)
    finish_out(2)
    finish_out(3)
    for copy in inner_back:
        copy.wait_recv()
    for i in (1, 2, 3):
        copy = pltpu.make_async_remote_copy(
            src_ref=done.at[0],
            dst_ref=out.at[:, columns(xs[i], span)],
            send_sem=out_send.at[i],
            recv_sem=out_recv.at[i],
            device_id=device(xs[i], z, y, c),
            device_id_type=pl.DeviceIdType.MESH,
        )
        copy.wait_recv()
        copy.wait_send()
    copies.finish()


def project(logs, ctx, wa, out_weight, gfull):
    half, span = wa.shape
    slots = TOK // (Y * C)
    return pl.pallas_call(
        project_kernel,
        out_shape=(
            jax.ShapeDtypeStruct((2,) + logs.shape, F32),
            jax.ShapeDtypeStruct(ctx.shape, BF),
            jax.ShapeDtypeStruct((slots, X * span), BF),
        ),
        in_specs=[VMEM] * 3 + [HBM] + [VMEM],
        out_specs=[VMEM] * 3,
        scratch_shapes=[
            pltpu.VMEM((half, span), BF),
            pltpu.VMEM((2, half, span), BF),
            pltpu.VMEM((Z - 1, 16, 2 * GROUP), F32),
            pltpu.VMEM((X, TOK, 2 * half), BF),
            pltpu.VMEM((X, X - 1, TOK, HD), BF),
            pltpu.VMEM((X, 2, TOK, HD), BF),
            pltpu.VMEM((X, 8, TOK, HD), BF),
            pltpu.VMEM((X, Y, C, slots, 2 * half), BF),
            pltpu.VMEM((X, Y, slots, 2 * half), BF),
            pltpu.VMEM((X, Y, slots, span), BF),
            pltpu.VMEM((X, 4, slots, span), BF),
            pltpu.VMEM((X, slots, span), BF),
            pltpu.SemaphoreType.DMA((144,)),
            pltpu.SemaphoreType.DMA((144,)),
            pltpu.SemaphoreType.DMA((4,)),
            pltpu.SemaphoreType.DMA((4,)),
            pltpu.SemaphoreType.DMA((8,)),
        ],
        compiler_params=pltpu.CompilerParams(
            collective_id=1, has_side_effects=True, vmem_limit_bytes=LIMIT
        ),
        name="project",
    )(logs, ctx, wa, out_weight, gfull)


def grads_kernel(
    ids, qall, upall, ktab, vtab, sums, gq, dkey, dvalue, groups, names, dk, dv
):
    n = list_uses(ids, groups, names)
    for ref in (gq, dk, dv):
        clear(ref)

    left = lax.broadcasted_iota(jnp.int32, (1, 2 * GROUP), 1) < GROUP
    zero = jnp.zeros((), BF)

    def dot(a, b):
        return jnp.dot(a, b, preferred_element_type=F32)

    def pair(p, carry):
        a, b = 2 * p, 2 * p + 1
        ga, gb, na, nb = groups[a], groups[b], names[a], names[b]
        qq = jnp.concatenate(pair_rows(qall, ga, gb, GROUP), axis=0)
        uu = jnp.concatenate(pair_rows(upall, ga, gb, GROUP), axis=0)
        keys = pair_rows(ktab, na, nb, NLEN)
        values = pair_rows(vtab, na, nb, NLEN)
        scores = pair_scores(*keys, qq, left) * SCALE
        grad_probs = pair_scores(*values, uu, left)
        log_total = jnp.where(left, sums[0, pl.ds(ga, 1), :], sums[0, pl.ds(gb, 1), :])
        inner = jnp.where(left, sums[1, pl.ds(ga, 1), :], sums[1, pl.ds(gb, 1), :])
        real = left | (b < n)
        prob = jnp.where(real, jnp.exp(scores - log_total), 0.0)
        grad_scores = prob * (grad_probs - inner)
        grad_t = grad_scores.T.astype(BF)
        prob, grad_scores = prob.astype(BF), grad_scores.astype(BF)

        def halves(v):
            return jnp.concatenate([jnp.where(left, v, zero), jnp.where(left, zero, v)], axis=0)

        grad_q = dot(grad_t, jnp.concatenate(keys, axis=1)) * SCALE
        grad_v = dot(halves(prob), uu)
        grad_k = dot(halves(grad_scores), qq) * SCALE
        add_rows(gq, ga, GROUP, grad_q[:GROUP, :HD])
        add_rows(gq, gb, GROUP, grad_q[GROUP:, HD:])
        add_rows(dv, na, NLEN, grad_v[:NLEN])
        add_rows(dv, nb, NLEN, grad_v[NLEN:])
        add_rows(dk, na, NLEN, grad_k[:NLEN])
        add_rows(dk, nb, NLEN, grad_k[NLEN:])
        return carry

    lax.fori_loop(0, (n + 1) // 2, pair, 0)
    for src, dst in ((dk, dkey), (dv, dvalue)):
        rows = 512

        @pl.loop(0, src.shape[0] // rows)
        def _(i, src=src, dst=dst):
            at = pl.ds(pl.multiple_of(i * rows, rows), rows)
            dst[at, :] = src[at, :].astype(BF)


def grads_of_uses(ids, qall, upall, ktab, vtab, sums):
    tokens, rows = qall.shape[0], ktab.shape[0]
    return pl.pallas_call(
        grads_kernel,
        out_shape=(
            jax.ShapeDtypeStruct((tokens, HD), BF),
            jax.ShapeDtypeStruct((rows, HD), BF),
            jax.ShapeDtypeStruct((rows, HD), BF),
        ),
        in_specs=[SMEM] + [VMEM] * 5,
        out_specs=[VMEM] * 3,
        scratch_shapes=[
            pltpu.SMEM((264,), jnp.int32),
            pltpu.SMEM((264,), jnp.int32),
            pltpu.VMEM((rows, HD), F32),
            pltpu.VMEM((rows, HD), F32),
        ],
        compiler_params=pltpu.CompilerParams(vmem_limit_bytes=LIMIT),
        name="grads",
    )(ids, qall, upall, ktab, vtab, sums)


def collect_kernel(
    gq, dkey, dvalue, gq_out, dk_out, dv_out, held, gq_done, send, recv, local
):
    x, z, y, c = place()
    xs = [step_from(x, i, X) for i in range(X)]
    along_z, _ = rings(x, z, y, c)
    enter([device(xs[i], z, y, c) for i in (1, 2, 3)] + list(along_z[2]))
    copies = Copies(send, recv)
    kept, table_in, gq_sent = [], [], []

    def piece(i):
        return Scatter(
            copies,
            lambda way, b: gq.at[b, xs[i]],
            lambda b: gq[b, xs[i]].astype(F32),
            lambda way, s: held.at[i, 4 * way + s],
            HOPS[i % 2],
            along_z,
        )

    grads = [piece(i) for i in range(X)]
    step_all(grads, 0)
    for src, dst in ((dkey, dk_out), (dvalue, dv_out)):
        goal = dst.at[:, columns(x, HD)]
        for i in (1, 3, 2):
            table_in.append(copies.start(src.at[xs[i]], goal, device(xs[i], z, y, c)))
        start_local(local, kept, src.at[x], goal)
    for s in (1, 2, 3):
        step_all(grads, s)
    for i in (1, 2, 3, 0):
        grads[i].step(4)
        gq_done[i] = grads[i].total().astype(BF)
        goal = gq_out.at[:, columns(x, HD)]
        if i == 0:
            start_local(local, kept, gq_done.at[i], goal)
        else:
            gq_sent.append(copies.start(gq_done.at[i], goal, device(xs[i], z, y, c)))
    for copy in table_in + gq_sent:
        copy.wait_recv()
    for copy in kept:
        copy.wait()
    copies.finish()


def collect(gq, dkey, dvalue):
    rows = dkey.shape[1]
    return pl.pallas_call(
        collect_kernel,
        out_shape=(
            jax.ShapeDtypeStruct((TOK, X * HD), BF),
            jax.ShapeDtypeStruct((rows, X * HD), BF),
            jax.ShapeDtypeStruct((rows, X * HD), BF),
        ),
        in_specs=[VMEM] * 3,
        out_specs=[VMEM] * 3,
        scratch_shapes=[
            pltpu.VMEM((X, 8, TOK, HD), BF),
            pltpu.VMEM((X, TOK, HD), BF),
            pltpu.SemaphoreType.DMA((40,)),
            pltpu.SemaphoreType.DMA((40,)),
            pltpu.SemaphoreType.DMA((8,)),
        ],
        compiler_params=pltpu.CompilerParams(
            collective_id=2, has_side_effects=True, vmem_limit_bytes=LIMIT
        ),
        name="collect",
    )(gq, dkey, dvalue)


def shards(queries, keys, values, out_weight, grad_out, neighbour_owner, neighbour_local):
    ids = jnp.stack([neighbour_owner, neighbour_local], axis=-1).reshape(1, -1)
    ids = jnp.pad(ids, ((0, 0), (0, 128 - ids.shape[1])))
    ids, qall, ktab, vtab, wa, gfull = spread(ids, queries, keys, values, out_weight, grad_out)
    qall = qall.reshape(Z * X * TOK, HD)
    ktab, vtab = (a.reshape(X * keys.shape[0], HD) for a in (ktab, vtab))
    logs, ctx = attend(ids, qall, ktab, vtab)
    sums, upall, out = project(logs, ctx.reshape(Z, X, TOK, HD), wa, out_weight, gfull)
    upall = upall.reshape(Z * X * TOK, HD)
    gq, dkey, dvalue = grads_of_uses(ids, qall, upall, ktab, vtab, sums)
    dkey, dvalue = (a.reshape((X,) + keys.shape[:1] + (HD,)) for a in (dkey, dvalue))
    grad_queries, grad_keys, grad_values = collect(gq.reshape(Z, X, TOK, HD), dkey, dvalue)
    return out, grad_queries, grad_keys.astype(F32), grad_values.astype(F32)


def solution(mesh):
    return jax.shard_map(
        shards,
        mesh=mesh,
        in_specs=(
            P("dp", "tensor"),
            P("dp", "tensor"),
            P("dp", "tensor"),
            P("tensor", "dp"),
            P(("dp", "tensor"), None),
            P("dp", None),
            P("dp", None),
        ),
        out_specs=(
            P(("dp", "tensor"), None),
            P("dp", "tensor"),
            P("dp", "tensor"),
            P("dp", "tensor"),
        ),
        check_vma=False,
    )
```

```python
import jax
import jax.numpy as jnp
from jax import lax
from jax.experimental import pallas as pl
from jax.experimental.pallas import tpu as pltpu
from jax.sharding import PartitionSpec as P

X, Z, Y, C = 4, 8, 4, 2
HD = 128
GROUP = 64
NLEN = 128
NB_DEV = 8
TOK = 256
SCALE = HD**-0.5
LOW = -1e30
BF = jnp.bfloat16
F32 = jnp.float32
VMEM = pl.BlockSpec(memory_space=pltpu.VMEM)
SMEM = pl.BlockSpec(memory_space=pltpu.SMEM)
HBM = pl.BlockSpec(memory_space=pltpu.HBM)
LIMIT = 28 * 1024 * 1024
PAIRS, GRAD_PAIRS = 8, 4


def place():
    dp, t = lax.axis_index("dp"), lax.axis_index("tensor")
    return lax.div(dp, Z), lax.rem(dp, Z), lax.div(t, C), lax.rem(t, C)


def device(x, z, y, c):
    return (x * Z + z, y * C + c)


def step_from(i, by, n):
    return lax.rem(i + (by + n), n)


def columns(i, width):
    return pl.ds(pl.multiple_of(i * width, width), width)


def enter(peers):
    barrier = pltpu.get_barrier_semaphore()
    for peer in peers:
        pl.semaphore_signal(barrier, inc=1, device_id=peer, device_id_type=pl.DeviceIdType.MESH)
    pl.semaphore_wait(barrier, len(peers))


class Copies:
    def __init__(self, send, recv):
        self.send, self.recv, self.count, self.started = send, recv, 0, []

    def take(self, n=1):
        first = self.count
        self.count += n
        return first

    def make(self, sem, src, dst, to):
        return pltpu.make_async_remote_copy(
            src_ref=src,
            dst_ref=dst,
            send_sem=self.send.at[sem],
            recv_sem=self.recv.at[sem],
            device_id=to,
            device_id_type=pl.DeviceIdType.MESH,
        )

    def start(self, src, dst, to):
        copy = self.make(self.take(), src, dst, to)
        copy.start()
        self.started.append(copy)
        return copy

    def finish(self):
        for copy in self.started:
            copy.wait_send()


class Gather:
    def __init__(self, copies, first, view, hops, ring, arrived=None):
        self.copies, self.first, self.view, self.hops = copies, first, view, hops
        self.place, self.size, self.sides = ring
        self.arrived = arrived
        self.sent = [[], []]

    def step(self, s):
        for way, sign in ((0, 1), (1, -1)):
            block = step_from(self.place, -sign * s, self.size)
            if 0 < s <= self.hops[way]:
                self.sent[way][s - 1].wait_recv()
            if s < self.hops[way]:
                src = self.first if s == 0 else self.view(block)
                self.sent[way].append(self.copies.start(src, self.view(block), self.sides[way]))
            if self.arrived is not None and 0 < s <= self.hops[way]:
                self.arrived(block)


class Scatter:
    def __init__(self, copies, first, join, held, hops, ring):
        self.copies, self.first, self.join, self.held, self.hops = copies, first, join, held, hops
        self.place, self.size, self.sides = ring
        self.sent = [[], []]

    def step(self, s):
        for way, sign in ((0, 1), (1, -1)):
            n = self.hops[way]
            if 0 < s <= n:
                self.sent[way][s - 1].wait_recv()
            if s < n:
                goal = step_from(self.place, sign * (n - s), self.size)
                if s == 0:
                    src = self.first(way, goal)
                else:
                    src = self.held(way, s - 1)
                    self.join(src, goal)
                self.sent[way].append(self.copies.start(src, self.held(way, s), self.sides[way]))

    def arrived(self):
        return [self.held(way, self.hops[way] - 1) for way in (0, 1)]


class Sum(Scatter):
    def __init__(self, copies, part, held, hops, ring):
        def join(ref, goal):
            ref[...] = (ref[...].astype(F32) + part(goal)[...].astype(F32)).astype(BF)

        super().__init__(copies, lambda way, b: part(b), join, held, hops, ring)
        self.part = part

    def total(self):
        total = self.part(self.place)[...].astype(F32)
        for ref in self.arrived():
            total += ref[...].astype(F32)
        return total


def rings(x, z, y, c):
    along_z = z, Z, tuple(device(x, step_from(z, i, Z), y, c) for i in (1, -1))
    along_y = y, Y, tuple(device(x, z, step_from(y, i, Y), c) for i in (1, -1))
    return along_z, along_y


HOPS = ((4, 3), (3, 4))
HOPS_Y = ((2, 1), (1, 2))


def start_local(local, kept, src, dst):
    copy = pltpu.make_async_copy(src, dst, local.at[len(kept)])
    copy.start()
    kept.append(copy)


def step_all(pieces, s):
    for one in pieces:
        one.step(s)


def spread_kernel(
    ids_ref, q_ref, k_ref, v_ref, w_ref, g_ref,
    idall, qall, ktab, vtab, wf, gfull,
    send, recv, local,
):
    x, z, y, c = place()
    t = y * C + c
    width = w_ref.shape[1]
    depth = w_ref.shape[0] // 4
    span = Z * width
    xs = [step_from(x, i, X) for i in range(X)]
    along_z, along_y = rings(x, z, y, c)
    sibling = device(x, z, y, 1 - c)
    enter(
        [device(xs[i], z, y, c) for i in (1, 2, 3)]
        + list(along_z[2])
        + list(along_y[2])
        + [sibling]
    )
    copies = Copies(send, recv)
    kept = []

    def keep(src, dst):
        start_local(local, kept, src, dst)

    table_in, q_in, g_core = [], [], {}

    def piece(ref, i):
        return Gather(copies, ref.at[z, i], lambda b: ref.at[b, i], HOPS[i % 2], along_z)

    def weight_piece(i):
        rows = pl.ds(i * depth, depth)
        return Gather(
            copies, w_ref.at[rows], lambda b: wf.at[rows, columns(b, width)], HOPS[i % 2], along_z
        )

    weights = [weight_piece(i) for i in range(4)]
    asked = [piece(qall, i) for i in range(X)]
    asked.append(Gather(copies, idall.at[z], lambda b: idall.at[b], HOPS[0], along_z))

    def send_table(src, dst):
        for i in (1, 3, 2):
            to = device(xs[i], z, y, c)
            table_in.append(copies.start(src.at[:, columns(xs[i], HD)], dst.at[x], to))

    def hand_over(i, block):
        block = gfull.at[i, block * C + c]
        g_core[i].append(copies.start(block, block, sibling))

    def rows_piece(i):
        return Gather(
            copies,
            gfull.at[i, t],
            lambda b: gfull.at[i, b * C + c],
            HOPS_Y[i % 2],
            along_y,
            lambda b: hand_over(i, b),
        )

    rows = [rows_piece(i) for i in range(X)]

    def send_rows(i):
        rows[i].step(0)
        g_core[i] = []
        hand_over(i, y)

    for i in (1, 3, 2):
        to = device(xs[i], z, y, c)
        q_in.append(copies.start(q_ref.at[:, columns(xs[i], HD)], qall.at[z, x], to))
        q_in.append(copies.start(ids_ref, idall.at[z, x], to))
    step_all(weights, 0)
    g_in = [
        copies.start(g_ref.at[:, columns(xs[i], span)], gfull.at[x, t], device(xs[i], z, y, c))
        for i in (1, 3, 2)
    ]
    keep(q_ref.at[:, columns(x, HD)], qall.at[z, x])
    keep(ids_ref, idall.at[z, x])
    keep(g_ref.at[:, columns(x, span)], gfull.at[x, t])
    keep(w_ref, wf.at[:, columns(z, width)])
    keep(k_ref.at[:, columns(x, HD)], ktab.at[x])
    keep(v_ref.at[:, columns(x, HD)], vtab.at[x])
    for copy in q_in:
        copy.wait_recv()
    for copy in kept[:2]:
        copy.wait()
    step_all(asked, 0)
    send_table(k_ref, ktab)
    send_table(v_ref, vtab)
    step_all(weights, 1)
    kept[2].wait()
    for copy in g_in:
        copy.wait_recv()
    send_rows(0)
    send_rows(1)
    step_all(asked, 1)
    step_all(rows[:2], 1)
    send_rows(2)
    send_rows(3)
    step_all(weights, 2)
    step_all(rows[:2], 2)
    step_all(asked, 2)
    step_all(rows[2:], 1)
    step_all(weights, 3)
    step_all(rows[2:], 2)
    step_all(asked, 3)
    step_all(weights, 4)
    step_all(asked, 4)
    for i in range(X):
        for copy in g_core[i]:
            copy.wait_recv()
    for copy in table_in:
        copy.wait_recv()
    for copy in kept[3:]:
        copy.wait()
    copies.finish()


def spread(ids, queries, keys, values, out_weight, grad_out):
    depth, width = out_weight.shape
    rows = keys.shape[0]
    return pl.pallas_call(
        spread_kernel,
        out_shape=(
            jax.ShapeDtypeStruct((Z, X) + ids.shape, jnp.int32),
            jax.ShapeDtypeStruct((Z, X, TOK, HD), BF),
            jax.ShapeDtypeStruct((X, rows, HD), BF),
            jax.ShapeDtypeStruct((X, rows, HD), BF),
            jax.ShapeDtypeStruct((depth, Z * width), BF),
            jax.ShapeDtypeStruct((X, Y * C, grad_out.shape[0], Z * width), BF),
        ),
        in_specs=[VMEM] + [HBM] * 5,
        out_specs=[VMEM] * 6,
        scratch_shapes=[
            pltpu.SemaphoreType.DMA((112,)),
            pltpu.SemaphoreType.DMA((112,)),
            pltpu.SemaphoreType.DMA((8,)),
        ],
        compiler_params=pltpu.CompilerParams(
            collective_id=0, has_side_effects=True, vmem_limit_bytes=LIMIT
        ),
        name="spread",
    )(ids, queries, keys, values, out_weight, grad_out)


TAIL = 16
LISTED = 256 + 32


def list_uses(ids, uses):
    z = lax.rem(lax.axis_index("dp"), Z)

    def add(i, n):
        dp_z, dp_x = lax.shift_right_logical(i, 5), lax.shift_right_logical(i, 3) & 3
        owner, name = (ids[dp_z, dp_x, 0, 2 * (i & 7) + j] for j in (0, 1))
        uses[n] = lax.shift_right_logical(i, 1)
        uses[LISTED + n] = lax.shift_right_logical(owner, 3) * NB_DEV + name
        return n + ((owner & 7) == z).astype(jnp.int32)

    n = lax.fori_loop(0, X * Z * 8, add, jnp.int32(0), unroll=8)
    last = jnp.maximum(n - 1, 0)
    for i in range(2 * PAIRS - 1):
        uses[n + i] = uses[last]
        uses[LISTED + n + i] = uses[LISTED + last]
    uses[2 * LISTED] = n
    return n


def uses_at(uses, p, n, pairs):
    lane = lax.broadcasted_iota(jnp.int32, (1, 2 * GROUP), 1)
    out = []
    for i in range(pairs):
        a = 2 * (pairs * p + i)
        b = a + 1
        real = jnp.where(lane < GROUP, a, b) < n
        out.append((uses[a], uses[b], uses[LISTED + a], uses[LISTED + b], real))
    return out


def turns(n, pairs):
    return lax.div(n + (2 * pairs - 1), 2 * pairs)


def pair_rows(ref, a, b, size):
    return [ref[pl.ds(pl.multiple_of(i * size, size), size), :] for i in (a, b)]


def pair_scores(first, second, both, left):
    product = lax.dot_general(
        jnp.concatenate([first, second], axis=0),
        both,
        (((1,), (1,)), ((), ())),
        preferred_element_type=F32,
    )
    return jnp.where(left, product[:NLEN], product[NLEN:])


def merge(one, two):
    peak = jnp.maximum(one[0], two[0])
    return peak, jnp.exp(one[0] - peak) * one[1] + jnp.exp(two[0] - peak) * two[1]


def clear(ref, rows=512):
    @pl.loop(0, ref.shape[0] // rows)
    def _(i):
        ref[pl.ds(pl.multiple_of(i * rows, rows), rows), :] = jnp.zeros((rows, HD), ref.dtype)


def add_rows(ref, i, size, value):
    at = pl.ds(pl.multiple_of(i * size, size), size)
    ref[at, :] = (ref[at, :].astype(F32) + value).astype(ref.dtype)


def attend_kernel(ids, qall, ktab, vtab, logs, ctx, uses, stats):
    n = list_uses(ids, uses)
    stats[0] = jnp.full(stats.shape[1:], LOW, F32)
    stats[1] = jnp.zeros(stats.shape[1:], F32)
    clear(ctx)
    left = lax.broadcasted_iota(jnp.int32, (1, 2 * GROUP), 1) < GROUP

    def scores_of(ga, gb, na, nb):
        qq = jnp.concatenate(pair_rows(qall, ga, gb, GROUP), axis=0)
        return pair_scores(*pair_rows(ktab, na, nb, NLEN), qq, left) * SCALE

    def measure(p, carry):
        pairs = uses_at(uses, p, n, PAIRS)
        found = []
        for ga, gb, na, nb, real in pairs:
            scores = scores_of(ga, gb, na, nb)
            peak = jnp.max(scores, axis=0, keepdims=True)
            total = jnp.sum(jnp.exp(scores - peak), axis=0, keepdims=True)
            found.append((jnp.where(real, peak, LOW), jnp.where(real, total, 0.0)))
        for (ga, gb, *_), new in zip(pairs, found):
            for g, mine in ((ga, left), (gb, jnp.logical_not(left))):
                old = tuple(stats[i, pl.ds(g, 1), :] for i in range(2))
                merged = merge(old, new)
                for i in range(2):
                    stats[i, pl.ds(g, 1), :] = jnp.where(mine, merged[i], old[i])
        return carry

    def weigh(p, carry):
        pairs = uses_at(uses, p, n, PAIRS)
        found = []
        for ga, gb, na, nb, real in pairs:
            scores = scores_of(ga, gb, na, nb)
            log_total = jnp.where(left, logs[pl.ds(ga, 1), :], logs[pl.ds(gb, 1), :])
            prob = jnp.where(real, jnp.exp(scores - log_total), 0.0)
            values = pair_rows(vtab, na, nb, NLEN)
            found.append(
                jnp.dot(
                    prob.T.astype(BF),
                    jnp.concatenate(values, axis=1),
                    preferred_element_type=F32,
                )
            )
        for (ga, gb, *_), context in zip(pairs, found):
            add_rows(ctx, ga, GROUP, context[:GROUP, :HD])
            add_rows(ctx, gb, GROUP, context[GROUP:, HD:])
        return carry

    lax.fori_loop(0, turns(n, PAIRS), measure, 0)
    state = stats[0], stats[1]
    peak, total = merge(state, tuple(pltpu.roll(v, GROUP, 1) for v in state))
    logs[...] = jnp.where(total > 0.0, peak + jnp.log(jnp.maximum(total, 1e-30)), LOW)
    lax.fori_loop(0, turns(n, PAIRS), weigh, 0)


def attend(ids, qall, ktab, vtab):
    return pl.pallas_call(
        attend_kernel,
        out_shape=(
            jax.ShapeDtypeStruct((16 * Z, 2 * GROUP), F32),
            jax.ShapeDtypeStruct(qall.shape, BF),
            jax.ShapeDtypeStruct((2 * LISTED + 64,), jnp.int32),
        ),
        in_specs=[SMEM] + [VMEM] * 3,
        out_specs=[VMEM] * 2 + [SMEM],
        scratch_shapes=[
            pltpu.VMEM((2, 16 * Z, 2 * GROUP), F32),
        ],
        compiler_params=pltpu.CompilerParams(vmem_limit_bytes=LIMIT),
        name="attend",
    )(ids, qall, ktab, vtab)


def project_kernel(
    logs, ctx, wf, gfull,
    sums, upall, out,
    wf_other, upp, upr, staged, held, ctx4, ctx_other, part, y_held, done,
    send, recv, out_send, out_recv, local,
):
    x, z, y, c = place()
    head_cols, span = wf.shape
    slots = TOK // (Y * C)
    xs = [step_from(x, i, X) for i in range(X)]
    zs = [step_from(z, i, Z) for i in range(Z)]
    order = (4, 3, 5, 2, 6, 1, 7)
    along_z, along_y = rings(x, z, y, c)
    sibling = device(x, z, y, 1 - c)
    enter(
        [device(xs[i], z, y, c) for i in (1, 2, 3)]
        + [device(x, zs[i], y, c) for i in order]
        + list(along_y[2])
        + [sibling]
    )
    copies = Copies(send, recv)
    left = lax.broadcasted_iota(jnp.int32, (1, 2 * GROUP), 1) < GROUP
    own = pl.ds(pl.multiple_of(z * 16, 16), 16)
    up_in, ctx_in, core_in = {}, {}, {}

    def multiply_rows(i):
        upp[i] = lax.dot_general(
            gfull[i].reshape(TOK, span),
            wf[...],
            (((1,), (1,)), ((), ())),
            preferred_element_type=F32,
        ).astype(BF)
        up_in[i] = [
            copies.start(
                upp.at[i, :, columns(xs[j], HD)], upr.at[i, j - 1], device(xs[j], z, y, c)
            )
            for j in (1, 3, 2)
        ]

    def total_up(i):
        for copy in up_in[i]:
            copy.wait_recv()
        value = upp[i, :, columns(x, HD)].astype(F32)
        for j in range(3):
            value += upr[i, j].astype(F32)
        upall[z, i] = value.astype(BF)
        upstream[i].step(0)

    def mine(b, i):
        rows = [logs[pl.ds(b * 16 + i * 4 + j, 1), :] for j in range(4)]
        return ctx[b, i].astype(F32), [jnp.where(left, *rows[j : j + 2]) for j in (0, 2)]

    def write(ref, state):
        ref[:TOK] = state[0].astype(BF)
        rows = []
        for rest in state[1]:
            for _ in range(3):
                rows.append(rest.astype(BF).astype(F32))
                rest = rest - rows[-1]
        rows.append(jnp.zeros((TAIL - len(rows), HD), F32))
        ref[TOK:] = jnp.concatenate(rows, axis=0).astype(BF)

    def read(ref):
        rows = ref[TOK:].astype(F32)
        sums_of = [rows[3 * j : 3 * j + 1] + rows[3 * j + 1 : 3 * j + 2] for j in range(2)]
        return ref[:TOK].astype(F32), [v + rows[3 * j + 2 : 3 * j + 3] for j, v in enumerate(sums_of)]

    def joined(one, two):
        blocks, log_sums = [], []
        for j in range(2):
            peak = jnp.maximum(one[1][j], two[1][j])
            log_sum = peak + jnp.log(jnp.exp(one[1][j] - peak) + jnp.exp(two[1][j] - peak))
            block = 0.0
            for context, logs_of in (one, two):
                factor = jnp.broadcast_to(jnp.exp(logs_of[j] - log_sum), (2 * GROUP, HD)).T
                block += factor * context[j * 2 * GROUP : (j + 1) * 2 * GROUP]
            blocks.append(block)
            log_sums.append(log_sum)
        return jnp.concatenate(blocks, axis=0), log_sums

    def both_halves(at, row):
        turned = pltpu.roll(row, GROUP, 1)
        return (at, jnp.where(left, row, turned)), (at + 1, jnp.where(left, turned, row))

    def context_piece(i):
        def first(way, b):
            write(staged.at[i, way], mine(b, i))
            return staged.at[i, way]

        return Scatter(
            copies,
            first,
            lambda ref, b: write(ref, joined(read(ref), mine(b, i))),
            lambda way, s: held.at[i, 4 * way + s],
            HOPS[i % 2],
            along_z,
        )

    def out_piece(i):
        return Sum(
            copies,
            lambda b: part.at[i, b],
            lambda way, s: y_held.at[i, 2 * way + s],
            HOPS_Y[i % 2],
            along_y,
        )

    contexts = [context_piece(i) for i in range(X)]
    outs = [out_piece(i) for i in range(X)]
    upstream = [
        Gather(copies, upall.at[z, i], lambda b, i=i: upall.at[b, i], HOPS[i % 2], along_z)
        for i in range(X)
    ]

    def share(i):
        state = mine(z, i)
        for ref in contexts[i].arrived():
            state = joined(state, read(ref))
        at = ctx4.at[i, :, :, :, columns(x, HD)]
        at[...] = state[0].astype(BF).reshape(Y, C, slots, HD)
        ctx_in[i] = [copies.start(at, at, device(xs[j], z, y, c)) for j in (1, 3, 2)]
        for j in range(2):
            for row, value in both_halves(z * 16 + i * 4 + 2 * j, state[1][j]):
                sums[0, pl.ds(row, 1), :] = value

    def inner(i):
        context = ctx4[i, :, :, :, columns(x, HD)].reshape(TOK, HD)
        product = upall[z, i].astype(F32) * context.astype(F32)
        for j in range(2):
            rows = product[j * 2 * GROUP : (j + 1) * 2 * GROUP]
            total = jnp.sum(rows.T, axis=0, keepdims=True)
            for row, value in both_halves(z * 16 + i * 4 + 2 * j, total):
                sums[1, pl.ds(row, 1), :] = value

    def tell():
        ref = sums.at[:, own]
        return [copies.start(ref, ref, device(x, zs[i], y, c)) for i in order]

    def swap(i):
        for copy in ctx_in[i]:
            copy.wait_recv()
        core_in[i] = copies.start(ctx4.at[i, :, 1 - c], ctx_other.at[i], sibling)

    def multiply(i):
        core_in[i].wait_recv()
        mine = ctx4[i, :, c].reshape(Y * slots, head_cols)
        others = ctx_other[i].reshape(Y * slots, head_cols)
        for j in range(2):
            cols = pl.ds(j * (span // 2), span // 2)
            product = jnp.dot(mine, wf[:, cols], preferred_element_type=F32)
            product += jnp.dot(others, wf_other[:, cols], preferred_element_type=F32)
            part[i, :, :, cols] = product.astype(BF).reshape(Y, slots, span // 2)
        outs[i].step(0)

    def finish_out(i):
        outs[i].step(2)
        done[i] = outs[i].total().astype(BF)
        goal = out.at[:, columns(x, span)]

        @pl.when(x == i)
        def _():
            copy = pltpu.make_async_copy(done.at[i], goal, local.at[7])
            copy.start()
            copy.wait()

        @pl.when(x != i)
        def _():
            sem = step_from(i - x, 0, X)
            pltpu.make_async_remote_copy(
                src_ref=done.at[i],
                dst_ref=goal,
                send_sem=out_send.at[sem],
                recv_sem=out_recv.at[sem],
                device_id=device(i, z, y, c),
                device_id_type=pl.DeviceIdType.MESH,
            ).start()

    step_all(contexts, 0)
    weight_in = copies.start(wf, wf_other, sibling)
    for i in range(X):
        multiply_rows(i)
    for s in (1, 2, 3):
        step_all(contexts, s)
    for i in range(X):
        total_up(i)
    for i in range(X):
        contexts[i].step(4)
        share(i)
    weight_in.wait_recv()
    step_all(upstream[:2], 1)
    swap(0)
    multiply(0)
    step_all(upstream[2:], 1)
    swap(1)
    multiply(1)
    step_all(upstream[:2], 2)
    swap(2)
    multiply(2)
    step_all(upstream[2:], 2)
    swap(3)
    step_all(outs[:1], 1)
    multiply(3)
    for i in range(X):
        inner(i)
    told = tell()
    step_all(outs[1:2], 1)
    step_all(upstream, 3)
    step_all(outs[2:], 1)
    finish_out(0)
    finish_out(1)
    step_all(upstream, 4)
    finish_out(2)
    finish_out(3)
    for copy in told:
        copy.wait_recv()
    for i in (1, 2, 3):
        copy = pltpu.make_async_remote_copy(
            src_ref=done.at[0],
            dst_ref=out.at[:, columns(xs[i], span)],
            send_sem=out_send.at[i],
            recv_sem=out_recv.at[i],
            device_id=device(xs[i], z, y, c),
            device_id_type=pl.DeviceIdType.MESH,
        )
        copy.wait_recv()
        copy.wait_send()
    copies.finish()


def project(logs, ctx, wf, gfull):
    head_cols, span = wf.shape
    slots = TOK // (Y * C)
    return pl.pallas_call(
        project_kernel,
        out_shape=(
            jax.ShapeDtypeStruct((2,) + logs.shape, F32),
            jax.ShapeDtypeStruct(ctx.shape, BF),
            jax.ShapeDtypeStruct((slots, X * span), BF),
        ),
        in_specs=[VMEM] * 4,
        out_specs=[VMEM] * 3,
        scratch_shapes=[
            pltpu.VMEM((head_cols, span), BF),
            pltpu.VMEM((X, TOK, head_cols), BF),
            pltpu.VMEM((X, X - 1, TOK, HD), BF),
            pltpu.VMEM((X, 2, TOK + TAIL, HD), BF),
            pltpu.VMEM((X, 8, TOK + TAIL, HD), BF),
            pltpu.VMEM((X, Y, C, slots, head_cols), BF),
            pltpu.VMEM((X, Y, slots, head_cols), BF),
            pltpu.VMEM((X, Y, slots, span), BF),
            pltpu.VMEM((X, 4, slots, span), BF),
            pltpu.VMEM((X, slots, span), BF),
            pltpu.SemaphoreType.DMA((144,)),
            pltpu.SemaphoreType.DMA((144,)),
            pltpu.SemaphoreType.DMA((4,)),
            pltpu.SemaphoreType.DMA((4,)),
            pltpu.SemaphoreType.DMA((8,)),
        ],
        compiler_params=pltpu.CompilerParams(
            collective_id=1, has_side_effects=True, vmem_limit_bytes=LIMIT
        ),
        name="project",
    )(logs, ctx, wf, gfull)


def grads_kernel(uses, qall, upall, ktab, vtab, sums, gq, dkey, dvalue, dk, dv):
    n = uses[2 * LISTED]
    for ref in (gq, dk, dv):
        clear(ref)

    left = lax.broadcasted_iota(jnp.int32, (1, 2 * GROUP), 1) < GROUP
    zero = jnp.zeros((), BF)

    def dot(a, b):
        return jnp.dot(a, b, preferred_element_type=F32)

    def some(p, carry):
        pairs = uses_at(uses, p, n, GRAD_PAIRS)
        found = []
        for ga, gb, na, nb, real in pairs:
            qq = jnp.concatenate(pair_rows(qall, ga, gb, GROUP), axis=0)
            uu = jnp.concatenate(pair_rows(upall, ga, gb, GROUP), axis=0)
            keys = pair_rows(ktab, na, nb, NLEN)
            values = pair_rows(vtab, na, nb, NLEN)
            scores = pair_scores(*keys, qq, left) * SCALE
            grad_probs = pair_scores(*values, uu, left)
            log_total = jnp.where(left, sums[0, pl.ds(ga, 1), :], sums[0, pl.ds(gb, 1), :])
            inner = jnp.where(left, sums[1, pl.ds(ga, 1), :], sums[1, pl.ds(gb, 1), :])
            prob = jnp.where(real, jnp.exp(scores - log_total), 0.0)
            grad_scores = prob * (grad_probs - inner)
            grad_t = grad_scores.T.astype(BF)
            grad_q = dot(grad_t, jnp.concatenate(keys, axis=1)) * SCALE
            grad_v = dot(halves(prob.astype(BF)), uu)
            grad_k = dot(halves(grad_scores.astype(BF)), qq) * SCALE
            found.append((grad_q, grad_v, grad_k))
        for (ga, gb, na, nb, _), (grad_q, grad_v, grad_k) in zip(pairs, found):
            add_rows(gq, ga, GROUP, grad_q[:GROUP, :HD])
            add_rows(gq, gb, GROUP, grad_q[GROUP:, HD:])
            add_rows(dv, na, NLEN, grad_v[:NLEN])
            add_rows(dv, nb, NLEN, grad_v[NLEN:])
            add_rows(dk, na, NLEN, grad_k[:NLEN])
            add_rows(dk, nb, NLEN, grad_k[NLEN:])
        return carry

    def halves(v):
        return jnp.concatenate([jnp.where(left, v, zero), jnp.where(left, zero, v)], axis=0)

    lax.fori_loop(0, turns(n, GRAD_PAIRS), some, 0)
    for src, dst in ((dk, dkey), (dv, dvalue)):
        rows = 512

        @pl.loop(0, src.shape[0] // rows)
        def _(i, src=src, dst=dst):
            at = pl.ds(pl.multiple_of(i * rows, rows), rows)
            dst[at, :] = src[at, :].astype(BF)


def grads_of_uses(uses, qall, upall, ktab, vtab, sums):
    tokens, rows = qall.shape[0], ktab.shape[0]
    return pl.pallas_call(
        grads_kernel,
        out_shape=(
            jax.ShapeDtypeStruct((tokens, HD), BF),
            jax.ShapeDtypeStruct((rows, HD), BF),
            jax.ShapeDtypeStruct((rows, HD), BF),
        ),
        in_specs=[SMEM] + [VMEM] * 5,
        out_specs=[VMEM] * 3,
        scratch_shapes=[
            pltpu.VMEM((rows, HD), F32),
            pltpu.VMEM((rows, HD), F32),
        ],
        compiler_params=pltpu.CompilerParams(vmem_limit_bytes=LIMIT),
        name="grads",
    )(uses, qall, upall, ktab, vtab, sums)


def collect_kernel(
    gq, dkey, dvalue, gq_out, dk_out, dv_out, held, gq_done, send, recv, local
):
    x, z, y, c = place()
    xs = [step_from(x, i, X) for i in range(X)]
    along_z, _ = rings(x, z, y, c)
    enter([device(xs[i], z, y, c) for i in (1, 2, 3)] + list(along_z[2]))
    copies = Copies(send, recv)
    kept, table_in, gq_sent = [], [], []

    def piece(i):
        return Sum(
            copies,
            lambda b: gq.at[b, xs[i]],
            lambda way, s: held.at[i, 4 * way + s],
            HOPS[i % 2],
            along_z,
        )

    grads = [piece(i) for i in range(X)]
    step_all(grads, 0)
    for src, dst in ((dkey, dk_out), (dvalue, dv_out)):
        goal = dst.at[:, columns(x, HD)]
        for i in (1, 3, 2):
            table_in.append(copies.start(src.at[xs[i]], goal, device(xs[i], z, y, c)))
        start_local(local, kept, src.at[x], goal)
    for s in (1, 2, 3):
        step_all(grads, s)
    for i in (1, 2, 3, 0):
        grads[i].step(4)
        gq_done[i] = grads[i].total().astype(BF)
        goal = gq_out.at[:, columns(x, HD)]
        if i == 0:
            start_local(local, kept, gq_done.at[i], goal)
        else:
            gq_sent.append(copies.start(gq_done.at[i], goal, device(xs[i], z, y, c)))
    for copy in table_in + gq_sent:
        copy.wait_recv()
    for copy in kept:
        copy.wait()
    copies.finish()


def collect(gq, dkey, dvalue):
    rows = dkey.shape[1]
    return pl.pallas_call(
        collect_kernel,
        out_shape=(
            jax.ShapeDtypeStruct((TOK, X * HD), BF),
            jax.ShapeDtypeStruct((rows, X * HD), BF),
            jax.ShapeDtypeStruct((rows, X * HD), BF),
        ),
        in_specs=[VMEM] * 3,
        out_specs=[VMEM] * 3,
        scratch_shapes=[
            pltpu.VMEM((X, 8, TOK, HD), BF),
            pltpu.VMEM((X, TOK, HD), BF),
            pltpu.SemaphoreType.DMA((40,)),
            pltpu.SemaphoreType.DMA((40,)),
            pltpu.SemaphoreType.DMA((8,)),
        ],
        compiler_params=pltpu.CompilerParams(
            collective_id=2, has_side_effects=True, vmem_limit_bytes=LIMIT
        ),
        name="collect",
    )(gq, dkey, dvalue)


def shards(queries, keys, values, out_weight, grad_out, neighbour_owner, neighbour_local):
    ids = jnp.stack([neighbour_owner, neighbour_local], axis=-1).reshape(1, -1)
    ids = jnp.pad(ids, ((0, 0), (0, 128 - ids.shape[1])))
    ids, qall, ktab, vtab, wf, gfull = spread(ids, queries, keys, values, out_weight, grad_out)
    qall = qall.reshape(Z * X * TOK, HD)
    ktab, vtab = (a.reshape(X * keys.shape[0], HD) for a in (ktab, vtab))
    logs, ctx, uses = attend(ids, qall, ktab, vtab)
    sums, upall, out = project(logs, ctx.reshape(Z, X, TOK, HD), wf, gfull)
    upall = upall.reshape(Z * X * TOK, HD)
    gq, dkey, dvalue = grads_of_uses(uses, qall, upall, ktab, vtab, sums)
    dkey, dvalue = (a.reshape((X,) + keys.shape[:1] + (HD,)) for a in (dkey, dvalue))
    grad_queries, grad_keys, grad_values = collect(gq.reshape(Z, X, TOK, HD), dkey, dvalue)
    return out, grad_queries, grad_keys.astype(F32), grad_values.astype(F32)


def solution(mesh):
    return jax.shard_map(
        shards,
        mesh=mesh,
        in_specs=(
            P("dp", "tensor"),
            P("dp", "tensor"),
            P("dp", "tensor"),
            P("tensor", "dp"),
            P(("dp", "tensor"), None),
            P("dp", None),
            P("dp", None),
        ),
        out_specs=(
            P(("dp", "tensor"), None),
            P("dp", "tensor"),
            P("dp", "tensor"),
            P("dp", "tensor"),
        ),
        check_vma=False,
    )
```

```python
import jax
import jax.numpy as jnp
from jax import lax
from jax.experimental import pallas as pl
from jax.experimental.pallas import tpu as pltpu
from jax.sharding import PartitionSpec as P

X, Z, Y, C = 4, 8, 4, 2
HD = 128
GROUP = 64
NLEN = 128
NB_DEV = 8
TOK = 256
SCALE = HD**-0.5
LOW = -1e30
BF = jnp.bfloat16
F32 = jnp.float32
VMEM = pl.BlockSpec(memory_space=pltpu.VMEM)
SMEM = pl.BlockSpec(memory_space=pltpu.SMEM)
HBM = pl.BlockSpec(memory_space=pltpu.HBM)
LIMIT = 28 * 1024 * 1024
PAIRS, GRAD_PAIRS = 8, 4


def place():
    dp, t = lax.axis_index("dp"), lax.axis_index("tensor")
    return lax.div(dp, Z), lax.rem(dp, Z), lax.div(t, C), lax.rem(t, C)


def device(x, z, y, c):
    return (x * Z + z, y * C + c)


def step_from(i, by, n):
    return lax.rem(i + (by + n), n)


def columns(i, width):
    return pl.ds(pl.multiple_of(i * width, width), width)


def enter(peers):
    barrier = pltpu.get_barrier_semaphore()
    for peer in peers:
        pl.semaphore_signal(barrier, inc=1, device_id=peer, device_id_type=pl.DeviceIdType.MESH)
    pl.semaphore_wait(barrier, len(peers))


class Copies:
    def __init__(self, send, recv):
        self.send, self.recv, self.count, self.started = send, recv, 0, []

    def take(self, n=1):
        first = self.count
        self.count += n
        return first

    def make(self, sem, src, dst, to):
        return pltpu.make_async_remote_copy(
            src_ref=src,
            dst_ref=dst,
            send_sem=self.send.at[sem],
            recv_sem=self.recv.at[sem],
            device_id=to,
            device_id_type=pl.DeviceIdType.MESH,
        )

    def start(self, src, dst, to):
        copy = self.make(self.take(), src, dst, to)
        copy.start()
        self.started.append(copy)
        return copy

    def finish(self):
        for copy in self.started:
            copy.wait_send()


class Gather:
    def __init__(self, copies, first, view, hops, ring, arrived=None):
        self.copies, self.first, self.view, self.hops = copies, first, view, hops
        self.place, self.size, self.sides = ring
        self.arrived = arrived
        self.sent = [[], []]

    def step(self, s):
        for way, sign in ((0, 1), (1, -1)):
            block = step_from(self.place, -sign * s, self.size)
            if 0 < s <= self.hops[way]:
                self.sent[way][s - 1].wait_recv()
            if s < self.hops[way]:
                src = self.first if s == 0 else self.view(block)
                self.sent[way].append(self.copies.start(src, self.view(block), self.sides[way]))
            if self.arrived is not None and 0 < s <= self.hops[way]:
                self.arrived(block)


class Scatter:
    def __init__(self, copies, first, join, held, hops, ring):
        self.copies, self.first, self.join, self.held, self.hops = copies, first, join, held, hops
        self.place, self.size, self.sides = ring
        self.sent = [[], []]

    def step(self, s):
        for way, sign in ((0, 1), (1, -1)):
            n = self.hops[way]
            if 0 < s <= n:
                self.sent[way][s - 1].wait_recv()
            if s < n:
                goal = step_from(self.place, sign * (n - s), self.size)
                if s == 0:
                    src = self.first(way, goal)
                else:
                    src = self.held(way, s - 1)
                    self.join(src, goal)
                self.sent[way].append(self.copies.start(src, self.held(way, s), self.sides[way]))

    def arrived(self):
        return [self.held(way, self.hops[way] - 1) for way in (0, 1)]


class Sum(Scatter):
    def __init__(self, copies, part, held, hops, ring):
        def join(ref, goal):
            ref[...] = (ref[...].astype(F32) + part(goal)[...].astype(F32)).astype(BF)

        super().__init__(copies, lambda way, b: part(b), join, held, hops, ring)
        self.part = part

    def total(self):
        total = self.part(self.place)[...].astype(F32)
        for ref in self.arrived():
            total += ref[...].astype(F32)
        return total


def rings(x, z, y, c):
    along_z = z, Z, tuple(device(x, step_from(z, i, Z), y, c) for i in (1, -1))
    along_y = y, Y, tuple(device(x, z, step_from(y, i, Y), c) for i in (1, -1))
    return along_z, along_y


HOPS = ((4, 3), (3, 4))
HOPS_Y = ((2, 1), (1, 2))


def start_local(local, kept, src, dst):
    copy = pltpu.make_async_copy(src, dst, local.at[len(kept)])
    copy.start()
    kept.append(copy)


def step_all(pieces, s):
    for one in pieces:
        one.step(s)


def spread_kernel(
    ids_ref, q_ref, k_ref, v_ref, w_ref, g_ref,
    idall, qall, ktab, vtab, wf, gfull,
    send, recv, local,
):
    x, z, y, c = place()
    t = y * C + c
    width = w_ref.shape[1]
    depth = w_ref.shape[0] // 4
    span = Z * width
    xs = [step_from(x, i, X) for i in range(X)]
    along_z, along_y = rings(x, z, y, c)
    sibling = device(x, z, y, 1 - c)
    enter(
        [device(xs[i], z, y, c) for i in (1, 2, 3)]
        + list(along_z[2])
        + list(along_y[2])
        + [sibling]
    )
    copies = Copies(send, recv)
    kept = []

    def keep(src, dst):
        start_local(local, kept, src, dst)

    table_in, q_in, g_core = [], [], {}

    def piece(ref, i):
        return Gather(copies, ref.at[z, i], lambda b: ref.at[b, i], HOPS[i % 2], along_z)

    def weight_piece(i):
        rows = pl.ds(i * depth, depth)
        return Gather(
            copies, w_ref.at[rows], lambda b: wf.at[rows, columns(b, width)], HOPS[i % 2], along_z
        )

    weights = [weight_piece(i) for i in range(4)]
    asked = [piece(qall, i) for i in range(X)]
    asked.append(Gather(copies, idall.at[z], lambda b: idall.at[b], HOPS[0], along_z))

    def send_table(src, dst):
        for i in (1, 3, 2):
            to = device(xs[i], z, y, c)
            table_in.append(copies.start(src.at[:, columns(xs[i], HD)], dst.at[x], to))

    def hand_over(i, block):
        block = gfull.at[i, block * C + c]
        g_core[i].append(copies.start(block, block, sibling))

    def rows_piece(i):
        return Gather(
            copies,
            gfull.at[i, t],
            lambda b: gfull.at[i, b * C + c],
            HOPS_Y[i % 2],
            along_y,
            lambda b: hand_over(i, b),
        )

    rows = [rows_piece(i) for i in range(X)]

    def send_rows(i):
        rows[i].step(0)
        g_core[i] = []
        hand_over(i, y)

    for i in (1, 3, 2):
        to = device(xs[i], z, y, c)
        q_in.append(copies.start(q_ref.at[:, columns(xs[i], HD)], qall.at[z, x], to))
        q_in.append(copies.start(ids_ref, idall.at[z, x], to))
    step_all(weights, 0)
    g_in = [
        copies.start(g_ref.at[:, columns(xs[i], span)], gfull.at[x, t], device(xs[i], z, y, c))
        for i in (1, 3, 2)
    ]
    keep(q_ref.at[:, columns(x, HD)], qall.at[z, x])
    keep(ids_ref, idall.at[z, x])
    keep(g_ref.at[:, columns(x, span)], gfull.at[x, t])
    keep(w_ref, wf.at[:, columns(z, width)])
    keep(k_ref.at[:, columns(x, HD)], ktab.at[x])
    keep(v_ref.at[:, columns(x, HD)], vtab.at[x])
    for copy in q_in:
        copy.wait_recv()
    for copy in kept[:2]:
        copy.wait()
    step_all(asked, 0)
    send_table(k_ref, ktab)
    send_table(v_ref, vtab)
    step_all(weights, 1)
    kept[2].wait()
    for copy in g_in:
        copy.wait_recv()
    send_rows(0)
    send_rows(1)
    step_all(asked, 1)
    step_all(rows[:2], 1)
    send_rows(2)
    send_rows(3)
    step_all(weights, 2)
    step_all(rows[:2], 2)
    step_all(asked, 2)
    step_all(rows[2:], 1)
    step_all(weights, 3)
    step_all(rows[2:], 2)
    step_all(asked, 3)
    step_all(weights, 4)
    step_all(asked, 4)
    for i in range(X):
        for copy in g_core[i]:
            copy.wait_recv()
    for copy in table_in:
        copy.wait_recv()
    for copy in kept[3:]:
        copy.wait()
    copies.finish()


def spread(ids, queries, keys, values, out_weight, grad_out):
    depth, width = out_weight.shape
    rows = keys.shape[0]
    return pl.pallas_call(
        spread_kernel,
        out_shape=(
            jax.ShapeDtypeStruct((Z, X) + ids.shape, jnp.int32),
            jax.ShapeDtypeStruct((Z, X, TOK, HD), BF),
            jax.ShapeDtypeStruct((X, rows, HD), BF),
            jax.ShapeDtypeStruct((X, rows, HD), BF),
            jax.ShapeDtypeStruct((depth, Z * width), BF),
            jax.ShapeDtypeStruct((X, Y * C, grad_out.shape[0], Z * width), BF),
        ),
        in_specs=[VMEM] + [HBM] * 5,
        out_specs=[VMEM] * 6,
        scratch_shapes=[
            pltpu.SemaphoreType.DMA((112,)),
            pltpu.SemaphoreType.DMA((112,)),
            pltpu.SemaphoreType.DMA((8,)),
        ],
        compiler_params=pltpu.CompilerParams(
            collective_id=0, has_side_effects=True, vmem_limit_bytes=LIMIT
        ),
        name="spread",
    )(ids, queries, keys, values, out_weight, grad_out)


TAIL = 16
LISTED = 256 + 32


def list_uses(ids, uses):
    z = lax.rem(lax.axis_index("dp"), Z)

    def add(dp, n):
        dp_z, dp_x = lax.shift_right_logical(dp, 2), dp & 3
        named = [ids[dp_z, dp_x, 0, j] for j in range(16)]
        for j in range(8):
            owner, name = named[2 * j : 2 * j + 2]
            uses[n] = dp * 4 + j // 2
            uses[LISTED + n] = lax.shift_right_logical(owner, 3) * NB_DEV + name
            n = n + ((owner & 7) == z).astype(jnp.int32)
        return n

    n = lax.fori_loop(0, X * Z, add, jnp.int32(0), unroll=2)
    last = jnp.maximum(n - 1, 0)
    for i in range(2 * PAIRS - 1):
        uses[n + i] = uses[last]
        uses[LISTED + n + i] = uses[LISTED + last]
    uses[2 * LISTED] = n
    return n


def uses_at(uses, p, n, pairs):
    lane = lax.broadcasted_iota(jnp.int32, (1, 2 * GROUP), 1)
    out = []
    for i in range(pairs):
        a = 2 * (pairs * p + i)
        b = a + 1
        real = jnp.where(lane < GROUP, a, b) < n
        out.append((uses[a], uses[b], uses[LISTED + a], uses[LISTED + b], real))
    return out


def turns(n, pairs):
    return lax.div(n + (2 * pairs - 1), 2 * pairs)


def pair_rows(ref, a, b, size):
    return [ref[pl.ds(pl.multiple_of(i * size, size), size), :] for i in (a, b)]


def pair_scores(first, second, both, left):
    product = lax.dot_general(
        jnp.concatenate([first, second], axis=0),
        both,
        (((1,), (1,)), ((), ())),
        preferred_element_type=F32,
    )
    return jnp.where(left, product[:NLEN], product[NLEN:])


def merge(one, two):
    peak = jnp.maximum(one[0], two[0])
    return peak, jnp.exp(one[0] - peak) * one[1] + jnp.exp(two[0] - peak) * two[1]


def clear(ref, rows=512):
    @pl.loop(0, ref.shape[0] // rows)
    def _(i):
        ref[pl.ds(pl.multiple_of(i * rows, rows), rows), :] = jnp.zeros((rows, HD), ref.dtype)


def add_rows(ref, i, size, value):
    at = pl.ds(pl.multiple_of(i * size, size), size)
    ref[at, :] = (ref[at, :].astype(F32) + value).astype(ref.dtype)


def attend_kernel(ids, qall, ktab, vtab, logs, ctx, uses, stats):
    n = list_uses(ids, uses)
    stats[0] = jnp.full(stats.shape[1:], LOW, F32)
    stats[1] = jnp.zeros(stats.shape[1:], F32)
    clear(ctx)
    left = lax.broadcasted_iota(jnp.int32, (1, 2 * GROUP), 1) < GROUP

    def scores_of(ga, gb, na, nb):
        qq = jnp.concatenate(pair_rows(qall, ga, gb, GROUP), axis=0)
        return pair_scores(*pair_rows(ktab, na, nb, NLEN), qq, left) * SCALE

    def measure(p, carry):
        pairs = uses_at(uses, p, n, PAIRS)
        found = []
        for ga, gb, na, nb, real in pairs:
            scores = scores_of(ga, gb, na, nb)
            peak = jnp.max(scores, axis=0, keepdims=True)
            total = jnp.sum(jnp.exp(scores - peak), axis=0, keepdims=True)
            found.append((jnp.where(real, peak, LOW), jnp.where(real, total, 0.0)))
        for (ga, gb, *_), new in zip(pairs, found):
            for g, mine in ((ga, left), (gb, jnp.logical_not(left))):
                old = tuple(stats[i, pl.ds(g, 1), :] for i in range(2))
                merged = merge(old, new)
                for i in range(2):
                    stats[i, pl.ds(g, 1), :] = jnp.where(mine, merged[i], old[i])
        return carry

    def weigh(p, carry):
        pairs = uses_at(uses, p, n, PAIRS)
        found = []
        for ga, gb, na, nb, real in pairs:
            scores = scores_of(ga, gb, na, nb)
            log_total = jnp.where(left, logs[pl.ds(ga, 1), :], logs[pl.ds(gb, 1), :])
            prob = jnp.where(real, jnp.exp(scores - log_total), 0.0)
            values = pair_rows(vtab, na, nb, NLEN)
            found.append(
                jnp.dot(
                    prob.T.astype(BF),
                    jnp.concatenate(values, axis=1),
                    preferred_element_type=F32,
                )
            )
        for (ga, gb, *_), context in zip(pairs, found):
            add_rows(ctx, ga, GROUP, context[:GROUP, :HD])
            add_rows(ctx, gb, GROUP, context[GROUP:, HD:])
        return carry

    lax.fori_loop(0, turns(n, PAIRS), measure, 0)
    state = stats[0], stats[1]
    peak, total = merge(state, tuple(pltpu.roll(v, GROUP, 1) for v in state))
    logs[...] = jnp.where(total > 0.0, peak + jnp.log(jnp.maximum(total, 1e-30)), LOW)
    lax.fori_loop(0, turns(n, PAIRS), weigh, 0)


def attend(ids, qall, ktab, vtab):
    return pl.pallas_call(
        attend_kernel,
        out_shape=(
            jax.ShapeDtypeStruct((16 * Z, 2 * GROUP), F32),
            jax.ShapeDtypeStruct(qall.shape, BF),
            jax.ShapeDtypeStruct((2 * LISTED + 64,), jnp.int32),
        ),
        in_specs=[SMEM] + [VMEM] * 3,
        out_specs=[VMEM] * 2 + [SMEM],
        scratch_shapes=[
            pltpu.VMEM((2, 16 * Z, 2 * GROUP), F32),
        ],
        compiler_params=pltpu.CompilerParams(vmem_limit_bytes=LIMIT),
        name="attend",
    )(ids, qall, ktab, vtab)


def project_kernel(
    logs, ctx, wf, gfull,
    sums, upall, out,
    wf_other, upp, upr, staged, held, ctx4, ctx_other, part, y_held, done,
    send, recv, out_send, out_recv, local,
):
    x, z, y, c = place()
    head_cols, span = wf.shape
    slots = TOK // (Y * C)
    xs = [step_from(x, i, X) for i in range(X)]
    along_z, along_y = rings(x, z, y, c)
    sibling = device(x, z, y, 1 - c)
    enter(
        [device(xs[i], z, y, c) for i in (1, 2, 3)]
        + list(along_z[2])
        + list(along_y[2])
        + [sibling]
    )
    copies = Copies(send, recv)
    left = lax.broadcasted_iota(jnp.int32, (1, 2 * GROUP), 1) < GROUP
    up_in, ctx_in, core_in = {}, {}, {}

    def multiply_rows(i):
        upp[i] = lax.dot_general(
            gfull[i].reshape(TOK, span),
            wf[...],
            (((1,), (1,)), ((), ())),
            preferred_element_type=F32,
        ).astype(BF)
        up_in[i] = [
            copies.start(
                upp.at[i, :, columns(xs[j], HD)], upr.at[i, j - 1], device(xs[j], z, y, c)
            )
            for j in (1, 3, 2)
        ]

    def total_up(i):
        for copy in up_in[i]:
            copy.wait_recv()
        value = upp[i, :, columns(x, HD)].astype(F32)
        for j in range(3):
            value += upr[i, j].astype(F32)
        upall[z, i] = value.astype(BF)
        upstream[i].step(0)

    def mine(b, i):
        rows = [logs[pl.ds(b * 16 + i * 4 + j, 1), :] for j in range(4)]
        return ctx[b, i].astype(F32), [jnp.where(left, *rows[j : j + 2]) for j in (0, 2)]

    def write(ref, state):
        ref[:TOK] = state[0].astype(BF)
        rows = []
        for rest in state[1]:
            for _ in range(3):
                rows.append(rest.astype(BF).astype(F32))
                rest = rest - rows[-1]
        rows.append(jnp.zeros((TAIL - len(rows), HD), F32))
        ref[TOK:] = jnp.concatenate(rows, axis=0).astype(BF)

    def read(ref):
        rows = ref[TOK:].astype(F32)
        sums_of = [rows[3 * j : 3 * j + 1] + rows[3 * j + 1 : 3 * j + 2] for j in range(2)]
        return ref[:TOK].astype(F32), [v + rows[3 * j + 2 : 3 * j + 3] for j, v in enumerate(sums_of)]

    def joined(one, two):
        blocks, log_sums = [], []
        for j in range(2):
            peak = jnp.maximum(one[1][j], two[1][j])
            log_sum = peak + jnp.log(jnp.exp(one[1][j] - peak) + jnp.exp(two[1][j] - peak))
            block = 0.0
            for context, logs_of in (one, two):
                factor = jnp.broadcast_to(jnp.exp(logs_of[j] - log_sum), (2 * GROUP, HD)).T
                block += factor * context[j * 2 * GROUP : (j + 1) * 2 * GROUP]
            blocks.append(block)
            log_sums.append(log_sum)
        return jnp.concatenate(blocks, axis=0), log_sums

    def both_halves(at, row):
        turned = pltpu.roll(row, GROUP, 1)
        return (at, jnp.where(left, row, turned)), (at + 1, jnp.where(left, turned, row))

    def context_piece(i):
        def first(way, b):
            write(staged.at[i, way], mine(b, i))
            return staged.at[i, way]

        return Scatter(
            copies,
            first,
            lambda ref, b: write(ref, joined(read(ref), mine(b, i))),
            lambda way, s: held.at[i, 4 * way + s],
            HOPS[i % 2],
            along_z,
        )

    def out_piece(i):
        return Sum(
            copies,
            lambda b: part.at[i, b],
            lambda way, s: y_held.at[i, 2 * way + s],
            HOPS_Y[i % 2],
            along_y,
        )

    contexts = [context_piece(i) for i in range(X)]
    outs = [out_piece(i) for i in range(X)]
    upstream = [
        Gather(copies, upall.at[z, i], lambda b, i=i: upall.at[b, i], HOPS[i % 2], along_z)
        for i in range(X)
    ]

    def share(i):
        state = mine(z, i)
        for ref in contexts[i].arrived():
            state = joined(state, read(ref))
        at = ctx4.at[i, :, :, :, columns(x, HD)]
        at[...] = state[0].astype(BF).reshape(Y, C, slots, HD)
        ctx_in[i] = [copies.start(at, at, device(xs[j], z, y, c)) for j in (1, 3, 2)]
        for j in range(2):
            for row, value in both_halves(z * 16 + i * 4 + 2 * j, state[1][j]):
                sums[0, pl.ds(row, 1), :] = value

    def inner(i):
        context = ctx4[i, :, :, :, columns(x, HD)].reshape(TOK, HD)
        product = upall[z, i].astype(F32) * context.astype(F32)
        for j in range(2):
            rows = product[j * 2 * GROUP : (j + 1) * 2 * GROUP]
            total = jnp.sum(rows.T, axis=0, keepdims=True)
            for row, value in both_halves(z * 16 + i * 4 + 2 * j, total):
                sums[1, pl.ds(row, 1), :] = value

    def swap(i):
        for copy in ctx_in[i]:
            copy.wait_recv()
        core_in[i] = copies.start(ctx4.at[i, :, 1 - c], ctx_other.at[i], sibling)

    def multiply(i):
        core_in[i].wait_recv()
        mine = ctx4[i, :, c].reshape(Y * slots, head_cols)
        others = ctx_other[i].reshape(Y * slots, head_cols)
        for j in range(2):
            cols = pl.ds(j * (span // 2), span // 2)
            product = jnp.dot(mine, wf[:, cols], preferred_element_type=F32)
            product += jnp.dot(others, wf_other[:, cols], preferred_element_type=F32)
            part[i, :, :, cols] = product.astype(BF).reshape(Y, slots, span // 2)
        outs[i].step(0)

    def finish_out(i):
        outs[i].step(2)
        done[i] = outs[i].total().astype(BF)
        goal = out.at[:, columns(x, span)]

        @pl.when(x == i)
        def _():
            copy = pltpu.make_async_copy(done.at[i], goal, local.at[7])
            copy.start()
            copy.wait()

        @pl.when(x != i)
        def _():
            sem = step_from(i - x, 0, X)
            pltpu.make_async_remote_copy(
                src_ref=done.at[i],
                dst_ref=goal,
                send_sem=out_send.at[sem],
                recv_sem=out_recv.at[sem],
                device_id=device(i, z, y, c),
                device_id_type=pl.DeviceIdType.MESH,
            ).start()

    told = Gather(
        copies,
        sums.at[:, columns(z, 16)],
        lambda b: sums.at[:, columns(b, 16)],
        HOPS[0],
        along_z,
    )

    step_all(contexts, 0)
    weight_in = copies.start(wf, wf_other, sibling)
    for i in range(X):
        multiply_rows(i)
    for s in (1, 2, 3):
        step_all(contexts, s)
    for i in range(X):
        total_up(i)
    for i in range(X):
        contexts[i].step(4)
        share(i)
    weight_in.wait_recv()
    step_all(upstream[:2], 1)
    for i in range(X):
        inner(i)
    told.step(0)
    swap(0)
    multiply(0)
    step_all(upstream[2:], 1)
    swap(1)
    multiply(1)
    told.step(1)
    step_all(upstream[:2], 2)
    swap(2)
    multiply(2)
    step_all(upstream[2:], 2)
    swap(3)
    step_all(outs[:1], 1)
    multiply(3)
    told.step(2)
    step_all(outs[1:2], 1)
    step_all(upstream, 3)
    step_all(outs[2:], 1)
    told.step(3)
    finish_out(0)
    finish_out(1)
    step_all(upstream, 4)
    told.step(4)
    finish_out(2)
    finish_out(3)
    for i in (1, 2, 3):
        copy = pltpu.make_async_remote_copy(
            src_ref=done.at[0],
            dst_ref=out.at[:, columns(xs[i], span)],
            send_sem=out_send.at[i],
            recv_sem=out_recv.at[i],
            device_id=device(xs[i], z, y, c),
            device_id_type=pl.DeviceIdType.MESH,
        )
        copy.wait_recv()
        copy.wait_send()
    copies.finish()


def project(logs, ctx, wf, gfull):
    head_cols, span = wf.shape
    slots = TOK // (Y * C)
    return pl.pallas_call(
        project_kernel,
        out_shape=(
            jax.ShapeDtypeStruct((2,) + logs.shape, F32),
            jax.ShapeDtypeStruct(ctx.shape, BF),
            jax.ShapeDtypeStruct((slots, X * span), BF),
        ),
        in_specs=[VMEM] * 4,
        out_specs=[VMEM] * 3,
        scratch_shapes=[
            pltpu.VMEM((head_cols, span), BF),
            pltpu.VMEM((X, TOK, head_cols), BF),
            pltpu.VMEM((X, X - 1, TOK, HD), BF),
            pltpu.VMEM((X, 2, TOK + TAIL, HD), BF),
            pltpu.VMEM((X, 8, TOK + TAIL, HD), BF),
            pltpu.VMEM((X, Y, C, slots, head_cols), BF),
            pltpu.VMEM((X, Y, slots, head_cols), BF),
            pltpu.VMEM((X, Y, slots, span), BF),
            pltpu.VMEM((X, 4, slots, span), BF),
            pltpu.VMEM((X, slots, span), BF),
            pltpu.SemaphoreType.DMA((144,)),
            pltpu.SemaphoreType.DMA((144,)),
            pltpu.SemaphoreType.DMA((4,)),
            pltpu.SemaphoreType.DMA((4,)),
            pltpu.SemaphoreType.DMA((8,)),
        ],
        compiler_params=pltpu.CompilerParams(
            collective_id=1, has_side_effects=True, vmem_limit_bytes=LIMIT
        ),
        name="project",
    )(logs, ctx, wf, gfull)


def grads_kernel(uses, qall, upall, ktab, vtab, sums, gq, dkey, dvalue, dk, dv):
    n = uses[2 * LISTED]
    for ref in (gq, dk, dv):
        clear(ref)

    left = lax.broadcasted_iota(jnp.int32, (1, 2 * GROUP), 1) < GROUP
    zero = jnp.zeros((), BF)

    def dot(a, b):
        return jnp.dot(a, b, preferred_element_type=F32)

    def some(p, carry):
        pairs = uses_at(uses, p, n, GRAD_PAIRS)
        found = []
        for ga, gb, na, nb, real in pairs:
            qq = jnp.concatenate(pair_rows(qall, ga, gb, GROUP), axis=0)
            uu = jnp.concatenate(pair_rows(upall, ga, gb, GROUP), axis=0)
            keys = pair_rows(ktab, na, nb, NLEN)
            values = pair_rows(vtab, na, nb, NLEN)
            scores = pair_scores(*keys, qq, left) * SCALE
            grad_probs = pair_scores(*values, uu, left)
            log_total = jnp.where(left, sums[0, pl.ds(ga, 1), :], sums[0, pl.ds(gb, 1), :])
            inner = jnp.where(left, sums[1, pl.ds(ga, 1), :], sums[1, pl.ds(gb, 1), :])
            prob = jnp.where(real, jnp.exp(scores - log_total), 0.0)
            grad_scores = prob * (grad_probs - inner)
            grad_t = grad_scores.T.astype(BF)
            grad_q = dot(grad_t, jnp.concatenate(keys, axis=1)) * SCALE
            grad_v = dot(halves(prob.astype(BF)), uu)
            grad_k = dot(halves(grad_scores.astype(BF)), qq) * SCALE
            found.append((grad_q, grad_v, grad_k))
        for (ga, gb, na, nb, _), (grad_q, grad_v, grad_k) in zip(pairs, found):
            add_rows(gq, ga, GROUP, grad_q[:GROUP, :HD])
            add_rows(gq, gb, GROUP, grad_q[GROUP:, HD:])
            add_rows(dv, na, NLEN, grad_v[:NLEN])
            add_rows(dv, nb, NLEN, grad_v[NLEN:])
            add_rows(dk, na, NLEN, grad_k[:NLEN])
            add_rows(dk, nb, NLEN, grad_k[NLEN:])
        return carry

    def halves(v):
        return jnp.concatenate([jnp.where(left, v, zero), jnp.where(left, zero, v)], axis=0)

    lax.fori_loop(0, turns(n, GRAD_PAIRS), some, 0)
    for src, dst in ((dk, dkey), (dv, dvalue)):
        rows = 512

        @pl.loop(0, src.shape[0] // rows)
        def _(i, src=src, dst=dst):
            at = pl.ds(pl.multiple_of(i * rows, rows), rows)
            dst[at, :] = src[at, :].astype(BF)


def grads_of_uses(uses, qall, upall, ktab, vtab, sums):
    tokens, rows = qall.shape[0], ktab.shape[0]
    return pl.pallas_call(
        grads_kernel,
        out_shape=(
            jax.ShapeDtypeStruct((tokens, HD), BF),
            jax.ShapeDtypeStruct((rows, HD), BF),
            jax.ShapeDtypeStruct((rows, HD), BF),
        ),
        in_specs=[SMEM] + [VMEM] * 5,
        out_specs=[VMEM] * 3,
        scratch_shapes=[
            pltpu.VMEM((rows, HD), F32),
            pltpu.VMEM((rows, HD), F32),
        ],
        compiler_params=pltpu.CompilerParams(vmem_limit_bytes=LIMIT),
        name="grads",
    )(uses, qall, upall, ktab, vtab, sums)


def collect_kernel(
    gq, dkey, dvalue, gq_out, dk_out, dv_out, held, gq_done, send, recv, local
):
    x, z, y, c = place()
    xs = [step_from(x, i, X) for i in range(X)]
    along_z, _ = rings(x, z, y, c)
    enter([device(xs[i], z, y, c) for i in (1, 2, 3)] + list(along_z[2]))
    copies = Copies(send, recv)
    kept, table_in, gq_sent = [], [], []

    def piece(i):
        return Sum(
            copies,
            lambda b: gq.at[b, xs[i]],
            lambda way, s: held.at[i, 4 * way + s],
            HOPS[i % 2],
            along_z,
        )

    grads = [piece(i) for i in range(X)]
    step_all(grads, 0)
    for src, dst in ((dkey, dk_out), (dvalue, dv_out)):
        goal = dst.at[:, columns(x, HD)]
        for i in (1, 3, 2):
            table_in.append(copies.start(src.at[xs[i]], goal, device(xs[i], z, y, c)))
        start_local(local, kept, src.at[x], goal)
    for s in (1, 2, 3):
        step_all(grads, s)
    for i in (1, 2, 3, 0):
        grads[i].step(4)
        gq_done[i] = grads[i].total().astype(BF)
        goal = gq_out.at[:, columns(x, HD)]
        if i == 0:
            start_local(local, kept, gq_done.at[i], goal)
        else:
            gq_sent.append(copies.start(gq_done.at[i], goal, device(xs[i], z, y, c)))
    for copy in table_in + gq_sent:
        copy.wait_recv()
    for copy in kept:
        copy.wait()
    copies.finish()


def collect(gq, dkey, dvalue):
    rows = dkey.shape[1]
    return pl.pallas_call(
        collect_kernel,
        out_shape=(
            jax.ShapeDtypeStruct((TOK, X * HD), BF),
            jax.ShapeDtypeStruct((rows, X * HD), BF),
            jax.ShapeDtypeStruct((rows, X * HD), BF),
        ),
        in_specs=[VMEM] * 3,
        out_specs=[VMEM] * 3,
        scratch_shapes=[
            pltpu.VMEM((X, 8, TOK, HD), BF),
            pltpu.VMEM((X, TOK, HD), BF),
            pltpu.SemaphoreType.DMA((40,)),
            pltpu.SemaphoreType.DMA((40,)),
            pltpu.SemaphoreType.DMA((8,)),
        ],
        compiler_params=pltpu.CompilerParams(
            collective_id=2, has_side_effects=True, vmem_limit_bytes=LIMIT
        ),
        name="collect",
    )(gq, dkey, dvalue)


def finish_kernel(out, gq, dkey, dvalue, out_to, gq_to, dk_to, dv_to, wide, sems):
    copies = []

    def send(src, dst):
        copies.append(pltpu.make_async_copy(src, dst, sems.at[len(copies)]))
        copies[-1].start()

    rows = dkey.shape[0] // 4
    for i, (src, dst) in enumerate(((dkey, dk_to), (dvalue, dv_to))):
        for j in range(4):
            at = pl.ds(j * rows, rows)
            wide[i, at] = src[at].astype(F32)
            send(wide.at[i, at], dst.at[at])
    send(out, out_to)
    send(gq, gq_to)
    for copy in copies:
        copy.wait()


def finish(out, gq, dkey, dvalue):
    return pl.pallas_call(
        finish_kernel,
        out_shape=(
            jax.ShapeDtypeStruct(out.shape, BF),
            jax.ShapeDtypeStruct(gq.shape, BF),
            jax.ShapeDtypeStruct(dkey.shape, F32),
            jax.ShapeDtypeStruct(dvalue.shape, F32),
        ),
        in_specs=[VMEM] * 4,
        out_specs=[HBM] * 4,
        scratch_shapes=[
            pltpu.VMEM((2,) + dkey.shape, F32),
            pltpu.SemaphoreType.DMA((10,)),
        ],
        compiler_params=pltpu.CompilerParams(vmem_limit_bytes=LIMIT),
        name="finish",
    )(out, gq, dkey, dvalue)


def shards(queries, keys, values, out_weight, grad_out, neighbour_owner, neighbour_local):
    ids = jnp.stack([neighbour_owner, neighbour_local], axis=-1).reshape(1, -1)
    ids = jnp.pad(ids, ((0, 0), (0, 128 - ids.shape[1])))
    ids, qall, ktab, vtab, wf, gfull = spread(ids, queries, keys, values, out_weight, grad_out)
    qall = qall.reshape(Z * X * TOK, HD)
    ktab, vtab = (a.reshape(X * keys.shape[0], HD) for a in (ktab, vtab))
    logs, ctx, uses = attend(ids, qall, ktab, vtab)
    sums, upall, out = project(logs, ctx.reshape(Z, X, TOK, HD), wf, gfull)
    upall = upall.reshape(Z * X * TOK, HD)
    gq, dkey, dvalue = grads_of_uses(uses, qall, upall, ktab, vtab, sums)
    dkey, dvalue = (a.reshape((X,) + keys.shape[:1] + (HD,)) for a in (dkey, dvalue))
    grad_queries, grad_keys, grad_values = collect(gq.reshape(Z, X, TOK, HD), dkey, dvalue)
    return finish(out, grad_queries, grad_keys, grad_values)


def solution(mesh):
    return jax.shard_map(
        shards,
        mesh=mesh,
        in_specs=(
            P("dp", "tensor"),
            P("dp", "tensor"),
            P("dp", "tensor"),
            P("tensor", "dp"),
            P(("dp", "tensor"), None),
            P("dp", None),
            P("dp", None),
        ),
        out_specs=(
            P(("dp", "tensor"), None),
            P("dp", "tensor"),
            P("dp", "tensor"),
            P("dp", "tensor"),
        ),
        check_vma=False,
    )
```

```python
import jax
import jax.numpy as jnp
from jax import lax
from jax.experimental import pallas as pl
from jax.experimental.pallas import tpu as pltpu
from jax.sharding import PartitionSpec as P

X, Z, Y, C = 4, 8, 4, 2
HD = 128
GROUP = 64
NLEN = 128
NB_DEV = 8
TOK = 256
SCALE = HD**-0.5
LOW = -1e30
BF = jnp.bfloat16
F32 = jnp.float32
VMEM = pl.BlockSpec(memory_space=pltpu.VMEM)
SMEM = pl.BlockSpec(memory_space=pltpu.SMEM)
HBM = pl.BlockSpec(memory_space=pltpu.HBM)
LIMIT = 28 * 1024 * 1024
PAIRS, GRAD_PAIRS = 8, 4


def place():
    dp, t = lax.axis_index("dp"), lax.axis_index("tensor")
    return lax.div(dp, Z), lax.rem(dp, Z), lax.div(t, C), lax.rem(t, C)


def device(x, z, y, c):
    return (x * Z + z, y * C + c)


def step_from(i, by, n):
    return lax.rem(i + (by + n), n)


def columns(i, width):
    return pl.ds(pl.multiple_of(i * width, width), width)


def enter(peers):
    barrier = pltpu.get_barrier_semaphore()
    for peer in peers:
        pl.semaphore_signal(barrier, inc=1, device_id=peer, device_id_type=pl.DeviceIdType.MESH)
    pl.semaphore_wait(barrier, len(peers))


class Copies:
    def __init__(self, send, recv):
        self.send, self.recv, self.count, self.started = send, recv, 0, []

    def take(self, n=1):
        first = self.count
        self.count += n
        return first

    def make(self, sem, src, dst, to):
        return pltpu.make_async_remote_copy(
            src_ref=src,
            dst_ref=dst,
            send_sem=self.send.at[sem],
            recv_sem=self.recv.at[sem],
            device_id=to,
            device_id_type=pl.DeviceIdType.MESH,
        )

    def start(self, src, dst, to):
        copy = self.make(self.take(), src, dst, to)
        copy.start()
        self.started.append(copy)
        return copy

    def finish(self):
        for copy in self.started:
            copy.wait_send()


class Gather:
    def __init__(self, copies, first, view, hops, ring, arrived=None):
        self.copies, self.first, self.view, self.hops = copies, first, view, hops
        self.place, self.size, self.sides = ring
        self.arrived = arrived
        self.sent = [[], []]

    def step(self, s):
        for way, sign in ((0, 1), (1, -1)):
            block = step_from(self.place, -sign * s, self.size)
            if 0 < s <= self.hops[way]:
                self.sent[way][s - 1].wait_recv()
            if s < self.hops[way]:
                src = self.first if s == 0 else self.view(block)
                self.sent[way].append(self.copies.start(src, self.view(block), self.sides[way]))
            if self.arrived is not None and 0 < s <= self.hops[way]:
                self.arrived(block)


class Scatter:
    def __init__(self, copies, first, join, held, hops, ring):
        self.copies, self.first, self.join, self.held, self.hops = copies, first, join, held, hops
        self.place, self.size, self.sides = ring
        self.sent = [[], []]

    def step(self, s):
        for way, sign in ((0, 1), (1, -1)):
            n = self.hops[way]
            if 0 < s <= n:
                self.sent[way][s - 1].wait_recv()
            if s < n:
                goal = step_from(self.place, sign * (n - s), self.size)
                if s == 0:
                    src = self.first(way, goal)
                else:
                    src = self.held(way, s - 1)
                    self.join(src, goal)
                self.sent[way].append(self.copies.start(src, self.held(way, s), self.sides[way]))

    def arrived(self):
        return [self.held(way, self.hops[way] - 1) for way in (0, 1)]


class Sum(Scatter):
    def __init__(self, copies, part, held, hops, ring):
        def join(ref, goal):
            ref[...] = (ref[...].astype(F32) + part(goal)[...].astype(F32)).astype(BF)

        super().__init__(copies, lambda way, b: part(b), join, held, hops, ring)
        self.part = part

    def total(self):
        total = self.part(self.place)[...].astype(F32)
        for ref in self.arrived():
            total += ref[...].astype(F32)
        return total


def rings(x, z, y, c):
    along_z = z, Z, tuple(device(x, step_from(z, i, Z), y, c) for i in (1, -1))
    along_y = y, Y, tuple(device(x, z, step_from(y, i, Y), c) for i in (1, -1))
    return along_z, along_y


HOPS = ((4, 3), (3, 4))
HOPS_Y = ((2, 1), (1, 2))


def start_local(local, kept, src, dst):
    copy = pltpu.make_async_copy(src, dst, local.at[len(kept)])
    copy.start()
    kept.append(copy)


def step_all(pieces, s):
    for one in pieces:
        one.step(s)


def spread_kernel(
    ids_ref, q_ref, k_ref, v_ref, w_ref, g_ref,
    idall, qall, ktab, vtab, wf, gfull,
    send, recv, local,
):
    x, z, y, c = place()
    t = y * C + c
    width = w_ref.shape[1]
    depth = w_ref.shape[0] // 4
    span = Z * width
    xs = [step_from(x, i, X) for i in range(X)]
    along_z, along_y = rings(x, z, y, c)
    sibling = device(x, z, y, 1 - c)
    enter(
        [device(xs[i], z, y, c) for i in (1, 2, 3)]
        + list(along_z[2])
        + list(along_y[2])
        + [sibling]
    )
    copies = Copies(send, recv)
    kept = []

    def keep(src, dst):
        start_local(local, kept, src, dst)

    table_in, q_in, g_core = [], [], {}

    def piece(ref, i):
        return Gather(copies, ref.at[z, i], lambda b: ref.at[b, i], HOPS[i % 2], along_z)

    def weight_piece(i):
        rows = pl.ds(i * depth, depth)
        return Gather(
            copies, w_ref.at[rows], lambda b: wf.at[rows, columns(b, width)], HOPS[i % 2], along_z
        )

    weights = [weight_piece(i) for i in range(4)]
    asked = [piece(qall, i) for i in range(X)]
    asked.append(Gather(copies, idall.at[z], lambda b: idall.at[b], HOPS[0], along_z))

    def send_table(src, dst):
        for i in (1, 3, 2):
            to = device(xs[i], z, y, c)
            table_in.append(copies.start(src.at[:, columns(xs[i], HD)], dst.at[x], to))

    def hand_over(i, block):
        block = gfull.at[i, block * C + c]
        g_core[i].append(copies.start(block, block, sibling))

    def rows_piece(i):
        return Gather(
            copies,
            gfull.at[i, t],
            lambda b: gfull.at[i, b * C + c],
            HOPS_Y[i % 2],
            along_y,
            lambda b: hand_over(i, b),
        )

    rows = [rows_piece(i) for i in range(X)]

    def send_rows(i):
        rows[i].step(0)
        g_core[i] = []
        hand_over(i, y)

    for i in (1, 3, 2):
        to = device(xs[i], z, y, c)
        q_in.append(copies.start(q_ref.at[:, columns(xs[i], HD)], qall.at[z, x], to))
        q_in.append(copies.start(ids_ref, idall.at[z, x], to))
    step_all(weights, 0)
    g_in = [
        copies.start(g_ref.at[:, columns(xs[i], span)], gfull.at[x, t], device(xs[i], z, y, c))
        for i in (1, 3, 2)
    ]
    keep(q_ref.at[:, columns(x, HD)], qall.at[z, x])
    keep(ids_ref, idall.at[z, x])
    keep(g_ref.at[:, columns(x, span)], gfull.at[x, t])
    keep(w_ref, wf.at[:, columns(z, width)])
    keep(k_ref.at[:, columns(x, HD)], ktab.at[x])
    keep(v_ref.at[:, columns(x, HD)], vtab.at[x])
    for copy in q_in:
        copy.wait_recv()
    for copy in kept[:2]:
        copy.wait()
    step_all(asked, 0)
    send_table(k_ref, ktab)
    send_table(v_ref, vtab)
    step_all(weights, 1)
    kept[2].wait()
    for copy in g_in:
        copy.wait_recv()
    send_rows(0)
    send_rows(1)
    step_all(asked, 1)
    step_all(rows[:2], 1)
    send_rows(2)
    send_rows(3)
    step_all(weights, 2)
    step_all(rows[:2], 2)
    step_all(asked, 2)
    step_all(rows[2:], 1)
    step_all(weights, 3)
    step_all(rows[2:], 2)
    step_all(asked, 3)
    step_all(weights, 4)
    step_all(asked, 4)
    for i in range(X):
        for copy in g_core[i]:
            copy.wait_recv()
    for copy in table_in:
        copy.wait_recv()
    for copy in kept[3:]:
        copy.wait()
    copies.finish()


def spread(ids, queries, keys, values, out_weight, grad_out):
    depth, width = out_weight.shape
    rows = keys.shape[0]
    return pl.pallas_call(
        spread_kernel,
        out_shape=(
            jax.ShapeDtypeStruct((Z, X) + ids.shape, jnp.int32),
            jax.ShapeDtypeStruct((Z, X, TOK, HD), BF),
            jax.ShapeDtypeStruct((X, rows, HD), BF),
            jax.ShapeDtypeStruct((X, rows, HD), BF),
            jax.ShapeDtypeStruct((depth, Z * width), BF),
            jax.ShapeDtypeStruct((X, Y * C, grad_out.shape[0], Z * width), BF),
        ),
        in_specs=[VMEM] + [HBM] * 5,
        out_specs=[VMEM] * 6,
        scratch_shapes=[
            pltpu.SemaphoreType.DMA((112,)),
            pltpu.SemaphoreType.DMA((112,)),
            pltpu.SemaphoreType.DMA((8,)),
        ],
        compiler_params=pltpu.CompilerParams(
            collective_id=0, has_side_effects=True, vmem_limit_bytes=LIMIT
        ),
        name="spread",
    )(ids, queries, keys, values, out_weight, grad_out)


TAIL = 16
LISTED = 256 + 32


def list_uses(ids, uses):
    z = lax.rem(lax.axis_index("dp"), Z)

    def add(dp, n):
        dp_z, dp_x = lax.shift_right_logical(dp, 2), dp & 3
        named = [ids[dp_z, dp_x, 0, j] for j in range(16)]
        for j in range(8):
            owner, name = named[2 * j : 2 * j + 2]
            uses[n] = dp * 4 + j // 2
            uses[LISTED + n] = lax.shift_right_logical(owner, 3) * NB_DEV + name
            n = n + ((owner & 7) == z).astype(jnp.int32)
        return n

    n = lax.fori_loop(0, X * Z, add, jnp.int32(0), unroll=2)
    last = jnp.maximum(n - 1, 0)
    for i in range(2 * PAIRS - 1):
        uses[n + i] = uses[last]
        uses[LISTED + n + i] = uses[LISTED + last]
    uses[2 * LISTED] = n
    return n


def uses_at(uses, p, n, pairs):
    lane = lax.broadcasted_iota(jnp.int32, (1, 2 * GROUP), 1)
    out = []
    for i in range(pairs):
        a = 2 * (pairs * p + i)
        b = a + 1
        real = jnp.where(lane < GROUP, a, b) < n
        out.append((uses[a], uses[b], uses[LISTED + a], uses[LISTED + b], real))
    return out


def turns(n, pairs):
    return lax.div(n + (2 * pairs - 1), 2 * pairs)


def pair_rows(ref, a, b, size):
    return [ref[pl.ds(pl.multiple_of(i * size, size), size), :] for i in (a, b)]


def pair_scores(first, second, both, left):
    product = lax.dot_general(
        jnp.concatenate([first, second], axis=0),
        both,
        (((1,), (1,)), ((), ())),
        preferred_element_type=F32,
    )
    return jnp.where(left, product[:NLEN], product[NLEN:])


def merge(one, two):
    peak = jnp.maximum(one[0], two[0])
    return peak, jnp.exp(one[0] - peak) * one[1] + jnp.exp(two[0] - peak) * two[1]


def clear(ref, rows=512):
    @pl.loop(0, ref.shape[0] // rows)
    def _(i):
        ref[pl.ds(pl.multiple_of(i * rows, rows), rows), :] = jnp.zeros((rows, HD), ref.dtype)


def add_rows(ref, i, size, value):
    at = pl.ds(pl.multiple_of(i * size, size), size)
    ref[at, :] = (ref[at, :].astype(F32) + value).astype(ref.dtype)


def attend_kernel(ids, qall, ktab, vtab, logs, ctx, uses, stats):
    n = list_uses(ids, uses)
    stats[0] = jnp.full(stats.shape[1:], LOW, F32)
    stats[1] = jnp.zeros(stats.shape[1:], F32)
    clear(ctx)
    left = lax.broadcasted_iota(jnp.int32, (1, 2 * GROUP), 1) < GROUP

    def scores_of(ga, gb, na, nb):
        qq = jnp.concatenate(pair_rows(qall, ga, gb, GROUP), axis=0)
        return pair_scores(*pair_rows(ktab, na, nb, NLEN), qq, left) * SCALE

    def measure(p, carry):
        pairs = uses_at(uses, p, n, PAIRS)
        found = []
        for ga, gb, na, nb, real in pairs:
            scores = scores_of(ga, gb, na, nb)
            peak = jnp.max(scores, axis=0, keepdims=True)
            total = jnp.sum(jnp.exp(scores - peak), axis=0, keepdims=True)
            found.append((jnp.where(real, peak, LOW), jnp.where(real, total, 0.0)))
        for (ga, gb, *_), new in zip(pairs, found):
            for g, mine in ((ga, left), (gb, jnp.logical_not(left))):
                old = tuple(stats[i, pl.ds(g, 1), :] for i in range(2))
                merged = merge(old, new)
                for i in range(2):
                    stats[i, pl.ds(g, 1), :] = jnp.where(mine, merged[i], old[i])
        return carry

    def weigh(p, carry):
        pairs = uses_at(uses, p, n, PAIRS)
        found = []
        for ga, gb, na, nb, real in pairs:
            scores = scores_of(ga, gb, na, nb)
            log_total = jnp.where(left, logs[pl.ds(ga, 1), :], logs[pl.ds(gb, 1), :])
            prob = jnp.where(real, jnp.exp(scores - log_total), 0.0)
            values = pair_rows(vtab, na, nb, NLEN)
            found.append(
                jnp.dot(
                    prob.T.astype(BF),
                    jnp.concatenate(values, axis=1),
                    preferred_element_type=F32,
                )
            )
        for (ga, gb, *_), context in zip(pairs, found):
            add_rows(ctx, ga, GROUP, context[:GROUP, :HD])
            add_rows(ctx, gb, GROUP, context[GROUP:, HD:])
        return carry

    lax.fori_loop(0, turns(n, PAIRS), measure, 0)
    state = stats[0], stats[1]
    peak, total = merge(state, tuple(pltpu.roll(v, GROUP, 1) for v in state))
    logs[...] = jnp.where(total > 0.0, peak + jnp.log(jnp.maximum(total, 1e-30)), LOW)
    lax.fori_loop(0, turns(n, PAIRS), weigh, 0)


def attend(ids, qall, ktab, vtab):
    return pl.pallas_call(
        attend_kernel,
        out_shape=(
            jax.ShapeDtypeStruct((16 * Z, 2 * GROUP), F32),
            jax.ShapeDtypeStruct(qall.shape, BF),
            jax.ShapeDtypeStruct((2 * LISTED + 64,), jnp.int32),
        ),
        in_specs=[SMEM] + [VMEM] * 3,
        out_specs=[VMEM] * 2 + [SMEM],
        scratch_shapes=[
            pltpu.VMEM((2, 16 * Z, 2 * GROUP), F32),
        ],
        compiler_params=pltpu.CompilerParams(vmem_limit_bytes=LIMIT),
        name="attend",
    )(ids, qall, ktab, vtab)


def project_kernel(
    logs, ctx, wf, gfull,
    sums, upall, out,
    wf_other, upp, upr, staged, held, ctx4, ctx_other, part, y_held, done,
    send, recv, out_send, out_recv, local,
):
    x, z, y, c = place()
    head_cols, span = wf.shape
    slots = TOK // (Y * C)
    xs = [step_from(x, i, X) for i in range(X)]
    along_z, along_y = rings(x, z, y, c)
    sibling = device(x, z, y, 1 - c)
    enter(
        [device(xs[i], z, y, c) for i in (1, 2, 3)]
        + list(along_z[2])
        + list(along_y[2])
        + [sibling]
    )
    copies = Copies(send, recv)
    left = lax.broadcasted_iota(jnp.int32, (1, 2 * GROUP), 1) < GROUP
    up_in, ctx_in, core_in = {}, {}, {}

    def multiply_rows(i):
        upp[i] = lax.dot_general(
            gfull[i].reshape(TOK, span),
            wf[...],
            (((1,), (1,)), ((), ())),
            preferred_element_type=F32,
        ).astype(BF)
        up_in[i] = [
            copies.start(
                upp.at[i, :, columns(xs[j], HD)], upr.at[i, j - 1], device(xs[j], z, y, c)
            )
            for j in (1, 3, 2)
        ]

    def total_up(i):
        for copy in up_in[i]:
            copy.wait_recv()
        value = upp[i, :, columns(x, HD)].astype(F32)
        for j in range(3):
            value += upr[i, j].astype(F32)
        upall[z, i] = value.astype(BF)
        upstream[i].step(0)

    def mine(b, i):
        rows = [logs[pl.ds(b * 16 + i * 4 + j, 1), :] for j in range(4)]
        return ctx[b, i].astype(F32), [jnp.where(left, *rows[j : j + 2]) for j in (0, 2)]

    def write(ref, state):
        ref[:TOK] = state[0].astype(BF)
        rows = []
        for rest in state[1]:
            for _ in range(3):
                rows.append(rest.astype(BF).astype(F32))
                rest = rest - rows[-1]
        rows.append(jnp.zeros((TAIL - len(rows), HD), F32))
        ref[TOK:] = jnp.concatenate(rows, axis=0).astype(BF)

    def read(ref):
        rows = ref[TOK:].astype(F32)
        sums_of = [rows[3 * j : 3 * j + 1] + rows[3 * j + 1 : 3 * j + 2] for j in range(2)]
        return ref[:TOK].astype(F32), [v + rows[3 * j + 2 : 3 * j + 3] for j, v in enumerate(sums_of)]

    def joined(one, two):
        blocks, log_sums = [], []
        for j in range(2):
            peak = jnp.maximum(one[1][j], two[1][j])
            log_sum = peak + jnp.log(jnp.exp(one[1][j] - peak) + jnp.exp(two[1][j] - peak))
            block = 0.0
            for context, logs_of in (one, two):
                factor = jnp.broadcast_to(jnp.exp(logs_of[j] - log_sum), (2 * GROUP, HD)).T
                block += factor * context[j * 2 * GROUP : (j + 1) * 2 * GROUP]
            blocks.append(block)
            log_sums.append(log_sum)
        return jnp.concatenate(blocks, axis=0), log_sums

    def both_halves(at, row):
        turned = pltpu.roll(row, GROUP, 1)
        return (at, jnp.where(left, row, turned)), (at + 1, jnp.where(left, turned, row))

    def context_piece(i):
        def first(way, b):
            write(staged.at[i, way], mine(b, i))
            return staged.at[i, way]

        return Scatter(
            copies,
            first,
            lambda ref, b: write(ref, joined(read(ref), mine(b, i))),
            lambda way, s: held.at[i, 4 * way + s],
            HOPS[i % 2],
            along_z,
        )

    def out_piece(i):
        return Sum(
            copies,
            lambda b: part.at[i, b],
            lambda way, s: y_held.at[i, 2 * way + s],
            HOPS_Y[i % 2],
            along_y,
        )

    contexts = [context_piece(i) for i in range(X)]
    outs = [out_piece(i) for i in range(X)]
    upstream = [
        Gather(copies, upall.at[z, i], lambda b, i=i: upall.at[b, i], HOPS[i % 2], along_z)
        for i in range(X)
    ]

    def share(i):
        state = mine(z, i)
        for ref in contexts[i].arrived():
            state = joined(state, read(ref))
        at = ctx4.at[i, :, :, :, columns(x, HD)]
        at[...] = state[0].astype(BF).reshape(Y, C, slots, HD)
        ctx_in[i] = [copies.start(at, at, device(xs[j], z, y, c)) for j in (1, 3, 2)]
        for j in range(2):
            for row, value in both_halves(z * 16 + i * 4 + 2 * j, state[1][j]):
                sums[0, pl.ds(row, 1), :] = value

    def inner(i):
        context = ctx4[i, :, :, :, columns(x, HD)].reshape(TOK, HD)
        product = upall[z, i].astype(F32) * context.astype(F32)
        for j in range(2):
            rows = product[j * 2 * GROUP : (j + 1) * 2 * GROUP]
            total = jnp.sum(rows.T, axis=0, keepdims=True)
            for row, value in both_halves(z * 16 + i * 4 + 2 * j, total):
                sums[1, pl.ds(row, 1), :] = value

    def swap(i):
        for copy in ctx_in[i]:
            copy.wait_recv()
        core_in[i] = copies.start(ctx4.at[i, :, 1 - c], ctx_other.at[i], sibling)

    def multiply(i):
        core_in[i].wait_recv()
        mine = ctx4[i, :, c].reshape(Y * slots, head_cols)
        others = ctx_other[i].reshape(Y * slots, head_cols)
        for j in range(2):
            cols = pl.ds(j * (span // 2), span // 2)
            product = jnp.dot(mine, wf[:, cols], preferred_element_type=F32)
            product += jnp.dot(others, wf_other[:, cols], preferred_element_type=F32)
            part[i, :, :, cols] = product.astype(BF).reshape(Y, slots, span // 2)
        outs[i].step(0)

    def finish_out(i):
        outs[i].step(2)
        done[i] = outs[i].total().astype(BF)
        goal = out.at[:, columns(x, span)]

        @pl.when(x == i)
        def _():
            copy = pltpu.make_async_copy(done.at[i], goal, local.at[7])
            copy.start()
            copy.wait()

        @pl.when(x != i)
        def _():
            sem = step_from(i - x, 0, X)
            pltpu.make_async_remote_copy(
                src_ref=done.at[i],
                dst_ref=goal,
                send_sem=out_send.at[sem],
                recv_sem=out_recv.at[sem],
                device_id=device(i, z, y, c),
                device_id_type=pl.DeviceIdType.MESH,
            ).start()

    told = Gather(
        copies,
        sums.at[:, columns(z, 16)],
        lambda b: sums.at[:, columns(b, 16)],
        HOPS[0],
        along_z,
    )

    step_all(contexts, 0)
    weight_in = copies.start(wf, wf_other, sibling)
    for i in range(X):
        multiply_rows(i)
    for s in (1, 2):
        step_all(contexts, s)
    total_up(0)
    total_up(1)
    step_all(contexts, 3)
    total_up(2)
    total_up(3)
    for i in range(X):
        contexts[i].step(4)
        share(i)
    weight_in.wait_recv()
    step_all(upstream[:2], 1)
    for i in range(X):
        inner(i)
    told.step(0)
    swap(0)
    multiply(0)
    step_all(upstream[2:], 1)
    swap(1)
    multiply(1)
    told.step(1)
    step_all(upstream[:2], 2)
    swap(2)
    multiply(2)
    step_all(upstream[2:], 2)
    swap(3)
    step_all(outs[:1], 1)
    multiply(3)
    told.step(2)
    step_all(outs[1:2], 1)
    step_all(upstream, 3)
    step_all(outs[2:], 1)
    told.step(3)
    finish_out(0)
    finish_out(1)
    step_all(upstream, 4)
    told.step(4)
    finish_out(2)
    finish_out(3)
    for i in (1, 2, 3):
        copy = pltpu.make_async_remote_copy(
            src_ref=done.at[0],
            dst_ref=out.at[:, columns(xs[i], span)],
            send_sem=out_send.at[i],
            recv_sem=out_recv.at[i],
            device_id=device(xs[i], z, y, c),
            device_id_type=pl.DeviceIdType.MESH,
        )
        copy.wait_recv()
        copy.wait_send()
    copies.finish()


def project(logs, ctx, wf, gfull):
    head_cols, span = wf.shape
    slots = TOK // (Y * C)
    return pl.pallas_call(
        project_kernel,
        out_shape=(
            jax.ShapeDtypeStruct((2,) + logs.shape, F32),
            jax.ShapeDtypeStruct(ctx.shape, BF),
            jax.ShapeDtypeStruct((slots, X * span), BF),
        ),
        in_specs=[VMEM] * 4,
        out_specs=[VMEM] * 3,
        scratch_shapes=[
            pltpu.VMEM((head_cols, span), BF),
            pltpu.VMEM((X, TOK, head_cols), BF),
            pltpu.VMEM((X, X - 1, TOK, HD), BF),
            pltpu.VMEM((X, 2, TOK + TAIL, HD), BF),
            pltpu.VMEM((X, 8, TOK + TAIL, HD), BF),
            pltpu.VMEM((X, Y, C, slots, head_cols), BF),
            pltpu.VMEM((X, Y, slots, head_cols), BF),
            pltpu.VMEM((X, Y, slots, span), BF),
            pltpu.VMEM((X, 4, slots, span), BF),
            pltpu.VMEM((X, slots, span), BF),
            pltpu.SemaphoreType.DMA((144,)),
            pltpu.SemaphoreType.DMA((144,)),
            pltpu.SemaphoreType.DMA((4,)),
            pltpu.SemaphoreType.DMA((4,)),
            pltpu.SemaphoreType.DMA((8,)),
        ],
        compiler_params=pltpu.CompilerParams(
            collective_id=1, has_side_effects=True, vmem_limit_bytes=LIMIT
        ),
        name="project",
    )(logs, ctx, wf, gfull)


def grads_kernel(uses, qall, upall, ktab, vtab, sums, gq, dkey, dvalue, dk, dv):
    n = uses[2 * LISTED]
    for ref in (gq, dk, dv):
        clear(ref)

    left = lax.broadcasted_iota(jnp.int32, (1, 2 * GROUP), 1) < GROUP
    zero = jnp.zeros((), BF)

    def dot(a, b):
        return jnp.dot(a, b, preferred_element_type=F32)

    def some(p, carry):
        pairs = uses_at(uses, p, n, GRAD_PAIRS)
        found = []
        for ga, gb, na, nb, real in pairs:
            qq = jnp.concatenate(pair_rows(qall, ga, gb, GROUP), axis=0)
            uu = jnp.concatenate(pair_rows(upall, ga, gb, GROUP), axis=0)
            keys = pair_rows(ktab, na, nb, NLEN)
            values = pair_rows(vtab, na, nb, NLEN)
            scores = pair_scores(*keys, qq, left) * SCALE
            grad_probs = pair_scores(*values, uu, left)
            log_total = jnp.where(left, sums[0, pl.ds(ga, 1), :], sums[0, pl.ds(gb, 1), :])
            inner = jnp.where(left, sums[1, pl.ds(ga, 1), :], sums[1, pl.ds(gb, 1), :])
            prob = jnp.where(real, jnp.exp(scores - log_total), 0.0)
            grad_scores = prob * (grad_probs - inner)
            grad_t = grad_scores.T.astype(BF)
            grad_q = dot(grad_t, jnp.concatenate(keys, axis=1)) * SCALE
            grad_v = dot(halves(prob.astype(BF)), uu)
            grad_k = dot(halves(grad_scores.astype(BF)), qq) * SCALE
            found.append((grad_q, grad_v, grad_k))
        for (ga, gb, na, nb, _), (grad_q, grad_v, grad_k) in zip(pairs, found):
            add_rows(gq, ga, GROUP, grad_q[:GROUP, :HD])
            add_rows(gq, gb, GROUP, grad_q[GROUP:, HD:])
            add_rows(dv, na, NLEN, grad_v[:NLEN])
            add_rows(dv, nb, NLEN, grad_v[NLEN:])
            add_rows(dk, na, NLEN, grad_k[:NLEN])
            add_rows(dk, nb, NLEN, grad_k[NLEN:])
        return carry

    def halves(v):
        return jnp.concatenate([jnp.where(left, v, zero), jnp.where(left, zero, v)], axis=0)

    lax.fori_loop(0, turns(n, GRAD_PAIRS), some, 0)
    for src, dst in ((dk, dkey), (dv, dvalue)):
        rows = 512

        @pl.loop(0, src.shape[0] // rows)
        def _(i, src=src, dst=dst):
            at = pl.ds(pl.multiple_of(i * rows, rows), rows)
            dst[at, :] = src[at, :].astype(BF)


def grads_of_uses(uses, qall, upall, ktab, vtab, sums):
    tokens, rows = qall.shape[0], ktab.shape[0]
    return pl.pallas_call(
        grads_kernel,
        out_shape=(
            jax.ShapeDtypeStruct((tokens, HD), BF),
            jax.ShapeDtypeStruct((rows, HD), BF),
            jax.ShapeDtypeStruct((rows, HD), BF),
        ),
        in_specs=[SMEM] + [VMEM] * 5,
        out_specs=[VMEM] * 3,
        scratch_shapes=[
            pltpu.VMEM((rows, HD), F32),
            pltpu.VMEM((rows, HD), F32),
        ],
        compiler_params=pltpu.CompilerParams(vmem_limit_bytes=LIMIT),
        name="grads",
    )(uses, qall, upall, ktab, vtab, sums)


def collect_kernel(
    gq, dkey, dvalue, gq_out, dk_out, dv_out, held, gq_done, send, recv, local
):
    x, z, y, c = place()
    xs = [step_from(x, i, X) for i in range(X)]
    along_z, _ = rings(x, z, y, c)
    enter([device(xs[i], z, y, c) for i in (1, 2, 3)] + list(along_z[2]))
    copies = Copies(send, recv)
    kept, table_in, gq_sent = [], [], []

    def piece(i):
        return Sum(
            copies,
            lambda b: gq.at[b, xs[i]],
            lambda way, s: held.at[i, 4 * way + s],
            HOPS[i % 2],
            along_z,
        )

    grads = [piece(i) for i in range(X)]
    step_all(grads, 0)
    for src, dst in ((dkey, dk_out), (dvalue, dv_out)):
        goal = dst.at[:, columns(x, HD)]
        for i in (1, 3, 2):
            table_in.append(copies.start(src.at[xs[i]], goal, device(xs[i], z, y, c)))
        start_local(local, kept, src.at[x], goal)
    for s in (1, 2, 3):
        step_all(grads, s)
    for i in (1, 2, 3, 0):
        grads[i].step(4)
        gq_done[i] = grads[i].total().astype(BF)
        goal = gq_out.at[:, columns(x, HD)]
        if i == 0:
            start_local(local, kept, gq_done.at[i], goal)
        else:
            gq_sent.append(copies.start(gq_done.at[i], goal, device(xs[i], z, y, c)))
    for copy in table_in + gq_sent:
        copy.wait_recv()
    for copy in kept:
        copy.wait()
    copies.finish()


def collect(gq, dkey, dvalue):
    rows = dkey.shape[1]
    return pl.pallas_call(
        collect_kernel,
        out_shape=(
            jax.ShapeDtypeStruct((TOK, X * HD), BF),
            jax.ShapeDtypeStruct((rows, X * HD), BF),
            jax.ShapeDtypeStruct((rows, X * HD), BF),
        ),
        in_specs=[VMEM] * 3,
        out_specs=[VMEM] * 3,
        scratch_shapes=[
            pltpu.VMEM((X, 8, TOK, HD), BF),
            pltpu.VMEM((X, TOK, HD), BF),
            pltpu.SemaphoreType.DMA((40,)),
            pltpu.SemaphoreType.DMA((40,)),
            pltpu.SemaphoreType.DMA((8,)),
        ],
        compiler_params=pltpu.CompilerParams(
            collective_id=2, has_side_effects=True, vmem_limit_bytes=LIMIT
        ),
        name="collect",
    )(gq, dkey, dvalue)


def finish_kernel(out, gq, dkey, dvalue, out_to, gq_to, dk_to, dv_to, wide, sems):
    copies = []

    def send(src, dst):
        copies.append(pltpu.make_async_copy(src, dst, sems.at[len(copies)]))
        copies[-1].start()

    rows = dkey.shape[0] // 4
    for i, (src, dst) in enumerate(((dkey, dk_to), (dvalue, dv_to))):
        for j in range(4):
            at = pl.ds(j * rows, rows)
            wide[i, at] = src[at].astype(F32)
            send(wide.at[i, at], dst.at[at])
    send(out, out_to)
    send(gq, gq_to)
    for copy in copies:
        copy.wait()


def finish(out, gq, dkey, dvalue):
    return pl.pallas_call(
        finish_kernel,
        out_shape=(
            jax.ShapeDtypeStruct(out.shape, BF),
            jax.ShapeDtypeStruct(gq.shape, BF),
            jax.ShapeDtypeStruct(dkey.shape, F32),
            jax.ShapeDtypeStruct(dvalue.shape, F32),
        ),
        in_specs=[VMEM] * 4,
        out_specs=[HBM] * 4,
        scratch_shapes=[
            pltpu.VMEM((2,) + dkey.shape, F32),
            pltpu.SemaphoreType.DMA((10,)),
        ],
        compiler_params=pltpu.CompilerParams(vmem_limit_bytes=LIMIT),
        name="finish",
    )(out, gq, dkey, dvalue)


def shards(queries, keys, values, out_weight, grad_out, neighbour_owner, neighbour_local):
    ids = jnp.stack([neighbour_owner, neighbour_local], axis=-1).reshape(1, -1)
    ids = jnp.pad(ids, ((0, 0), (0, 128 - ids.shape[1])))
    ids, qall, ktab, vtab, wf, gfull = spread(ids, queries, keys, values, out_weight, grad_out)
    qall = qall.reshape(Z * X * TOK, HD)
    ktab, vtab = (a.reshape(X * keys.shape[0], HD) for a in (ktab, vtab))
    logs, ctx, uses = attend(ids, qall, ktab, vtab)
    sums, upall, out = project(logs, ctx.reshape(Z, X, TOK, HD), wf, gfull)
    upall = upall.reshape(Z * X * TOK, HD)
    gq, dkey, dvalue = grads_of_uses(uses, qall, upall, ktab, vtab, sums)
    dkey, dvalue = (a.reshape((X,) + keys.shape[:1] + (HD,)) for a in (dkey, dvalue))
    grad_queries, grad_keys, grad_values = collect(gq.reshape(Z, X, TOK, HD), dkey, dvalue)
    return finish(out, grad_queries, grad_keys, grad_values)


def solution(mesh):
    return jax.shard_map(
        shards,
        mesh=mesh,
        in_specs=(
            P("dp", "tensor"),
            P("dp", "tensor"),
            P("dp", "tensor"),
            P("tensor", "dp"),
            P(("dp", "tensor"), None),
            P("dp", None),
            P("dp", None),
        ),
        out_specs=(
            P(("dp", "tensor"), None),
            P("dp", "tensor"),
            P("dp", "tensor"),
            P("dp", "tensor"),
        ),
        check_vma=False,
    )
```
